256 devices in a mesh: row: 16 (over y, z_lo, core), col: 16 (over x, z_hi).
Axes of the slice: x: 4, y: 4, z: 8 (z_hi: 4, z_lo: 2; z = z_hi * 2 + z_lo), core: 2. Of those that a mesh axis runs over, the one named last changes fastest.
Arguments:
- rates: bfloat16 [192, 16384], P(None, 'col'), may hold values from -1 to 1
- targets: bfloat16 [192, 16384], P(None, 'row'), may hold values from -6 to 6
- readout_goal: float32 [16, 192], replicated, may hold values from -6 to 6
- inverse_corr: float32 [16384, 16384], P('row', 'col'), may hold values from -0.1 to 3.1, as said below
- recurrent: bfloat16 [16384, 16384], P('row', 'col'), may hold values from -0.046875 to 0.046875
- readout: float32 [16, 16384], P(None, 'col'), may hold values from -0.046875 to 0.046875
Outputs:
- corr_out: float32 [16384, 16384], P('row', 'col')
- recurrent_out: bfloat16 [16384, 16384], P('row', 'col')
- readout_out: float32 [16, 16384], P(None, 'col')
The draws below stay inside these ranges and needn't reach their ends.
Inputs may be any that keep to these rules, and one draw needn't show every extreme that they name: `inverse_corr`: symmetric and positive definite.
All inputs are finite; a program needn't handle non-finite values.
Results may differ from the reference program's by a relative error of at most 0.0057.
Values may be sent and summed in bfloat16 or wider, within the bound.
A program may use at most 64 MiB of HBM per device.

```python
import jax
import jax.numpy as jnp
from jax import lax

N = 16384
STEPS = 64
OUTS = 16
BLOCKS = 3
WSTEPS = 192


def draw_rates(key, part):
    key = jax.random.fold_in(key, 5)
    key_a, key_b, key_c = jax.random.split(key, 3)
    shared = jax.random.normal(key_a, (1, N), jnp.float32)
    noise = jax.random.normal(key_b, (BLOCKS * STEPS, N), jnp.float32)
    gains = jnp.exp(jax.random.uniform(key_c, (1, N), jnp.float32, -0.7, 0.0))
    return (jnp.tanh(1.2 * shared + 0.8 * noise) * gains).astype(jnp.bfloat16)


def draw_inverse_corr(key, part):
    key = jax.random.fold_in(key, 11)
    key_a, key_b = jax.random.split(key)
    raw = jax.random.normal(key_a, (N, N), jnp.float32) * (0.5 * N ** (-0.5))
    diagonal = jnp.exp(jax.random.uniform(key_b, (N,), jnp.float32, 0.0, 0.69))
    return 0.5 * (raw + raw.T) + jnp.diag(diagonal)


def level_of(rng, extent, cuts, low, top_value):
    level, own = 1.0, jax.random.fold_in(rng, 6)
    for axis_at, shards_of in cuts:
        draws = jnp.exp(jax.random.uniform(jax.random.fold_in(own, axis_at), (shards_of,), jnp.float32, low / len(cuts), top_value / len(cuts)))
        level = level * jnp.repeat(draws, extent[axis_at] // shards_of).reshape([-1 if axis == axis_at else 1 for axis in range(len(extent))])
    return level


def gaussian(own_key, extent, spread, limit, pieces=(), kind=jnp.bfloat16):
    loudness = level_of(own_key, extent, pieces, -0.22, 0.18) if pieces else 1.0
    entries = jax.random.normal(own_key, extent, jnp.float32) * spread * loudness
    return jnp.minimum(jnp.maximum(entries, -limit), limit).astype(kind)


def setup_inputs(seed: int = 0) -> dict:
    key_of = jax.random.split(jax.random.key(seed), 7)
    rates = draw_rates(jax.random.fold_in(key_of[6], 71), 0)
    targets = gaussian(key_of[1], (WSTEPS, N), 1.0, 6.0, ((1, 16),))
    readout_goal = gaussian(key_of[2], (OUTS, WSTEPS), 1.0, 6.0, (), jnp.float32)
    inverse_corr = draw_inverse_corr(jax.random.fold_in(key_of[6], 71), 0)
    recurrent = gaussian(key_of[4], (N, N), N ** -0.5, 0.046875, ((0, 16), (1, 16)))
    readout = gaussian(key_of[5], (OUTS, N), N ** -0.5, 0.046875, ((1, 16),), jnp.float32)
    return {"rates": rates, "targets": targets, "readout_goal": readout_goal, "inverse_corr": inverse_corr, "recurrent": recurrent, "readout": readout}


def reference(rates, targets, readout_goal, inverse_corr, recurrent, readout):
    high = lax.Precision.HIGHEST
    corr = inverse_corr
    weights = recurrent
    outward = readout
    eye = jnp.eye(STEPS, dtype=jnp.float32)
    for window in range(BLOCKS):
        start = window * STEPS
        rate_bf = rates[start:start + STEPS]
        rate32 = rate_bf.astype(jnp.float32)
        prod_t = jnp.dot(rate32, corr.T, precision=high)
        drive = jnp.dot(rate_bf.astype(jnp.float32), weights.T.astype(jnp.float32), preferred_element_type=jnp.float32)
        guess = jnp.dot(outward, rate32.T, precision=high)
        capacity = eye + jnp.dot(rate32, prod_t.T, precision=high)
        factor = jnp.linalg.cholesky(capacity)
        cinverse = jax.scipy.linalg.cho_solve((factor, True), eye)
        coef_p = jnp.dot(cinverse, prod_t, precision=high)
        err_j = drive - targets[start:start + STEPS].astype(jnp.float32)
        coef_j = jnp.dot(cinverse, err_j, precision=high)
        err_w = guess - readout_goal[:, start:start + STEPS]
        coef_w = jnp.dot(err_w, cinverse, precision=high)
        corr = corr - jnp.dot(coef_p.T, prod_t, precision=high)
        outward = outward - jnp.dot(coef_w, prod_t, precision=high)
        weights = (weights.astype(jnp.float32) - jnp.dot(coef_j.T, prod_t, precision=high)).astype(jnp.bfloat16)
    return (corr, weights, outward)
```

```python
import jax
import jax.numpy as jnp
from jax import lax
from jax.sharding import PartitionSpec as P


def on_device(rates, targets, readout_goal, inverse_corr, recurrent, readout):
    high = lax.Precision.HIGHEST
    steps = rates.shape[0]
    cols_local = inverse_corr.shape[1]
    col_index = lax.axis_index("col")
    eye = jnp.eye(steps, dtype=jnp.float32)
    rate32 = rates.astype(jnp.float32)
    prod_part = jnp.dot(rate32, inverse_corr.T, precision=high)
    drive_part = jnp.dot(rates, recurrent.T, preferred_element_type=jnp.float32)
    guess_part = jnp.dot(readout, rate32.T, precision=high)
    prod_rows, drive, guess = lax.psum((prod_part, drive_part, guess_part), "col")
    gathered = lax.all_gather(prod_rows, "row", axis=1, tiled=True)
    prod_cols = lax.dynamic_slice_in_dim(gathered, col_index * cols_local, cols_local, 1)
    cap_part = jnp.dot(rate32, prod_cols.T, precision=high)
    capacity = eye + lax.psum(cap_part, "col")
    factor = jnp.linalg.cholesky(capacity)
    cinverse = jax.scipy.linalg.cho_solve((factor, True), eye)
    scaled = jnp.dot(cinverse, prod_cols, precision=high)
    err_j = drive - targets.astype(jnp.float32)
    err_w = guess - readout_goal
    corr = inverse_corr - jnp.dot(prod_rows.T, scaled, precision=high)
    outward = readout - jnp.dot(err_w, scaled, precision=high)
    weights = (
        recurrent.astype(jnp.float32) - jnp.dot(err_j.T, scaled, precision=high)
    ).astype(jnp.bfloat16)
    return (corr, weights, outward)


def solution(mesh):
    placed = (P(None, "col"), P(None, "row"), P(), P("row", "col"), P("row", "col"), P(None, "col"))
    return jax.shard_map(
        on_device,
        mesh=mesh,
        in_specs=placed,
        out_specs=(P("row", "col"), P("row", "col"), P(None, "col")),
        check_vma=False,
    )
```

```python
import functools

import jax
import jax.numpy as jnp
from jax import lax
from jax.experimental import pallas as pl
from jax.experimental.pallas import tpu as pltpu
from jax.sharding import PartitionSpec as P

MESH = pl.DeviceIdType.MESH
BF, F32 = jnp.bfloat16, jnp.float32
HIGH = lax.Precision.HIGHEST

STEPS = 192
LOCAL = 1024
OUTS = 16
QUARTER = 256
SLICE = 48
HALF = 96
PIECE = 16
BLOCK = 64
PACKED = 3 * BLOCK + 2 * OUTS
OWNERS = PACKED // PIECE
LANES = 128
NT = (((1,), (1,)), ((), ()))
TN = (((0,), (0,)), ((), ()))
VMEM_LIMIT = 50 * 1024 * 1024


def split2(x):
    hi = x.astype(BF)
    return hi, (x - hi.astype(F32)).astype(BF)


def aligned(start, size):
    return pl.ds(pl.multiple_of(start, size), size)


class Sems:
    def __init__(self):
        self.at = 0

    def take(self, count):
        first = self.at
        self.at += count
        return first


def comm_kernel(
    rates_hbm, targets_hbm, readout_hbm, corr_hbm, rec_hbm,
    cap, gcol, grow, err,
    rates, rates_t, targets, readout, rrow, corr_v, rec_v, h,
    drive_out, drive_hold, drive_relay, drive_sum, drive_x, drive_mid, drive_z, drive_low,
    kpart, krow, ksum, kz, kmid, kx,
    hcore, gone, gy_relay, gy_sum, gy, gtwo, gz, gpiece,
    load_sem, send_sem, recv_sem,
):
    i = lax.axis_index("row")
    j = lax.axis_index("col")
    y, zl, c = i // 4, (i // 2) % 2, i % 2
    x, zh = j // 4, j % 4

    def sigma(z):
        return (z % 2) * 2 + z // 2

    def quarter(q):
        return aligned((q % 4) * QUARTER, QUARTER)

    my_steps = aligned(sigma(zh) * SLICE, SLICE)
    my_quarter = quarter(x)
    row_steps = aligned((c * 2 + zl) * SLICE, SLICE)
    row_quarter = quarter(y)
    half_steps = aligned(c * HALF, HALF)
    sems = Sems()

    def remote(src, dst, at, dev, land=None):
        return pltpu.make_async_remote_copy(
            src_ref=src, dst_ref=dst, send_sem=send_sem.at[at], recv_sem=recv_sem.at[at if land is None else land],
            device_id=dev, device_id_type=MESH,
        )

    def load(src, dst, at):
        copy = pltpu.make_async_copy(src, dst, load_sem.at[at])
        copy.start()
        return copy

    rates_load = load(rates_hbm, rates, 8)
    rec_loads, corr_loads = {}, {}
    for d in (2, 1, 3, 0):
        part = quarter(x + d)
        rec_loads[d] = load(rec_hbm.at[part], rec_v.at[part], d)
    for d in (0, 3, 1, 2):
        part = quarter(x + d)
        corr_loads[d] = load(corr_hbm.at[part], corr_v.at[part], 4 + d)
    readout_load = load(readout_hbm, readout, 9)
    targets_load = load(targets_hbm, targets, 10)

    barrier = pltpu.get_barrier_semaphore()

    def greet(dev):
        pl.semaphore_signal(barrier, inc=1, device_id=dev, device_id_type=MESH)

    @pl.loop(1, 16)
    def _(d):
        greet({"row": (i + d) % 16})

    for d in range(1, 4):
        greet({"col": x * 4 + (zh + d) % 4})
        greet({"col": ((x + d) % 4) * 4 + zh})

    for e in range(4):
        source = x * 4 + e

        @pl.when((source != i) | (i != j))
        def _():
            greet({"row": source, "col": i})

    pl.semaphore_wait(barrier, jnp.where(i == j, 24, 25))

    def z_dev(d):
        return {"col": x * 4 + (zh + d) % 4}

    def x_dev(d):
        return {"col": ((x + d) % 4) * 4 + zh}

    def y_dev(d):
        return {"row": ((y + d) % 4) * 4 + zl * 2 + c}

    sibling = {"row": i + 1 - 2 * c}
    neighbour = {"row": y * 4 + (1 - zl) * 2 + c}

    def swap_each(src, buf, at, act_remote, act_local):
        for z in range(4):
            dst = buf.at[row_steps, row_quarter]
            land = at + zl * 2 + c

            @pl.when((i != j) | (zh != z))
            def _():
                act_remote(remote(src, dst, at + z, {"row": j, "col": y * 4 + z}, land))

            if act_local is not None:

                @pl.when((i == j) & (zh == z))
                def _():
                    act_local(pltpu.make_async_copy(src, dst, recv_sem.at[land]))

    def swap_start(src, buf, at):
        swap_each(src, buf, at, lambda copy: copy.start(), lambda copy: copy.start())

    def swap_wait_send(src, buf, at):
        swap_each(src, buf, at, lambda copy: copy.wait_send(), None)

    def swap_wait_recv(src, buf, at):
        for e in range(4):
            dst = buf.at[aligned(((e % 2) * 2 + e // 2) * SLICE, SLICE), my_quarter]
            source = x * 4 + e

            @pl.when((source != i) | (i != j))
            def _():
                remote(src, dst, at, {"row": source, "col": i}, at + e).wait_recv()

            @pl.when((source == i) & (i == j))
            def _():
                pltpu.make_async_copy(src, dst, recv_sem.at[at + e]).wait()

    def gather_z_start(buf, at):
        for d in range(1, 4):
            mine = buf.at[my_steps, my_quarter]
            remote(mine, mine, at + d - 1, z_dev(d)).start()

    def gather_z_wait(buf, at):
        for d in range(1, 4):
            theirs = buf.at[aligned(sigma((zh + 4 - d) % 4) * SLICE, SLICE), my_quarter]
            copy = remote(theirs, theirs, at + d - 1, z_dev(d))
            copy.wait_recv()
            copy.wait_send()

    class Ring:
        def __init__(self, buf, base, half, me, dev):
            self.buf, self.me, self.dev = buf, me, dev
            self.rows = (aligned(base, half), aligned(base + half, half))
            self.at = sems.take(6)

        def copy(self, k, owner):
            rows = self.rows[(0, 1, 1, 0, 0, 1)[k]]
            block = self.buf.at[rows, quarter(owner)]
            return remote(block, block, self.at + k, self.dev((1, 1, 3, 3, 1, 3)[k]))

        def start(self):
            for k in (0, 2, 1, 3):
                self.copy(k, self.me).start()

        def forward(self):
            self.copy(0, self.me + 3).wait_recv()
            self.copy(4, self.me + 3).start()
            self.copy(2, self.me + 1).wait_recv()
            self.copy(5, self.me + 1).start()

        def wait_sides(self):
            self.copy(1, self.me + 3).wait_recv()
            self.copy(3, self.me + 1).wait_recv()

        def wait_far(self):
            self.copy(4, self.me + 2).wait_recv()
            self.copy(5, self.me + 2).wait_recv()

        def wait_sends(self):
            for k in range(4):
                self.copy(k, self.me).wait_send()
            self.copy(4, self.me + 3).wait_send()
            self.copy(5, self.me + 1).wait_send()

    rates_load.wait()
    r_t = sems.take(4)
    r_src = rates.at[row_steps, row_quarter]
    swap_start(r_src, rrow, r_t)

    d_x = sems.take(6)
    top, low = pl.ds(0, HALF), pl.ds(HALF, HALF)

    def drive_quarter(d):
        rec_loads[d].wait()
        return lax.dot_general(rates[...], rec_v[quarter(x + d), :], NT, preferred_element_type=F32)

    drive_out[0] = drive_quarter(2).astype(BF)
    d_copies = [
        remote(drive_out.at[0, top], drive_relay.at[0], d_x, x_dev(1)),
        remote(drive_out.at[0, low], drive_relay.at[1], d_x + 1, x_dev(3)),
        remote(drive_out.at[1, low], drive_x.at[0], d_x + 2, x_dev(1)),
        remote(drive_out.at[2, top], drive_x.at[1], d_x + 3, x_dev(3)),
        remote(drive_sum.at[0], drive_x.at[2], d_x + 4, x_dev(1)),
        remote(drive_sum.at[1], drive_x.at[3], d_x + 5, x_dev(3)),
    ]
    d_copies[0].start()
    d_copies[1].start()
    part = drive_quarter(1)
    drive_hold[0] = part[:HALF]
    drive_out[1] = part.astype(BF)
    part = drive_quarter(3)
    drive_hold[1] = part[HALF:]
    drive_out[2] = part.astype(BF)

    rates_t[...] = rates[...].T

    swap_wait_recv(r_src, rrow, r_t)
    r_ring = Ring(rrow, 0, HALF, x, x_dev)
    r_ring.start()
    d_copies[2].start()
    d_copies[3].start()

    def corr_quarter(d):
        corr_loads[d].wait()
        hi, lo = split2(corr_v[quarter(x + d), :])
        left = rrow[:, quarter(x + d)]
        return jnp.dot(left, hi, preferred_element_type=F32) + jnp.dot(left, lo, preferred_element_type=F32)

    drive_mid[...] = drive_quarter(0)
    h[...] = corr_quarter(0)
    r_ring.forward()

    d_copies[0].wait_recv()
    drive_sum[0] = (drive_hold[0] + drive_relay[0].astype(F32)).astype(BF)
    d_copies[4].start()
    d_copies[1].wait_recv()
    drive_sum[1] = (drive_hold[1] + drive_relay[1].astype(F32)).astype(BF)
    d_copies[5].start()

    readout_load.wait()
    guess = sum(
        jnp.dot(term, rates_t[...], preferred_element_type=F32) for term in split2(readout[...] * (1.0 / 16.0))
    )
    kpart[3 * BLOCK : 3 * BLOCK + OUTS, :] = guess[:, : 2 * BLOCK]
    kpart[3 * BLOCK + OUTS :, :] = jnp.concatenate([guess[:, 2 * BLOCK :], guess[:, 2 * BLOCK :]], axis=1)

    r_ring.wait_sides()
    h[...] += corr_quarter(3)
    h[...] += corr_quarter(1)
    r_ring.wait_far()
    h[...] += corr_quarter(2)

    g_c = sems.take(1)
    core_copy = remote(h.at[aligned((1 - c) * HALF, HALF)], hcore, g_c, sibling)
    whole = sum(jnp.dot(term, rates_t[...], preferred_element_type=F32) for term in split2(h[...]))
    kb = [[whole[r * BLOCK : (r + 1) * BLOCK, s * BLOCK : (s + 1) * BLOCK] for s in range(3)] for r in range(3)]
    kpart[:BLOCK, :] = jnp.concatenate([kb[0][0], kb[1][1]], axis=1)
    kpart[BLOCK : 2 * BLOCK, :] = jnp.concatenate([kb[2][2], kb[1][0]], axis=1)
    kpart[2 * BLOCK : 3 * BLOCK, :] = jnp.concatenate([kb[2][0], kb[2][1]], axis=1)
    k_r = sems.take(16)

    def k_copy(owner, d):
        return remote(kpart.at[aligned(owner * PIECE, PIECE)], krow.at[d - 1], k_r + d, {"row": owner})

    @pl.loop(1, 16)
    def _(d):
        owner = (i + d) % 16

        @pl.when(owner < OWNERS)
        def _():
            k_copy(owner, d).start()

    core_copy.start()

    for k in (2, 3, 4, 5):
        d_copies[k].wait_recv()
    total = drive_mid[...] + jnp.concatenate(
        [drive_x[2].astype(F32) + drive_x[1].astype(F32), drive_x[0].astype(F32) + drive_x[3].astype(F32)], axis=0
    )
    drive_mid[...] = total
    drive_low[...] = total.astype(BF)
    d_z = sems.take(3)

    def drive_z_copy(d):
        theirs = aligned(sigma((zh + d) % 4) * SLICE, SLICE)
        return remote(drive_low.at[theirs], drive_z.at[d - 1], d_z + d - 1, z_dev(d))

    for d in range(1, 4):
        drive_z_copy(d).start()

    k_z = sems.take(3)
    k_x = sems.take(3)

    @pl.when(i < OWNERS)
    def _():
        @pl.loop(1, 16)
        def _(d):
            remote(kpart.at[pl.ds(0, PIECE)], krow.at[d - 1], k_r + d, {"row": (i + 16 - d) % 16}).wait_recv()

        acc = kpart[aligned(i * PIECE, PIECE), :]
        for d in range(15):
            acc = acc + krow[d]
        ksum[...] = acc
        for d in range(1, 4):
            remote(ksum, kz.at[d - 1], k_z + d - 1, z_dev(d)).start()

    core_copy.wait_recv()
    gone[...] = h[half_steps, :] + hcore[...]
    g_y = sems.take(6)
    upper, lower = pl.ds(0, SLICE), pl.ds(SLICE, SLICE)
    y_copies = [
        remote(gone.at[upper, quarter(y + 2)], gy_relay.at[0], g_y, y_dev(1)),
        remote(gone.at[lower, quarter(y + 2)], gy_relay.at[1], g_y + 1, y_dev(3)),
        remote(gone.at[lower, quarter(y + 1)], gy.at[0], g_y + 2, y_dev(1)),
        remote(gone.at[upper, quarter(y + 3)], gy.at[1], g_y + 3, y_dev(3)),
        remote(gy_sum.at[0], gy.at[2], g_y + 4, y_dev(1)),
        remote(gy_sum.at[1], gy.at[3], g_y + 5, y_dev(3)),
    ]
    for k in range(4):
        y_copies[k].start()

    @pl.when(i < OWNERS)
    def _():
        acc = ksum[...]
        for d in range(1, 4):
            copy = remote(ksum, kz.at[d - 1], k_z + d - 1, z_dev(d))
            copy.wait_recv()
            copy.wait_send()
            acc = acc + kz[d - 1]
        kmid[...] = acc
        for d in range(1, 4):
            remote(kmid, kx.at[d - 1], k_x + d - 1, x_dev(d)).start()

    y_copies[0].wait_recv()
    gy_sum[0] = gone[upper, quarter(y + 1)] + gy_relay[0]
    y_copies[4].start()
    y_copies[1].wait_recv()
    gy_sum[1] = gone[lower, quarter(y + 3)] + gy_relay[1]
    y_copies[5].start()

    k_g = sems.take(16)
    own_rows = aligned(i * PIECE, PIECE)

    @pl.when(i < OWNERS)
    def _():
        acc = kmid[...]
        for d in range(1, 4):
            copy = remote(kmid, kx.at[d - 1], k_x + d - 1, x_dev(d))
            copy.wait_recv()
            copy.wait_send()
            acc = acc + kx[d - 1]
        cap[own_rows, :] = acc

        @pl.loop(1, 16)
        def _(d):
            remote(cap.at[own_rows], cap.at[own_rows], k_g + d, {"row": (i + d) % 16}).start()

    targets_load.wait()
    total = drive_mid[my_steps, :]
    for d in range(1, 4):
        copy = drive_z_copy(d)
        copy.wait_recv()
        copy.wait_send()
        total = total + drive_z[d - 1].astype(F32)
    total = total - targets[my_steps, my_quarter].astype(F32)
    err[my_steps, my_quarter] = total.astype(BF)
    e_z = sems.take(3)
    gather_z_start(err, e_z)

    for k in (2, 3, 4, 5):
        y_copies[k].wait_recv()
    gtwo[upper, :] = gone[upper, row_quarter] + gy[2] + gy[1]
    gtwo[lower, :] = gone[lower, row_quarter] + gy[0] + gy[3]
    g_z = sems.take(1)
    gz_copy = remote(gtwo.at[aligned((1 - zl) * SLICE, SLICE)], gz, g_z, neighbour)
    gz_copy.start()

    gather_z_wait(err, e_z)
    e_ring = Ring(err, 0, HALF, x, x_dev)
    e_ring.start()

    gz_copy.wait_recv()
    piece = gtwo[aligned(zl * SLICE, SLICE), :] + gz[...]
    gcol[row_steps, row_quarter] = piece
    gpiece[...] = piece.astype(BF)
    a_z = sems.take(1)
    mine = gcol.at[row_steps, row_quarter]
    az_copy = remote(mine, mine, a_z, neighbour)
    az_copy.start()
    t_g = sems.take(4)
    swap_start(gpiece, grow, t_g)

    e_ring.forward()

    theirs = gcol.at[aligned((c * 2 + 1 - zl) * SLICE, SLICE), row_quarter]
    remote(theirs, theirs, a_z, neighbour).wait_recv()
    y_ring = Ring(gcol, c * HALF, SLICE, y, y_dev)
    y_ring.start()

    swap_wait_recv(gpiece, grow, t_g)
    g_ring = Ring(grow, 0, HALF, x, x_dev)
    g_ring.start()

    @pl.loop(1, 16)
    def _(d):
        owner = (i + 16 - d) % 16

        @pl.when(owner < OWNERS)
        def _():
            theirs = cap.at[aligned(owner * PIECE, PIECE)]
            remote(theirs, theirs, k_g + d, {"row": owner}).wait_recv()

    y_ring.forward()
    g_ring.forward()
    y_ring.wait_sides()
    y_ring.wait_far()
    a_c = sems.take(1)
    mine = gcol.at[half_steps]
    ac_copy = remote(mine, mine, a_c, sibling)
    ac_copy.start()

    e_ring.wait_sides()
    e_ring.wait_far()
    g_ring.wait_sides()
    g_ring.wait_far()
    theirs = gcol.at[aligned((1 - c) * HALF, HALF)]
    remote(theirs, theirs, a_c, sibling).wait_recv()

    swap_wait_send(r_src, rrow, r_t)
    swap_wait_send(gpiece, grow, t_g)
    for copy in d_copies + y_copies + [core_copy, gz_copy, az_copy, ac_copy]:
        copy.wait_send()
    for ring in (r_ring, e_ring, y_ring, g_ring):
        ring.wait_sends()

    @pl.loop(1, 16)
    def _(d):
        owner = (i + d) % 16

        @pl.when(owner < OWNERS)
        def _():
            k_copy(owner, d).wait_send()

        @pl.when(i < OWNERS)
        def _():
            remote(cap.at[own_rows], cap.at[own_rows], k_g + d, {"row": owner}).wait_send()


N_SEMS = 112


def gather_all(rates, targets, readout, corr, rec):
    vmem = pl.BlockSpec(memory_space=pltpu.VMEM)
    hbm = pl.BlockSpec(memory_space=pl.ANY)
    return pl.pallas_call(
        comm_kernel,
        out_shape=[
            jax.ShapeDtypeStruct((PACKED, LANES), F32),
            jax.ShapeDtypeStruct((STEPS, LOCAL), F32),
            jax.ShapeDtypeStruct((STEPS, LOCAL), BF),
            jax.ShapeDtypeStruct((STEPS, LOCAL), BF),
        ],
        in_specs=[hbm] * 5,
        out_specs=[vmem] * 4,
        scratch_shapes=[
            pltpu.VMEM((STEPS, LOCAL), BF),
            pltpu.VMEM((LOCAL, STEPS), BF),
            pltpu.VMEM((STEPS, LOCAL), BF),
            pltpu.VMEM((OUTS, LOCAL), F32),
            pltpu.VMEM((STEPS, LOCAL), BF),
            pltpu.VMEM((LOCAL, LOCAL), F32),
            pltpu.VMEM((LOCAL, LOCAL), BF),
            pltpu.VMEM((STEPS, LOCAL), F32),
            pltpu.VMEM((3, STEPS, QUARTER), BF),
            pltpu.VMEM((2, HALF, QUARTER), F32),
            pltpu.VMEM((2, HALF, QUARTER), BF),
            pltpu.VMEM((2, HALF, QUARTER), BF),
            pltpu.VMEM((4, HALF, QUARTER), BF),
            pltpu.VMEM((STEPS, QUARTER), F32),
            pltpu.VMEM((3, SLICE, QUARTER), BF),
            pltpu.VMEM((STEPS, QUARTER), BF),
            pltpu.VMEM((PACKED, LANES), F32),
            pltpu.VMEM((15, PIECE, LANES), F32),
            pltpu.VMEM((PIECE, LANES), F32),
            pltpu.VMEM((3, PIECE, LANES), F32),
            pltpu.VMEM((PIECE, LANES), F32),
            pltpu.VMEM((3, PIECE, LANES), F32),
            pltpu.VMEM((HALF, LOCAL), F32),
            pltpu.VMEM((HALF, LOCAL), F32),
            pltpu.VMEM((2, SLICE, QUARTER), F32),
            pltpu.VMEM((2, SLICE, QUARTER), F32),
            pltpu.VMEM((4, SLICE, QUARTER), F32),
            pltpu.VMEM((HALF, QUARTER), F32),
            pltpu.VMEM((SLICE, QUARTER), F32),
            pltpu.VMEM((SLICE, QUARTER), BF),
            pltpu.SemaphoreType.DMA((11,)),
            pltpu.SemaphoreType.DMA((N_SEMS,)),
            pltpu.SemaphoreType.DMA((N_SEMS,)),
        ],
        compiler_params=pltpu.CompilerParams(
            collective_id=0, has_side_effects=True, vmem_limit_bytes=VMEM_LIMIT
        ),
        name="exchange",
    )(rates, targets, readout, corr, rec)


SUBS = 8
WIDE = 4


def reciprocal(v):
    r = pl.reciprocal(v, approx=True)
    r = r * (2.0 - v * r)
    return r * (2.0 - v * r)


def factor_two(a, b, d):
    ra = reciprocal(a)
    return b * ra, ra, a * reciprocal(a * d - b * b)


def factor_four(s):
    l = [[None] * WIDE for _ in range(WIDE)]
    l[1][0], rd0, rd1 = factor_two(s[0][0], s[1][0], s[1][1])
    c = {}
    for r in (2, 3):
        l[r][0] = s[r][0] * rd0
        c[r] = s[r][1] - l[1][0] * s[r][0]
        l[r][1] = c[r] * rd1

    def left(r, t):
        return s[r][t] - (l[r][0] * s[t][0] + l[r][1] * c[t])

    l[3][2], rd2, rd3 = factor_two(left(2, 2), left(3, 2), left(3, 3))
    return l, (rd0, rd1, rd2, rd3)


def eliminate(l, v):
    v1 = v[1] - l[1][0] * v[0]
    v2 = v[2] - l[2][0] * v[0] - l[2][1] * v1
    v3 = v[3] - l[3][0] * v[0] - l[3][1] * v1 - l[3][2] * v2
    return v[0], v1, v2, v3


def inverse_block(a):
    rows = [a[u * SUBS : (u + 1) * SUBS] for u in range(BLOCK // SUBS)]
    shape = (SUBS, BLOCK)
    lane = lax.broadcasted_iota(jnp.int32, shape, 1)
    sub = lax.broadcasted_iota(jnp.int32, shape, 0)
    for k in range(0, BLOCK, WIDE):
        v, first = k // SUBS, k % SUBS
        span = range(WIDE)
        col = [[jnp.broadcast_to(row[:, k + b : k + b + 1], shape) for row in rows] for b in span]
        s = [[jnp.broadcast_to(col[b][v][first + a : first + a + 1], shape) for b in range(a + 1)] for a in span]
        inside = (lane >= k) & (lane < k + WIDE)
        top = [
            jnp.where(inside, jnp.where(lane == k + b, 1.0, 0.0), jnp.broadcast_to(rows[v][first + b : first + b + 1], shape))
            for b in span
        ]
        l, rd = factor_four(s)
        top = eliminate(l, top)
        new = [None] * WIDE
        for a in reversed(span):
            new[a] = rd[a] * top[a]
            for b in range(a + 1, WIDE):
                new[a] = new[a] - l[b][a] * new[b]
        for u in range(len(rows)):
            m = eliminate(l, [col[b][u] for b in span])
            drop = ((m[0] * rd[0]) * top[0] + (m[1] * rd[1]) * top[1]) + ((m[2] * rd[2]) * top[2] + (m[3] * rd[3]) * top[3])
            rows[u] = jnp.where(inside, 0.0, rows[u]) - drop
        for a in span:
            rows[v] = jnp.where(sub == first + a, new[a], rows[v])
    return jnp.concatenate(rows, axis=0)


def dot32(a, b):
    return jnp.dot(a, b, precision=HIGH, preferred_element_type=F32)


def update_kernel(
    cap, gcol, grow, err, goal, readout, corr, rec, corr_out, rec_out, readout_out,
    minv, d_hi, d_lo,
):
    @pl.when(pl.program_id(0) == 0)
    def _():
        blocks = range(STEPS // BLOCK)
        eye = jnp.where(
            lax.broadcasted_iota(jnp.int32, (BLOCK, BLOCK), 0) == lax.broadcasted_iota(jnp.int32, (BLOCK, BLOCK), 1),
            1.0, 0.0,
        )
        packed = [
            [cap[r * BLOCK : (r + 1) * BLOCK, :BLOCK], cap[r * BLOCK : (r + 1) * BLOCK, BLOCK:]] for r in blocks
        ]
        (k00, k11), (k22, k10), (k20, k21) = packed
        a = [[k00 + eye, k10.T, k20.T], [k10, k11 + eye, k21.T], [k20, k21, k22 + eye]]
        for k in blocks:
            inv = inverse_block(a[k][k])
            new = [[None] * len(blocks) for _ in blocks]
            new[k][k] = inv
            for s in blocks:
                if s != k:
                    new[k][s] = dot32(inv, a[k][s])
            for r in blocks:
                if r != k:
                    new[r][k] = -dot32(a[r][k], inv)
                    for s in blocks:
                        if s != k:
                            new[r][s] = a[r][s] - dot32(a[r][k], new[k][s])
            a = new
        for r in blocks:
            for s in blocks:
                minv[r * BLOCK : (r + 1) * BLOCK, s * BLOCK : (s + 1) * BLOCK] = a[r][s]
        scaled = dot32(minv[...], gcol[...])
        hi, lo = split2(scaled)
        d_hi[...] = hi
        d_lo[...] = lo
        guess = jnp.concatenate(
            [cap[3 * BLOCK : 3 * BLOCK + OUTS, :], cap[3 * BLOCK + OUTS :, :BLOCK]], axis=1
        )
        readout_out[...] = readout[...] - dot32(guess - goal[...], scaled)

    def times(left):
        return lax.dot_general(left, d_hi[...], TN, preferred_element_type=F32) + lax.dot_general(
            left, d_lo[...], TN, preferred_element_type=F32
        )

    corr_out[...] = corr[...] - times(grow[...])
    rec_out[...] = (rec[...].astype(F32) - times(err[...])).astype(BF)


TILE = 128


def update(cap, gcol, grow, err, goal, readout, corr, rec):
    def whole(shape):
        return pl.BlockSpec(shape, lambda g: (0, 0))

    rows = pl.BlockSpec((TILE, LOCAL), lambda g: (g, 0))
    left = pl.BlockSpec((STEPS, TILE), lambda g: (0, g))
    return pl.pallas_call(
        update_kernel,
        grid=(LOCAL // TILE,),
        out_shape=[
            jax.ShapeDtypeStruct((LOCAL, LOCAL), F32),
            jax.ShapeDtypeStruct((LOCAL, LOCAL), BF),
            jax.ShapeDtypeStruct((OUTS, LOCAL), F32),
        ],
        in_specs=[
            whole((PACKED, LANES)), whole((STEPS, LOCAL)), left, left, whole((OUTS, STEPS)), whole((OUTS, LOCAL)),
            rows, rows,
        ],
        out_specs=[rows, rows, whole((OUTS, LOCAL))],
        scratch_shapes=[
            pltpu.VMEM((STEPS, STEPS), F32),
            pltpu.VMEM((STEPS, LOCAL), BF),
            pltpu.VMEM((STEPS, LOCAL), BF),
        ],
        compiler_params=pltpu.CompilerParams(vmem_limit_bytes=VMEM_LIMIT),
        name="update",
    )(cap, gcol, grow, err, goal, readout, corr, rec)


def on_device(rates, targets, goal, corr, rec, readout):
    cap, gcol, grow, err = gather_all(rates, targets, readout, corr, rec)
    return tuple(update(cap, gcol, grow, err, goal, readout, corr, rec))


def solution(mesh):
    placed = (P(None, "col"), P(None, "row"), P(), P("row", "col"), P("row", "col"), P(None, "col"))
    return jax.shard_map(
        on_device,
        mesh=mesh,
        in_specs=placed,
        out_specs=(P("row", "col"), P("row", "col"), P(None, "col")),
        check_vma=False,
    )
```

```python
import functools

import jax
import jax.numpy as jnp
from jax import lax
from jax.experimental import pallas as pl
from jax.experimental.pallas import tpu as pltpu
from jax.sharding import PartitionSpec as P

MESH = pl.DeviceIdType.MESH
BF, F32 = jnp.bfloat16, jnp.float32
HIGH = lax.Precision.HIGHEST

STEPS = 192
LOCAL = 1024
OUTS = 16
QUARTER = 256
GROUP = 64
PIECE = 16
BLOCK = 64
PACKED = 3 * BLOCK + 2 * OUTS
OWNERS = PACKED // PIECE
LANES = 128
FOLDED = GROUP * STEPS // LANES
NT = (((1,), (1,)), ((), ()))
VMEM_LIMIT = 60 * 1024 * 1024


def split2(x):
    hi = x.astype(BF)
    return hi, (x - hi.astype(F32)).astype(BF)


def aligned(start, size):
    return pl.ds(pl.multiple_of(start, size), size)


def fold(v):
    low = jnp.concatenate([v[: GROUP // 2, LANES:], v[GROUP // 2 :, LANES:]], axis=1)
    return jnp.concatenate([v[:, :LANES], low], axis=0)


def unfold(v):
    rest = STEPS - LANES
    high = jnp.concatenate([v[GROUP:, :rest], v[GROUP:, rest:]], axis=0)
    return jnp.concatenate([v[:GROUP], high], axis=1)


def groups(v):
    return [v[g * GROUP : (g + 1) * GROUP] for g in range(v.shape[0] // GROUP)]


class Sems:
    def __init__(self):
        self.at = 0

    def take(self, count):
        first = self.at
        self.at += count
        return first


SUBS = 8
WIDE = 4


def reciprocal(v):
    r = pl.reciprocal(v, approx=True)
    r = r * (2.0 - v * r)
    return r * (2.0 - v * r)


def factor_two(a, b, d):
    ra = reciprocal(a)
    return b * ra, ra, a * reciprocal(a * d - b * b)


def factor_four(s):
    l = [[None] * WIDE for _ in range(WIDE)]
    l[1][0], rd0, rd1 = factor_two(s[0][0], s[1][0], s[1][1])
    c = {}
    for r in (2, 3):
        l[r][0] = s[r][0] * rd0
        c[r] = s[r][1] - l[1][0] * s[r][0]
        l[r][1] = c[r] * rd1

    def left(r, t):
        return s[r][t] - (l[r][0] * s[t][0] + l[r][1] * c[t])

    l[3][2], rd2, rd3 = factor_two(left(2, 2), left(3, 2), left(3, 3))
    return l, (rd0, rd1, rd2, rd3)


def eliminate(l, v):
    v1 = v[1] - l[1][0] * v[0]
    v2 = v[2] - l[2][0] * v[0] - l[2][1] * v1
    v3 = v[3] - l[3][0] * v[0] - l[3][1] * v1 - l[3][2] * v2
    return v[0], v1, v2, v3


def inverse_block(a, services):
    rows = [a[u * SUBS : (u + 1) * SUBS] for u in range(BLOCK // SUBS)]
    shape = (SUBS, BLOCK)
    lane = lax.broadcasted_iota(jnp.int32, shape, 1)
    sub = lax.broadcasted_iota(jnp.int32, shape, 0)
    for k in range(0, BLOCK, WIDE):
        v, first = k // SUBS, k % SUBS
        span = range(WIDE)
        col = [[jnp.broadcast_to(row[:, k + b : k + b + 1], shape) for row in rows] for b in span]
        s = [[jnp.broadcast_to(col[b][v][first + a : first + a + 1], shape) for b in range(a + 1)] for a in span]
        inside = (lane >= k) & (lane < k + WIDE)
        top = [
            jnp.where(inside, jnp.where(lane == k + b, 1.0, 0.0), jnp.broadcast_to(rows[v][first + b : first + b + 1], shape))
            for b in span
        ]
        l, rd = factor_four(s)
        top = eliminate(l, top)
        new = [None] * WIDE
        for a in reversed(span):
            new[a] = rd[a] * top[a]
            for b in range(a + 1, WIDE):
                new[a] = new[a] - l[b][a] * new[b]
        for u in range(len(rows)):
            m = eliminate(l, [col[b][u] for b in span])
            drop = ((m[0] * rd[0]) * top[0] + (m[1] * rd[1]) * top[1]) + ((m[2] * rd[2]) * top[2] + (m[3] * rd[3]) * top[3])
            rows[u] = jnp.where(inside, 0.0, rows[u]) - drop
        for a in span:
            rows[v] = jnp.where(sub == first + a, new[a], rows[v])
        if k % (4 * WIDE) == 3 * WIDE:
            for serve in services:
                serve()
                break
    return jnp.concatenate(rows, axis=0)


def dot32(a, b):
    return jnp.dot(a, b, precision=HIGH, preferred_element_type=F32)


def invert(cap, minv, services):
    blocks = range(STEPS // BLOCK)
    shape = (BLOCK, BLOCK)
    eye = jnp.where(lax.broadcasted_iota(jnp.int32, shape, 0) == lax.broadcasted_iota(jnp.int32, shape, 1), 1.0, 0.0)
    (k00, k11), (k22, k10), (k20, k21) = [
        [cap[r * BLOCK : (r + 1) * BLOCK, :BLOCK], cap[r * BLOCK : (r + 1) * BLOCK, BLOCK:]] for r in blocks
    ]
    a = [[k00 + eye, k10.T, k20.T], [k10, k11 + eye, k21.T], [k20, k21, k22 + eye]]
    for k in blocks:
        inv = inverse_block(a[k][k], services)
        new = [[None] * len(blocks) for _ in blocks]
        new[k][k] = inv
        for s in blocks:
            if s != k:
                new[k][s] = dot32(inv, a[k][s])
        for r in blocks:
            if r != k:
                new[r][k] = -dot32(a[r][k], inv)
                for s in blocks:
                    if s != k:
                        new[r][s] = a[r][s] - dot32(a[r][k], new[k][s])
        a = new
    for r in blocks:
        for s in blocks:
            minv[r * BLOCK : (r + 1) * BLOCK, s * BLOCK : (s + 1) * BLOCK] = a[r][s]


def comm_kernel(
    rates_hbm, targets_hbm, readout_hbm, corr_hbm, rec_hbm,
    minv_out, guess_out, gcol_out, left_out,
    rates, rates_t, targets, readout, rx, corr_v, rec_v,
    g_part, g_mid, g_relay, g_sum, g_x, g_z, g_piece, g_all, g_col,
    e_part, e_hold, e_mid, e_relay, e_sum, e_x, e_low, e_z, left,
    kpart, krow, ksum, kz, kmid, kx, cap, minv,
    load_sem, store_sem, send_sem, recv_sem,
):
    i = lax.axis_index("row")
    j = lax.axis_index("col")
    y, zl, c = i // 4, (i // 2) % 2, i % 2
    x, zh = j // 4, j % 4
    sems = Sems()

    def quarter(q):
        return aligned((q % 4) * QUARTER, QUARTER)

    def remote(src, dst, at, dev, land=None):
        return pltpu.make_async_remote_copy(
            src_ref=src, dst_ref=dst, send_sem=send_sem.at[at], recv_sem=recv_sem.at[at if land is None else land],
            device_id=dev, device_id_type=MESH,
        )

    def load(src, dst, at):
        copy = pltpu.make_async_copy(src, dst, load_sem.at[at])
        copy.start()
        return copy

    rates_load = load(rates_hbm, rates, 8)
    rec_loads, corr_loads = {}, {}
    for d in (2, 1, 3, 0):
        part = quarter(x + d)
        corr_loads[d] = load(corr_hbm.at[part], corr_v.at[part], 4 + d)
    for d in (2, 1, 3, 0):
        part = quarter(x + d)
        rec_loads[d] = load(rec_hbm.at[part], rec_v.at[part], d)
    readout_load = load(readout_hbm, readout, 9)
    targets_load = load(targets_hbm, targets, 10)

    barrier = pltpu.get_barrier_semaphore()

    def greet(dev):
        pl.semaphore_signal(barrier, inc=1, device_id=dev, device_id_type=MESH)

    @pl.loop(1, 16)
    def _(d):
        greet({"row": (i + d) % 16})

    for d in range(1, 4):
        greet({"col": x * 4 + (zh + d) % 4})
        greet({"col": ((x + d) % 4) * 4 + zh})

    for z in range(4):

        @pl.when((i != j) | (zh != z))
        def _():
            greet({"row": j, "col": y * 4 + z})

    rates_load.wait()
    rates_t[...] = rates[...].T
    pl.semaphore_wait(barrier, jnp.where(i == j, 24, 25))

    def z_dev(d):
        return {"col": x * 4 + (zh + d) % 4}

    def x_dev(d):
        return {"col": ((x + d) % 4) * 4 + zh}

    def y_dev(d):
        return {"row": ((y + d) % 4) * 4 + zl * 2 + c}

    class RingSum:
        def __init__(self, part, hold, relay, total, landed):
            self.part, self.hold, self.relay, self.total, self.landed = part, hold, relay, total, landed
            at = sems.take(6)
            top, low = pl.ds(0, 2), pl.ds(2, 2)
            self.copies = [
                remote(part.at[0, top], relay.at[0], at, x_dev(1)),
                remote(part.at[0, low], relay.at[1], at + 1, x_dev(3)),
                remote(part.at[1, low], landed.at[0], at + 2, x_dev(1)),
                remote(part.at[2, top], landed.at[1], at + 3, x_dev(3)),
                remote(total.at[0], landed.at[2], at + 4, x_dev(1)),
                remote(total.at[1], landed.at[3], at + 5, x_dev(3)),
            ]

        def start(self, *which):
            for k in which:
                self.copies[k].start()

        def forward(self):
            for k in range(2):
                self.copies[k].wait_recv()
                self.total[k] = (self.hold(k) + self.relay[k].astype(F32)).astype(self.total.dtype)
                self.copies[4 + k].start()

        def finish(self, own):
            for k in range(2, 6):
                self.copies[k].wait_recv()
            got = [self.landed[k].astype(F32) for k in range(4)]
            own[:2] = own[:2] + got[2] + got[1]
            own[2:] = own[2:] + got[0] + got[3]

        def wait_sends(self):
            for copy in self.copies:
                copy.wait_send()

    class Ring:
        def __init__(self, block, me, dev):
            self.block, self.me, self.dev = block, me, dev
            self.at = sems.take(6)

        def copy(self, k, owner):
            block = self.block((0, 1, 1, 0, 0, 1)[k], owner % 4)
            return remote(block, block, self.at + k, self.dev((1, 1, 3, 3, 1, 3)[k]))

        def start(self):
            for k in (0, 2, 1, 3):
                self.copy(k, self.me).start()

        def forward(self):
            self.copy(0, self.me + 3).wait_recv()
            self.copy(4, self.me + 3).start()
            self.copy(2, self.me + 1).wait_recv()
            self.copy(5, self.me + 1).start()

        def finish(self):
            self.copy(1, self.me + 3).wait_recv()
            self.copy(3, self.me + 1).wait_recv()
            self.copy(4, self.me + 2).wait_recv()
            self.copy(5, self.me + 2).wait_recv()

        def wait_sends(self):
            for k in range(4):
                self.copy(k, self.me).wait_send()
            self.copy(4, self.me + 3).wait_send()
            self.copy(5, self.me + 1).wait_send()

    def prod_quarter(d, out):
        corr_loads[d].wait()
        hi, lo = split2(corr_v[quarter(x + d), :])
        value = jnp.dot(hi, rates_t[...], preferred_element_type=F32) + jnp.dot(
            lo, rates_t[...], preferred_element_type=F32
        )
        for g, part in enumerate(groups(value)):
            out[g] = fold(part)

    def drive_quarter(d):
        rec_loads[d].wait()
        value = jnp.dot(rec_v[quarter(x + d), :], rates_t[...], preferred_element_type=F32)
        return [fold(part) for part in groups(value)]

    g_ring = RingSum(g_part, lambda k: g_part[1, :2] if k == 0 else g_part[2, 2:], g_relay, g_sum, g_x)
    prod_quarter(2, g_part.at[0])
    g_ring.start(0, 1)
    prod_quarter(1, g_part.at[1])
    g_ring.start(2)
    prod_quarter(3, g_part.at[2])
    g_ring.start(3)

    r_t = sems.take(1)
    r_src = rates.at[:, quarter(y)]

    @pl.when(i != j)
    def _():
        remote(r_src, rx, r_t, {"row": j, "col": i}).start()

    @pl.when(i == j)
    def _():
        pltpu.make_async_copy(r_src, rx, recv_sem.at[r_t]).start()

    prod_quarter(0, g_mid)
    g_ring.forward()

    e_ring = RingSum(e_part, lambda k: e_hold[k], e_relay, e_sum, e_x)
    for g, part in enumerate(drive_quarter(2)):
        e_part[0, g] = part.astype(BF)
    e_ring.start(0, 1)
    for g, part in enumerate(drive_quarter(1)):
        if g < 2:
            e_hold[0, g] = part
        else:
            e_part[1, g] = part.astype(BF)
    e_ring.start(2)
    for g, part in enumerate(drive_quarter(3)):
        if g < 2:
            e_part[2, g] = part.astype(BF)
        else:
            e_hold[1, g - 2] = part
    e_ring.start(3)

    readout_load.wait()
    guess = sum(
        jnp.dot(term, rates_t[...], preferred_element_type=F32) for term in split2(readout[...] * (1.0 / 16.0))
    )
    kpart[3 * BLOCK : 3 * BLOCK + OUTS, :] = guess[:, :LANES]
    kpart[3 * BLOCK + OUTS :, :] = jnp.concatenate([guess[:, LANES:], guess[:, LANES:]], axis=1)

    g_ring.finish(g_mid)
    g_at = sems.take(3)

    def g_z_copy(d):
        return remote(g_mid.at[(zh + d) % 4], g_z.at[d - 1], g_at + d - 1, z_dev(d))

    for d in range(1, 4):
        g_z_copy(d).start()

    @pl.when(i != j)
    def _():
        remote(r_src, rx, r_t, {"row": j, "col": i}).wait_recv()

    @pl.when(i == j)
    def _():
        pltpu.make_async_copy(r_src, rx, recv_sem.at[r_t]).wait()

    whole = sum(
        jnp.dot(rx[...], term, preferred_element_type=F32)
        for term in split2(jnp.concatenate([unfold(g_mid[g]) for g in range(4)], axis=0))
    )
    kb = [[whole[r * BLOCK : (r + 1) * BLOCK, s * BLOCK : (s + 1) * BLOCK] for s in range(3)] for r in range(3)]
    kpart[:BLOCK, :] = jnp.concatenate([kb[0][0], kb[1][1]], axis=1)
    kpart[BLOCK : 2 * BLOCK, :] = jnp.concatenate([kb[2][2], kb[1][0]], axis=1)
    kpart[2 * BLOCK : 3 * BLOCK, :] = jnp.concatenate([kb[2][0], kb[2][1]], axis=1)

    k_r = sems.take(16)

    def k_copy(owner, d):
        return remote(kpart.at[aligned(owner * PIECE, PIECE)], krow.at[d - 1], k_r + d, {"row": owner})

    @pl.loop(1, 16)
    def _(d):
        owner = (i + d) % 16

        @pl.when(owner < OWNERS)
        def _():
            k_copy(owner, d).start()

    e_ring.forward()
    for g, part in enumerate(drive_quarter(0)):
        e_mid[g] = part

    k_z = sems.take(3)
    k_x = sems.take(3)

    @pl.when(i < OWNERS)
    def _():
        @pl.loop(1, 16)
        def _(d):
            remote(kpart.at[pl.ds(0, PIECE)], krow.at[d - 1], k_r + d, {"row": (i + 16 - d) % 16}).wait_recv()

        acc = kpart[aligned(i * PIECE, PIECE), :]
        for d in range(15):
            acc = acc + krow[d]
        ksum[...] = acc
        for d in range(1, 4):
            remote(ksum, kz.at[d - 1], k_z + d - 1, z_dev(d)).start()

    for d in range(1, 4):
        g_z_copy(d).wait_recv()
    piece = g_mid[zh] + g_z[0] + g_z[1] + g_z[2]
    g_piece[...] = piece
    own = aligned(x * QUARTER + zh * GROUP, GROUP)
    left[own, STEPS:] = unfold(piece).astype(BF)
    s_t = sems.take(4)

    def swap_each(act_remote, act_local):
        for e in range(4):
            dst = g_all.at[x * 4 + zh]

            @pl.when((i != j) | (i % 4 != e))
            def _():
                act_remote(remote(g_piece, dst, s_t + e, {"row": x * 4 + e, "col": i}, s_t + zh))

            if act_local is not None:

                @pl.when((i == j) & (i % 4 == e))
                def _():
                    act_local(pltpu.make_async_copy(g_piece, dst, recv_sem.at[s_t + zh]))

    swap_each(lambda copy: copy.start(), lambda copy: copy.start())

    e_ring.finish(e_mid)
    e_low[...] = e_mid[...].astype(BF)
    e_at = sems.take(3)

    def e_z_copy(d):
        return remote(e_low.at[(zh + d) % 4], e_z.at[d - 1], e_at + d - 1, z_dev(d))

    for d in range(1, 4):
        e_z_copy(d).start()

    @pl.when(i < OWNERS)
    def _():
        acc = ksum[...]
        for d in range(1, 4):
            copy = remote(ksum, kz.at[d - 1], k_z + d - 1, z_dev(d))
            copy.wait_recv()
            copy.wait_send()
            acc = acc + kz[d - 1]
        kmid[...] = acc
        for d in range(1, 4):
            remote(kmid, kx.at[d - 1], k_x + d - 1, x_dev(d)).start()

    targets_load.wait()
    aims = targets[:, quarter(x)].T
    e_hold[0] = jnp.stack([fold(part) for part in groups(aims[:LANES].astype(F32))])
    e_hold[1] = jnp.stack([fold(part) for part in groups(aims[LANES:].astype(F32))])

    k_g = sems.take(16)
    own_rows = aligned(i * PIECE, PIECE)

    @pl.when(i < OWNERS)
    def _():
        acc = kmid[...]
        for d in range(1, 4):
            copy = remote(kmid, kx.at[d - 1], k_x + d - 1, x_dev(d))
            copy.wait_recv()
            copy.wait_send()
            acc = acc + kx[d - 1]
        cap[own_rows, :] = acc

        @pl.loop(1, 16)
        def _(d):
            remote(cap.at[own_rows], cap.at[own_rows], k_g + d, {"row": (i + d) % 16}).start()

    for d in range(1, 4):
        e_z_copy(d).wait_recv()
    total = e_mid[zh] - e_hold[zh // 2, zh % 2]
    for d in range(3):
        total = total + e_z[d].astype(F32)
    left[own, :STEPS] = unfold(total).astype(BF)
    l_z = sems.take(3)

    def l_z_copy(d, z):
        rows = left.at[aligned(x * QUARTER + (z % 4) * GROUP, GROUP)]
        return remote(rows, rows, l_z + d - 1, z_dev(d))

    for d in range(1, 4):
        l_z_copy(d, zh).start()

    for z in range(4):
        dst = g_all.at[y * 4 + z]

        @pl.when((i != j) | (zh != z))
        def _():
            remote(g_piece, dst, s_t, {"row": j, "col": y * 4 + z}, s_t + z).wait_recv()

        @pl.when((i == j) & (zh == z))
        def _():
            pltpu.make_async_copy(g_piece, dst, recv_sem.at[s_t + z]).wait()

    y_ring = Ring(lambda half, owner: g_all.at[pl.ds(owner * 4 + half * 2, 2)], y, y_dev)
    y_ring.start()

    for d in range(1, 4):
        l_z_copy(d, zh + 4 - d).wait_recv()
    l_ring = Ring(lambda half, owner: left.at[aligned(owner * QUARTER + half * LANES, LANES)], x, x_dev)
    l_ring.start()

    @pl.loop(1, 16)
    def _(d):
        owner = (i + 16 - d) % 16

        @pl.when(owner < OWNERS)
        def _():
            theirs = cap.at[aligned(owner * PIECE, PIECE)]
            remote(theirs, theirs, k_g + d, {"row": owner}).wait_recv()

    stores = [
        pltpu.make_async_copy(left, left_out, store_sem.at[0]),
        pltpu.make_async_copy(g_col, gcol_out, store_sem.at[1]),
        pltpu.make_async_copy(cap.at[pl.ds(3 * BLOCK, 2 * OUTS)], guess_out, store_sem.at[2]),
        pltpu.make_async_copy(minv, minv_out, store_sem.at[3]),
    ]
    stores[2].start()

    def serve_left():
        l_ring.finish()
        stores[0].start()

    def serve_y():
        y_ring.finish()

        @pl.loop(0, LOCAL // GROUP)
        def _(g):
            g_col[aligned(g * GROUP, GROUP), :] = unfold(g_all[g])

        stores[1].start()

    def rest():
        pass

    invert(cap, minv, iter((rest, y_ring.forward, l_ring.forward, rest, rest, serve_y, rest, serve_left)))
    stores[3].start()

    @pl.when(i != j)
    def _():
        remote(r_src, rx, r_t, {"row": j, "col": i}).wait_send()

    swap_each(lambda copy: copy.wait_send(), None)
    for d in range(1, 4):
        g_z_copy(d).wait_send()
        e_z_copy(d).wait_send()
        l_z_copy(d, zh).wait_send()
    for ring in (g_ring, e_ring, y_ring, l_ring):
        ring.wait_sends()

    @pl.loop(1, 16)
    def _(d):
        owner = (i + d) % 16

        @pl.when(owner < OWNERS)
        def _():
            k_copy(owner, d).wait_send()

        @pl.when(i < OWNERS)
        def _():
            remote(cap.at[own_rows], cap.at[own_rows], k_g + d, {"row": owner}).wait_send()

    for store in stores:
        store.wait()


N_SEMS = 96


def gather_all(rates, targets, readout, corr, rec):
    hbm = pl.BlockSpec(memory_space=pl.ANY)

    def folded(dtype, *lead):
        return pltpu.VMEM((*lead, FOLDED, LANES), dtype)

    return pl.pallas_call(
        comm_kernel,
        out_shape=[
            jax.ShapeDtypeStruct((STEPS, STEPS), F32),
            jax.ShapeDtypeStruct((2 * OUTS, LANES), F32),
            jax.ShapeDtypeStruct((LOCAL, STEPS), F32),
            jax.ShapeDtypeStruct((LOCAL, 2 * STEPS), BF),
        ],
        in_specs=[hbm] * 5,
        out_specs=[hbm] * 4,
        scratch_shapes=[
            pltpu.VMEM((STEPS, LOCAL), BF),
            pltpu.VMEM((LOCAL, STEPS), BF),
            pltpu.VMEM((STEPS, LOCAL), BF),
            pltpu.VMEM((OUTS, LOCAL), F32),
            pltpu.VMEM((STEPS, QUARTER), BF),
            pltpu.VMEM((LOCAL, LOCAL), F32),
            pltpu.VMEM((LOCAL, LOCAL), BF),
            folded(F32, 3, 4),
            folded(F32, 4),
            folded(F32, 2, 2),
            folded(F32, 2, 2),
            folded(F32, 4, 2),
            folded(F32, 3),
            folded(F32),
            folded(F32, 16),
            pltpu.VMEM((LOCAL, STEPS), F32),
            folded(BF, 3, 4),
            folded(F32, 2, 2),
            folded(F32, 4),
            folded(BF, 2, 2),
            folded(BF, 2, 2),
            folded(BF, 4, 2),
            folded(BF, 4),
            folded(BF, 3),
            pltpu.VMEM((LOCAL, 2 * STEPS), BF),
            pltpu.VMEM((PACKED, LANES), F32),
            pltpu.VMEM((15, PIECE, LANES), F32),
            pltpu.VMEM((PIECE, LANES), F32),
            pltpu.VMEM((3, PIECE, LANES), F32),
            pltpu.VMEM((PIECE, LANES), F32),
            pltpu.VMEM((3, PIECE, LANES), F32),
            pltpu.VMEM((PACKED, LANES), F32),
            pltpu.VMEM((STEPS, STEPS), F32),
            pltpu.SemaphoreType.DMA((11,)),
            pltpu.SemaphoreType.DMA((4,)),
            pltpu.SemaphoreType.DMA((N_SEMS,)),
            pltpu.SemaphoreType.DMA((N_SEMS,)),
        ],
        compiler_params=pltpu.CompilerParams(
            collective_id=0, has_side_effects=True, vmem_limit_bytes=VMEM_LIMIT
        ),
        name="exchange",
    )(rates, targets, readout, corr, rec)


def update_kernel(
    minv, guess, gcol, left, goal, readout, corr, rec, corr_out, rec_out, readout_out, scaled,
):
    @pl.when(pl.program_id(0) == 0)
    def _():
        m_hi, m_lo = split2(minv[...])
        g_hi, g_lo = split2(gcol[...])
        value = sum(
            lax.dot_general(m, g, NT, preferred_element_type=F32) for m, g in ((m_hi, g_lo), (m_lo, g_hi), (m_hi, g_hi))
        )
        scaled[...] = value.astype(BF)
        drive = jnp.concatenate([guess[:OUTS, :], guess[OUTS:, : STEPS - LANES]], axis=1)
        readout_out[...] = readout[...] - dot32(drive - goal[...], value)

    drop = jnp.dot(left[:, STEPS:], scaled[...], preferred_element_type=F32)
    corr_out[...] = corr[...] - drop
    drop = jnp.dot(left[:, :STEPS], scaled[...], preferred_element_type=F32)
    rec_out[...] = (rec[...].astype(F32) - drop).astype(BF)


TILE = 256


def update(minv, guess, gcol, left, goal, readout, corr, rec):
    def whole(shape):
        return pl.BlockSpec(shape, lambda g: (0, 0))

    rows = pl.BlockSpec((TILE, LOCAL), lambda g: (g, 0))
    factors = pl.BlockSpec((TILE, 2 * STEPS), lambda g: (g, 0))
    return pl.pallas_call(
        update_kernel,
        grid=(LOCAL // TILE,),
        out_shape=[
            jax.ShapeDtypeStruct((LOCAL, LOCAL), F32),
            jax.ShapeDtypeStruct((LOCAL, LOCAL), BF),
            jax.ShapeDtypeStruct((OUTS, LOCAL), F32),
        ],
        in_specs=[
            whole((STEPS, STEPS)), whole((2 * OUTS, LANES)), whole((LOCAL, STEPS)), factors, whole((OUTS, STEPS)),
            whole((OUTS, LOCAL)), rows, rows,
        ],
        out_specs=[rows, rows, whole((OUTS, LOCAL))],
        scratch_shapes=[pltpu.VMEM((STEPS, LOCAL), BF)],
        compiler_params=pltpu.CompilerParams(vmem_limit_bytes=VMEM_LIMIT),
        name="update",
    )(minv, guess, gcol, left, goal, readout, corr, rec)


def on_device(rates, targets, goal, corr, rec, readout):
    minv, guess, gcol, left = gather_all(rates, targets, readout, corr, rec)
    return tuple(update(minv, guess, gcol, left, goal, readout, corr, rec))


def solution(mesh):
    placed = (P(None, "col"), P(None, "row"), P(), P("row", "col"), P("row", "col"), P(None, "col"))
    return jax.shard_map(
        on_device,
        mesh=mesh,
        in_specs=placed,
        out_specs=(P("row", "col"), P("row", "col"), P(None, "col")),
        check_vma=False,
    )
```

```python
import functools

import jax
import jax.numpy as jnp
from jax import lax
from jax.experimental import pallas as pl
from jax.experimental.pallas import tpu as pltpu
from jax.sharding import PartitionSpec as P

MESH = pl.DeviceIdType.MESH
BF, F32 = jnp.bfloat16, jnp.float32
HIGH = lax.Precision.HIGHEST

STEPS = 192
LOCAL = 1024
OUTS = 16
QUARTER = 256
GROUP = 64
PIECE = 16
BLOCK = 64
PACKED = 3 * BLOCK + 2 * OUTS
OWNERS = PACKED // PIECE
LANES = 128
FOLDED = GROUP * STEPS // LANES
NT = (((1,), (1,)), ((), ()))
VMEM_LIMIT = 60 * 1024 * 1024


def split2(x):
    hi = x.astype(BF)
    return hi, (x - hi.astype(F32)).astype(BF)


def aligned(start, size):
    return pl.ds(pl.multiple_of(start, size), size)


def fold(v):
    low = jnp.concatenate([v[: GROUP // 2, LANES:], v[GROUP // 2 :, LANES:]], axis=1)
    return jnp.concatenate([v[:, :LANES], low], axis=0)


def unfold(v):
    rest = STEPS - LANES
    high = jnp.concatenate([v[GROUP:, :rest], v[GROUP:, rest:]], axis=0)
    return jnp.concatenate([v[:GROUP], high], axis=1)


def groups(v):
    return [v[g * GROUP : (g + 1) * GROUP] for g in range(v.shape[0] // GROUP)]


class Sems:
    def __init__(self):
        self.at = 0

    def take(self, count):
        first = self.at
        self.at += count
        return first


SUBS = 8
WIDE = 4


def reciprocal(v):
    return pl.reciprocal(v, approx=True)


def factor_two(a, b, d):
    ra = reciprocal(a)
    return b * ra, ra, a * reciprocal(a * d - b * b)


def factor_four(s):
    l = [[None] * WIDE for _ in range(WIDE)]
    l[1][0], rd0, rd1 = factor_two(s[0][0], s[1][0], s[1][1])
    c = {}
    for r in (2, 3):
        l[r][0] = s[r][0] * rd0
        c[r] = s[r][1] - l[1][0] * s[r][0]
        l[r][1] = c[r] * rd1

    def left(r, t):
        return s[r][t] - (l[r][0] * s[t][0] + l[r][1] * c[t])

    l[3][2], rd2, rd3 = factor_two(left(2, 2), left(3, 2), left(3, 3))
    return l, (rd0, rd1, rd2, rd3)


def eliminate(l, v):
    v1 = v[1] - l[1][0] * v[0]
    v2 = v[2] - l[2][0] * v[0] - l[2][1] * v1
    v3 = v[3] - l[3][0] * v[0] - l[3][1] * v1 - l[3][2] * v2
    return v[0], v1, v2, v3


def inverse_block(a, services):
    rows = [a[u * SUBS : (u + 1) * SUBS] for u in range(BLOCK // SUBS)]
    shape = (SUBS, BLOCK)
    lane = lax.broadcasted_iota(jnp.int32, shape, 1)
    sub = lax.broadcasted_iota(jnp.int32, shape, 0)
    for k in range(0, BLOCK, WIDE):
        v, first = k // SUBS, k % SUBS
        span = range(WIDE)
        col = [[jnp.broadcast_to(row[:, k + b : k + b + 1], shape) for row in rows] for b in span]
        s = [[jnp.broadcast_to(col[b][v][first + a : first + a + 1], shape) for b in range(a + 1)] for a in span]
        inside = (lane >= k) & (lane < k + WIDE)
        top = [
            jnp.where(inside, jnp.where(lane == k + b, 1.0, 0.0), jnp.broadcast_to(rows[v][first + b : first + b + 1], shape))
            for b in span
        ]
        l, rd = factor_four(s)
        top = eliminate(l, top)
        new = [None] * WIDE
        for a in reversed(span):
            new[a] = rd[a] * top[a]
            for b in range(a + 1, WIDE):
                new[a] = new[a] - l[b][a] * new[b]
        for u in range(len(rows)):
            m = eliminate(l, [col[b][u] for b in span])
            drop = ((m[0] * rd[0]) * top[0] + (m[1] * rd[1]) * top[1]) + ((m[2] * rd[2]) * top[2] + (m[3] * rd[3]) * top[3])
            rows[u] = jnp.where(inside, 0.0, rows[u]) - drop
        for a in span:
            rows[v] = jnp.where(sub == first + a, new[a], rows[v])
        if k % (4 * WIDE) == 3 * WIDE:
            for serve in services:
                serve()
                break
    return jnp.concatenate(rows, axis=0)


def dot32(a, b):
    return jnp.dot(a, b, precision=HIGH, preferred_element_type=F32)


def invert(cap, minv, services):
    blocks = range(STEPS // BLOCK)
    shape = (BLOCK, BLOCK)
    eye = jnp.where(lax.broadcasted_iota(jnp.int32, shape, 0) == lax.broadcasted_iota(jnp.int32, shape, 1), 1.0, 0.0)
    (k00, k11), (k22, k10), (k20, k21) = [
        [cap[r * BLOCK : (r + 1) * BLOCK, :BLOCK], cap[r * BLOCK : (r + 1) * BLOCK, BLOCK:]] for r in blocks
    ]
    a = [[k00 + eye, k10.T, k20.T], [k10, k11 + eye, k21.T], [k20, k21, k22 + eye]]
    for k in blocks:
        inv = inverse_block(a[k][k], services)
        new = [[None] * len(blocks) for _ in blocks]
        new[k][k] = inv
        for s in blocks:
            if s != k:
                new[k][s] = dot32(inv, a[k][s])
        for r in blocks:
            if r != k:
                new[r][k] = -dot32(a[r][k], inv)
                for s in blocks:
                    if s != k:
                        new[r][s] = a[r][s] - dot32(a[r][k], new[k][s])
        a = new
    for r in blocks:
        for s in blocks:
            minv[r * BLOCK : (r + 1) * BLOCK, s * BLOCK : (s + 1) * BLOCK] = a[r][s]


def comm_kernel(
    rates_hbm, targets_hbm, goal_hbm, readout_hbm, corr_hbm, rec_hbm,
    scaled_out, readout_new, left_out,
    rates, rates_t, targets, goal, readout, rx, corr_v, rec_v,
    g_part, g_mid, g_relay, g_sum, g_x, g_z, g_piece, g_all, g_hi, g_lo, scaled,
    e_part, e_hold, e_mid, e_relay, e_sum, e_x, e_low, e_z, left,
    kpart, krow, ksum, kz, kmid, kx, cap, minv,
    load_sem, store_sem, send_sem, recv_sem,
):
    i = lax.axis_index("row")
    j = lax.axis_index("col")
    y, zl, c = i // 4, (i // 2) % 2, i % 2
    x, zh = j // 4, j % 4
    sems = Sems()

    def quarter(q):
        return aligned((q % 4) * QUARTER, QUARTER)

    def remote(src, dst, at, dev, land=None):
        return pltpu.make_async_remote_copy(
            src_ref=src, dst_ref=dst, send_sem=send_sem.at[at], recv_sem=recv_sem.at[at if land is None else land],
            device_id=dev, device_id_type=MESH,
        )

    def load(src, dst, at):
        copy = pltpu.make_async_copy(src, dst, load_sem.at[at])
        copy.start()
        return copy

    rates_load = load(rates_hbm, rates, 8)
    rec_loads, corr_loads = {}, {}

    def load_quarter(d, loads, src, dst, at):
        part = quarter(x + d)
        loads[d] = load(src.at[part], dst.at[part], at + d)

    load_quarter(2, corr_loads, corr_hbm, corr_v, 4)

    barrier = pltpu.get_barrier_semaphore()

    def greet(dev):
        pl.semaphore_signal(barrier, inc=1, device_id=dev, device_id_type=MESH)

    for d in range(1, 16):
        greet({"row": (i + d) % 16})

    for d in range(1, 4):
        greet({"col": x * 4 + (zh + d) % 4})
        greet({"col": ((x + d) % 4) * 4 + zh})

    for z in range(4):

        @pl.when((i != j) | (zh != z))
        def _():
            greet({"row": j, "col": y * 4 + z})

    for d in (1, 3, 0):
        load_quarter(d, corr_loads, corr_hbm, corr_v, 4)
    for d in (2, 1, 3, 0):
        load_quarter(d, rec_loads, rec_hbm, rec_v, 0)
    readout_load = load(readout_hbm, readout, 9)
    targets_load = load(targets_hbm, targets, 10)
    goal_load = load(goal_hbm, goal, 11)

    rates_load.wait()
    rates_t[...] = rates[...].T

    def z_dev(d):
        return {"col": x * 4 + (zh + d) % 4}

    def x_dev(d):
        return {"col": ((x + d) % 4) * 4 + zh}

    def y_dev(d):
        return {"row": ((y + d) % 4) * 4 + zl * 2 + c}

    class RingSum:
        def __init__(self, part, hold, relay, total, landed):
            self.part, self.hold, self.relay, self.total, self.landed = part, hold, relay, total, landed
            at = sems.take(6)
            top, low = pl.ds(0, 2), pl.ds(2, 2)
            self.copies = [
                remote(part.at[0, top], relay.at[0], at, x_dev(1)),
                remote(part.at[0, low], relay.at[1], at + 1, x_dev(3)),
                remote(part.at[1, low], landed.at[0], at + 2, x_dev(1), at + 2),
                remote(part.at[2, top], landed.at[1], at + 3, x_dev(3), at + 2),
                remote(total.at[0], landed.at[2], at + 4, x_dev(1), at + 2),
                remote(total.at[1], landed.at[3], at + 5, x_dev(3), at + 2),
            ]
            self.all = remote(landed, landed, at + 2, x_dev(1))

        def start(self, *which):
            for k in which:
                self.copies[k].start()

        def forward(self):
            for k in range(2):
                self.copies[k].wait_recv()
                self.total[k] = (self.hold(k) + self.relay[k].astype(F32)).astype(self.total.dtype)
                self.copies[4 + k].start()

        def finish(self, own):
            self.all.wait_recv()
            got = [self.landed[k].astype(F32) for k in range(4)]
            own[:2] = own[:2] + got[2] + got[1]
            own[2:] = own[2:] + got[0] + got[3]

        def wait_sends(self):
            for copy in self.copies:
                copy.wait_send()

    class Ring:
        def __init__(self, block, me, dev):
            self.block, self.me, self.dev = block, me, dev
            self.at = sems.take(6)

        def copy(self, k, owner):
            block = self.block((0, 1, 1, 0, 0, 1)[k], owner % 4)
            return remote(block, block, self.at + k, self.dev((1, 1, 3, 3, 1, 3)[k]))

        def start(self):
            for k in (0, 2, 1, 3):
                self.copy(k, self.me).start()

        def forward(self):
            self.copy(0, self.me + 3).wait_recv()
            self.copy(4, self.me + 3).start()
            self.copy(2, self.me + 1).wait_recv()
            self.copy(5, self.me + 1).start()

        def finish(self):
            self.copy(1, self.me + 3).wait_recv()
            self.copy(3, self.me + 1).wait_recv()
            self.copy(4, self.me + 2).wait_recv()
            self.copy(5, self.me + 2).wait_recv()

        def wait_sends(self):
            for k in range(4):
                self.copy(k, self.me).wait_send()
            self.copy(4, self.me + 3).wait_send()
            self.copy(5, self.me + 1).wait_send()

    def prod_quarter(d, out):
        corr_loads[d].wait()
        hi, lo = split2(corr_v[quarter(x + d), :])
        value = jnp.dot(hi, rates_t[...], preferred_element_type=F32) + jnp.dot(
            lo, rates_t[...], preferred_element_type=F32
        )
        for g, part in enumerate(groups(value)):
            out[g] = fold(part)

    def drive_quarter(d):
        rec_loads[d].wait()
        value = jnp.dot(rec_v[quarter(x + d), :], rates_t[...], preferred_element_type=F32)
        return [fold(part) for part in groups(value)]

    g_ring = RingSum(g_part, lambda k: g_part[1, :2] if k == 0 else g_part[2, 2:], g_relay, g_sum, g_x)
    prod_quarter(2, g_part.at[0])
    pl.semaphore_wait(barrier, jnp.where(i == j, 24, 25))
    g_ring.start(0, 1)
    prod_quarter(1, g_part.at[1])
    g_ring.start(2)
    prod_quarter(3, g_part.at[2])
    g_ring.start(3)

    r_t = sems.take(1)
    r_src = rates.at[:, quarter(y)]

    @pl.when(i != j)
    def _():
        remote(r_src, rx, r_t, {"row": j, "col": i}).start()

    @pl.when(i == j)
    def _():
        pltpu.make_async_copy(r_src, rx, recv_sem.at[r_t]).start()

    prod_quarter(0, g_mid)

    e_ring = RingSum(e_part, lambda k: e_hold[k], e_relay, e_sum, e_x)
    for g, part in enumerate(drive_quarter(2)):
        e_part[0, g] = part.astype(BF)
    g_ring.forward()
    e_ring.start(0, 1)
    for g, part in enumerate(drive_quarter(1)):
        if g < 2:
            e_hold[0, g] = part
        else:
            e_part[1, g] = part.astype(BF)
    e_ring.start(2)
    for g, part in enumerate(drive_quarter(3)):
        if g < 2:
            e_part[2, g] = part.astype(BF)
        else:
            e_hold[1, g - 2] = part
    e_ring.start(3)

    readout_load.wait()
    guess = sum(
        jnp.dot(term, rates_t[...], preferred_element_type=F32) for term in split2(readout[...] * (1.0 / 16.0))
    )
    kpart[3 * BLOCK : 3 * BLOCK + OUTS, :] = guess[:, :LANES]
    kpart[3 * BLOCK + OUTS :, :] = jnp.concatenate([guess[:, LANES:], guess[:, LANES:]], axis=1)

    g_ring.finish(g_mid)
    g_at = sems.take(3)

    def g_z_copy(d):
        return remote(g_mid.at[(zh + d) % 4], g_z.at[d - 1], g_at + d - 1, z_dev(d), g_at)

    for d in range(1, 4):
        g_z_copy(d).start()

    @pl.when(i != j)
    def _():
        remote(r_src, rx, r_t, {"row": j, "col": i}).wait_recv()

    @pl.when(i == j)
    def _():
        pltpu.make_async_copy(r_src, rx, recv_sem.at[r_t]).wait()

    whole = sum(
        jnp.dot(rx[...], term, preferred_element_type=F32)
        for term in split2(jnp.concatenate([unfold(g_mid[g]) for g in range(4)], axis=0))
    )
    kb = [[whole[r * BLOCK : (r + 1) * BLOCK, s * BLOCK : (s + 1) * BLOCK] for s in range(3)] for r in range(3)]
    kpart[:BLOCK, :] = jnp.concatenate([kb[0][0], kb[1][1]], axis=1)
    kpart[BLOCK : 2 * BLOCK, :] = jnp.concatenate([kb[2][2], kb[1][0]], axis=1)
    kpart[2 * BLOCK : 3 * BLOCK, :] = jnp.concatenate([kb[2][0], kb[2][1]], axis=1)

    k_r = sems.take(1)

    for d in range(1, 16):
        owner = (i + d) % 16

        @pl.when(owner < OWNERS)
        def _():
            remote(kpart.at[aligned(owner * PIECE, PIECE)], krow.at[d - 1], k_r, {"row": owner}).start()

    e_ring.forward()
    for g, part in enumerate(drive_quarter(0)):
        e_mid[g] = part

    remote(g_z, g_z, g_at, z_dev(1)).wait_recv()
    piece = g_mid[zh] + g_z[0] + g_z[1] + g_z[2]
    g_piece[...] = piece
    own = aligned(x * QUARTER + zh * GROUP, GROUP)
    left[own, STEPS:] = unfold(piece).astype(BF)
    s_t = sems.take(4)

    def swap_each(act_remote, act_local):
        for e in range(4):
            dst = g_all.at[x * 4 + zh]

            @pl.when((i != j) | (i % 4 != e))
            def _():
                act_remote(remote(g_piece, dst, s_t + e, {"row": x * 4 + e, "col": i}, s_t + zh))

            if act_local is not None:

                @pl.when((i == j) & (i % 4 == e))
                def _():
                    act_local(pltpu.make_async_copy(g_piece, dst, recv_sem.at[s_t + zh]))

    swap_each(lambda copy: copy.start(), lambda copy: copy.start())

    k_z = sems.take(3)
    k_x = sems.take(3)

    @pl.when(i < OWNERS)
    def _():
        remote(krow, krow, k_r, {"row": (i + 1) % 16}).wait_recv()
        acc = kpart[aligned(i * PIECE, PIECE), :]
        for d in range(15):
            acc = acc + krow[d]
        ksum[...] = acc
        for d in range(1, 4):
            remote(ksum, kz.at[d - 1], k_z + d - 1, z_dev(d), k_z).start()

    e_ring.finish(e_mid)
    e_low[...] = e_mid[...].astype(BF)
    e_at = sems.take(3)

    def e_z_copy(d):
        return remote(e_low.at[(zh + d) % 4], e_z.at[d - 1], e_at + d - 1, z_dev(d), e_at)

    for d in range(1, 4):
        e_z_copy(d).start()

    @pl.when(i < OWNERS)
    def _():
        remote(kz, kz, k_z, z_dev(1)).wait_recv()
        kmid[...] = ksum[...] + kz[0] + kz[1] + kz[2]
        for d in range(1, 4):
            remote(kmid, kx.at[d - 1], k_x + d - 1, x_dev(d), k_x).start()

    targets_load.wait()
    aims = targets[:, quarter(x)].T
    e_hold[0] = jnp.stack([fold(part) for part in groups(aims[:LANES].astype(F32))])
    e_hold[1] = jnp.stack([fold(part) for part in groups(aims[LANES:].astype(F32))])

    for z in range(4):
        dst = g_all.at[y * 4 + z]

        @pl.when((i != j) | (zh != z))
        def _():
            remote(g_piece, dst, s_t, {"row": j, "col": y * 4 + z}, s_t + z).wait_recv()

        @pl.when((i == j) & (zh == z))
        def _():
            pltpu.make_async_copy(g_piece, dst, recv_sem.at[s_t + z]).wait()

    y_ring = Ring(lambda half, owner: g_all.at[pl.ds(owner * 4 + half * 2, 2)], y, y_dev)
    y_ring.start()

    remote(e_z, e_z, e_at, z_dev(1)).wait_recv()
    total = e_mid[zh] - e_hold[zh // 2, zh % 2]
    for d in range(3):
        total = total + e_z[d].astype(F32)
    left[own, :STEPS] = unfold(total).astype(BF)
    l_z = sems.take(3)

    def l_z_copy(d, z):
        rows = left.at[aligned(x * QUARTER + (z % 4) * GROUP, GROUP)]
        return remote(rows, rows, l_z + d - 1, z_dev(d))

    for d in range(1, 4):
        l_z_copy(d, zh).start()

    k_g = sems.take(1)
    own_rows = aligned(i * PIECE, PIECE)

    @pl.when(i < OWNERS)
    def _():
        remote(kx, kx, k_x, x_dev(1)).wait_recv()
        cap[own_rows, :] = kmid[...] + kx[0] + kx[1] + kx[2]
        for d in range(1, 16):
            remote(cap.at[own_rows], cap.at[own_rows], k_g, {"row": (i + d) % 16}).start()

    y_ring.forward()

    for d in range(1, 4):
        l_z_copy(d, zh + 4 - d).wait_recv()
    l_ring = Ring(lambda half, owner: left.at[aligned(owner * QUARTER + half * LANES, LANES)], x, x_dev)
    l_ring.start()

    others = cap.at[pl.ds(0, PACKED - PIECE)]

    @pl.when(i < OWNERS)
    def _():
        remote(others, others, k_g, {"row": (i + 1) % 16}).wait_recv()

    @pl.when(i >= OWNERS)
    def _():
        remote(cap, cap, k_g, {"row": (i + 1) % 16}).wait_recv()

    def rest():
        pass

    def serve_y():
        y_ring.finish()

        @pl.loop(0, LOCAL // GROUP)
        def _(g):
            hi, lo = split2(unfold(g_all[g]))
            rows = aligned(g * GROUP, GROUP)
            g_hi[rows, :] = hi
            g_lo[rows, :] = lo

    invert(cap, minv, iter((rest, rest, l_ring.forward, rest, rest, rest, rest, serve_y)))

    m_hi, m_lo = split2(minv[...])
    value = sum(
        lax.dot_general(m, g, NT, preferred_element_type=F32)
        for m, g in ((m_hi, g_lo[...]), (m_lo, g_hi[...]), (m_hi, g_hi[...]))
    )
    scaled[...] = value.astype(BF)
    stores = [
        pltpu.make_async_copy(scaled, scaled_out, store_sem.at[0]),
        pltpu.make_async_copy(left, left_out, store_sem.at[1]),
        pltpu.make_async_copy(readout, readout_new, store_sem.at[2]),
    ]
    stores[0].start()
    l_ring.finish()
    stores[1].start()
    goal_load.wait()
    guess = jnp.concatenate([cap[3 * BLOCK : 3 * BLOCK + OUTS, :], cap[3 * BLOCK + OUTS :, : STEPS - LANES]], axis=1)
    readout[...] -= dot32(guess - goal[...], value)
    stores[2].start()

    @pl.when(i != j)
    def _():
        remote(r_src, rx, r_t, {"row": j, "col": i}).wait_send()

    swap_each(lambda copy: copy.wait_send(), None)
    for d in range(1, 4):
        g_z_copy(d).wait_send()
        e_z_copy(d).wait_send()
        l_z_copy(d, zh).wait_send()
    for ring in (g_ring, e_ring, y_ring, l_ring):
        ring.wait_sends()

    some = kpart.at[pl.ds(0, PACKED - PIECE)]

    @pl.when(i < OWNERS)
    def _():
        remote(some, some, k_r, {"row": (i + 1) % 16}).wait_send()
        for d in range(1, 4):
            remote(ksum, kz.at[d - 1], k_z + d - 1, z_dev(d)).wait_send()
            remote(kmid, kx.at[d - 1], k_x + d - 1, x_dev(d)).wait_send()
        remote(krow, krow, k_g, {"row": (i + 1) % 16}).wait_send()

    @pl.when(i >= OWNERS)
    def _():
        remote(kpart, kpart, k_r, {"row": (i + 1) % 16}).wait_send()

    for store in stores:
        store.wait()


N_SEMS = 96


def gather_all(rates, targets, goal, readout, corr, rec):
    hbm = pl.BlockSpec(memory_space=pl.ANY)

    def folded(dtype, *lead):
        return pltpu.VMEM((*lead, FOLDED, LANES), dtype)

    return pl.pallas_call(
        comm_kernel,
        out_shape=[
            jax.ShapeDtypeStruct((STEPS, LOCAL), BF),
            jax.ShapeDtypeStruct((OUTS, LOCAL), F32),
            jax.ShapeDtypeStruct((LOCAL, 2 * STEPS), BF),
        ],
        in_specs=[hbm] * 6,
        out_specs=[hbm] * 3,
        scratch_shapes=[
            pltpu.VMEM((STEPS, LOCAL), BF),
            pltpu.VMEM((LOCAL, STEPS), BF),
            pltpu.VMEM((STEPS, LOCAL), BF),
            pltpu.VMEM((OUTS, STEPS), F32),
            pltpu.VMEM((OUTS, LOCAL), F32),
            pltpu.VMEM((STEPS, QUARTER), BF),
            pltpu.VMEM((LOCAL, LOCAL), F32),
            pltpu.VMEM((LOCAL, LOCAL), BF),
            folded(F32, 3, 4),
            folded(F32, 4),
            folded(F32, 2, 2),
            folded(F32, 2, 2),
            folded(F32, 4, 2),
            folded(F32, 3),
            folded(F32),
            folded(F32, 16),
            pltpu.VMEM((LOCAL, STEPS), BF),
            pltpu.VMEM((LOCAL, STEPS), BF),
            pltpu.VMEM((STEPS, LOCAL), BF),
            folded(BF, 3, 4),
            folded(F32, 2, 2),
            folded(F32, 4),
            folded(BF, 2, 2),
            folded(BF, 2, 2),
            folded(BF, 4, 2),
            folded(BF, 4),
            folded(BF, 3),
            pltpu.VMEM((LOCAL, 2 * STEPS), BF),
            pltpu.VMEM((PACKED, LANES), F32),
            pltpu.VMEM((15, PIECE, LANES), F32),
            pltpu.VMEM((PIECE, LANES), F32),
            pltpu.VMEM((3, PIECE, LANES), F32),
            pltpu.VMEM((PIECE, LANES), F32),
            pltpu.VMEM((3, PIECE, LANES), F32),
            pltpu.VMEM((PACKED, LANES), F32),
            pltpu.VMEM((STEPS, STEPS), F32),
            pltpu.SemaphoreType.DMA((12,)),
            pltpu.SemaphoreType.DMA((3,)),
            pltpu.SemaphoreType.DMA((N_SEMS,)),
            pltpu.SemaphoreType.DMA((N_SEMS,)),
        ],
        compiler_params=pltpu.CompilerParams(
            collective_id=0, has_side_effects=True, vmem_limit_bytes=VMEM_LIMIT
        ),
        name="exchange",
    )(rates, targets, goal, readout, corr, rec)


def update_kernel(scaled, readout_new, left, corr, rec, corr_out, rec_out, readout_out):
    drop = jnp.dot(left[:, STEPS:], scaled[...], preferred_element_type=F32)
    corr_out[...] = corr[...] - drop
    drop = jnp.dot(left[:, :STEPS], scaled[...], preferred_element_type=F32)
    rec_out[...] = (rec[...].astype(F32) - drop).astype(BF)
    readout_out[...] = readout_new[...]


TILE = 256


def update(scaled, readout_new, left, corr, rec):
    def whole(shape):
        return pl.BlockSpec(shape, lambda g: (0, 0))

    rows = pl.BlockSpec((TILE, LOCAL), lambda g: (g, 0))
    factors = pl.BlockSpec((TILE, 2 * STEPS), lambda g: (g, 0))
    return pl.pallas_call(
        update_kernel,
        grid=(LOCAL // TILE,),
        out_shape=[
            jax.ShapeDtypeStruct((LOCAL, LOCAL), F32),
            jax.ShapeDtypeStruct((LOCAL, LOCAL), BF),
            jax.ShapeDtypeStruct((OUTS, LOCAL), F32),
        ],
        in_specs=[whole((STEPS, LOCAL)), whole((OUTS, LOCAL)), factors, rows, rows],
        out_specs=[rows, rows, whole((OUTS, LOCAL))],
        compiler_params=pltpu.CompilerParams(vmem_limit_bytes=VMEM_LIMIT),
        name="update",
    )(scaled, readout_new, left, corr, rec)


def on_device(rates, targets, goal, corr, rec, readout):
    scaled, readout_new, left = gather_all(rates, targets, goal, readout, corr, rec)
    return tuple(update(scaled, readout_new, left, corr, rec))


def solution(mesh):
    placed = (P(None, "col"), P(None, "row"), P(), P("row", "col"), P("row", "col"), P(None, "col"))
    return jax.shard_map(
        on_device,
        mesh=mesh,
        in_specs=placed,
        out_specs=(P("row", "col"), P("row", "col"), P(None, "col")),
        check_vma=False,
    )
```

```python
import functools

import jax
import jax.numpy as jnp
from jax import lax
from jax.experimental import pallas as pl
from jax.experimental.pallas import tpu as pltpu
from jax.sharding import PartitionSpec as P

MESH = pl.DeviceIdType.MESH
BF, F32 = jnp.bfloat16, jnp.float32
HIGH = lax.Precision.HIGHEST

STEPS = 192
LOCAL = 1024
OUTS = 16
QUARTER = 256
GROUP = 64
PIECE = 16
BLOCK = 64
PACKED = 3 * BLOCK + 2 * OUTS
OWNERS = PACKED // PIECE
LANES = 128
FOLDED = GROUP * STEPS // LANES
NT = (((1,), (1,)), ((), ()))
VMEM_LIMIT = 32 * 1024 * 1024


def split2(x):
    hi = x.astype(BF)
    return hi, (x - hi.astype(F32)).astype(BF)


def aligned(start, size):
    return pl.ds(pl.multiple_of(start, size), size)


def fold(v):
    low = jnp.concatenate([v[: GROUP // 2, LANES:], v[GROUP // 2 :, LANES:]], axis=1)
    return jnp.concatenate([v[:, :LANES], low], axis=0)


def unfold(v):
    rest = STEPS - LANES
    high = jnp.concatenate([v[GROUP:, :rest], v[GROUP:, rest:]], axis=0)
    return jnp.concatenate([v[:GROUP], high], axis=1)


def groups(v):
    return [v[g * GROUP : (g + 1) * GROUP] for g in range(v.shape[0] // GROUP)]


class Sems:
    def __init__(self):
        self.at = 0

    def take(self, count):
        first = self.at
        self.at += count
        return first


SUBS = 8
WIDE = 4


def reciprocal(v):
    return pl.reciprocal(v, approx=True)


def factor_two(a, b, d):
    ra = reciprocal(a)
    return b * ra, ra, a * reciprocal(a * d - b * b)


def factor_four(s):
    l = [[None] * WIDE for _ in range(WIDE)]
    l[1][0], rd0, rd1 = factor_two(s[0][0], s[1][0], s[1][1])
    c = {}
    for r in (2, 3):
        l[r][0] = s[r][0] * rd0
        c[r] = s[r][1] - l[1][0] * s[r][0]
        l[r][1] = c[r] * rd1

    def left(r, t):
        return s[r][t] - (l[r][0] * s[t][0] + l[r][1] * c[t])

    l[3][2], rd2, rd3 = factor_two(left(2, 2), left(3, 2), left(3, 3))
    return l, (rd0, rd1, rd2, rd3)


def eliminate(l, v):
    v1 = v[1] - l[1][0] * v[0]
    v2 = v[2] - l[2][0] * v[0] - l[2][1] * v1
    v3 = v[3] - l[3][0] * v[0] - l[3][1] * v1 - l[3][2] * v2
    return v[0], v1, v2, v3


def inverse_block(a, services):
    rows = [a[u * SUBS : (u + 1) * SUBS] for u in range(BLOCK // SUBS)]
    shape = (SUBS, BLOCK)
    lane = lax.broadcasted_iota(jnp.int32, shape, 1)
    sub = lax.broadcasted_iota(jnp.int32, shape, 0)
    for k in range(0, BLOCK, WIDE):
        v, first = k // SUBS, k % SUBS
        span = range(WIDE)
        col = [[jnp.broadcast_to(row[:, k + b : k + b + 1], shape) for row in rows] for b in span]
        s = [[jnp.broadcast_to(col[b][v][first + a : first + a + 1], shape) for b in range(a + 1)] for a in span]
        inside = (lane >= k) & (lane < k + WIDE)
        top = [
            jnp.where(inside, jnp.where(lane == k + b, 1.0, 0.0), jnp.broadcast_to(rows[v][first + b : first + b + 1], shape))
            for b in span
        ]
        l, rd = factor_four(s)
        top = eliminate(l, top)
        new = [None] * WIDE
        for a in reversed(span):
            new[a] = rd[a] * top[a]
            for b in range(a + 1, WIDE):
                new[a] = new[a] - l[b][a] * new[b]
        for u in range(len(rows)):
            m = eliminate(l, [col[b][u] for b in span])
            drop = ((m[0] * rd[0]) * top[0] + (m[1] * rd[1]) * top[1]) + ((m[2] * rd[2]) * top[2] + (m[3] * rd[3]) * top[3])
            rows[u] = jnp.where(inside, 0.0, rows[u]) - drop
        for a in span:
            rows[v] = jnp.where(sub == first + a, new[a], rows[v])
        if k % (4 * WIDE) == 3 * WIDE:
            for serve in services:
                serve()
                break
    return jnp.concatenate(rows, axis=0)


def dot32(a, b):
    return jnp.dot(a, b, precision=HIGH, preferred_element_type=F32)


def invert(cap, minv, services):
    blocks = range(STEPS // BLOCK)
    shape = (BLOCK, BLOCK)
    eye = jnp.where(lax.broadcasted_iota(jnp.int32, shape, 0) == lax.broadcasted_iota(jnp.int32, shape, 1), 1.0, 0.0)
    (k00, k11), (k22, k10), (k20, k21) = [
        [cap[r * BLOCK : (r + 1) * BLOCK, :BLOCK], cap[r * BLOCK : (r + 1) * BLOCK, BLOCK:]] for r in blocks
    ]
    a = [[k00 + eye, k10.T, k20.T], [k10, k11 + eye, k21.T], [k20, k21, k22 + eye]]
    for k in blocks:
        inv = inverse_block(a[k][k], services)
        new = [[None] * len(blocks) for _ in blocks]
        new[k][k] = inv
        for s in blocks:
            if s != k:
                new[k][s] = dot32(inv, a[k][s])
        for r in blocks:
            if r != k:
                new[r][k] = -dot32(a[r][k], inv)
                for s in blocks:
                    if s != k:
                        new[r][s] = a[r][s] - dot32(a[r][k], new[k][s])
        a = new
    for r in blocks:
        for s in blocks:
            minv[r * BLOCK : (r + 1) * BLOCK, s * BLOCK : (s + 1) * BLOCK] = a[r][s]


def comm_kernel(
    rates_hbm, targets_hbm, goal_hbm, readout_hbm, corr_hbm, rec_hbm,
    scaled, readout_new, left, corr_v, rec_v,
    rates, rates_t, targets, goal, readout, rx,
    g_part, g_mid, g_relay, g_sum, g_x, g_z, g_piece, g_all, g_hi, g_lo,
    e_part, e_hold, e_mid, e_relay, e_sum, e_x, e_low, e_z,
    kpart, krow, ksum, kz, kmid, kx, cap, minv,
    load_sem, send_sem, recv_sem,
):
    i = lax.axis_index("row")
    j = lax.axis_index("col")
    y, zl, c = i // 4, (i // 2) % 2, i % 2
    x, zh = j // 4, j % 4
    sems = Sems()

    def quarter(q):
        return aligned((q % 4) * QUARTER, QUARTER)

    def remote(src, dst, at, dev, land=None):
        return pltpu.make_async_remote_copy(
            src_ref=src, dst_ref=dst, send_sem=send_sem.at[at], recv_sem=recv_sem.at[at if land is None else land],
            device_id=dev, device_id_type=MESH,
        )

    def load(src, dst, at):
        copy = pltpu.make_async_copy(src, dst, load_sem.at[at])
        copy.start()
        return copy

    rates_load = load(rates_hbm, rates, 8)
    rec_loads, corr_loads = {}, {}

    def load_quarter(d, loads, src, dst, at):
        part = quarter(x + d)
        loads[d] = load(src.at[part], dst.at[part], at + d)

    load_quarter(2, corr_loads, corr_hbm, corr_v, 4)

    barrier = pltpu.get_barrier_semaphore()

    def greet(dev):
        pl.semaphore_signal(barrier, inc=1, device_id=dev, device_id_type=MESH)

    for d in range(1, 16):
        greet({"row": (i + d) % 16})

    for d in range(1, 4):
        greet({"col": x * 4 + (zh + d) % 4})
        greet({"col": ((x + d) % 4) * 4 + zh})

    @pl.when(i != j)
    def _():
        greet({"row": j, "col": i})

    for z in range(2):
        source = y * 4 + 2 * c + z

        @pl.when((i != j) | (source != j))
        def _():
            greet({"row": j, "col": source})

    for d in (1, 3, 0):
        load_quarter(d, corr_loads, corr_hbm, corr_v, 4)
    for d in (2, 1, 3, 0):
        load_quarter(d, rec_loads, rec_hbm, rec_v, 0)
    readout_load = load(readout_hbm, readout, 9)
    targets_load = load(targets_hbm, targets, 10)
    goal_load = load(goal_hbm, goal, 11)

    rates_load.wait()
    rates_t[...] = rates[...].T

    def z_dev(d):
        return {"col": x * 4 + (zh + d) % 4}

    def x_dev(d):
        return {"col": ((x + d) % 4) * 4 + zh}

    def y_dev(d):
        return {"row": ((y + d) % 4) * 4 + zl * 2 + c}

    class RingSum:
        def __init__(self, part, hold, relay, total, landed):
            self.part, self.hold, self.relay, self.total, self.landed = part, hold, relay, total, landed
            at = sems.take(6)
            top, low = pl.ds(0, 2), pl.ds(2, 2)
            self.copies = [
                remote(part.at[0, top], relay.at[0], at, x_dev(1)),
                remote(part.at[0, low], relay.at[1], at + 1, x_dev(3)),
                remote(part.at[1, low], landed.at[0], at + 2, x_dev(1), at + 2),
                remote(part.at[2, top], landed.at[1], at + 3, x_dev(3), at + 2),
                remote(total.at[0], landed.at[2], at + 4, x_dev(1), at + 2),
                remote(total.at[1], landed.at[3], at + 5, x_dev(3), at + 2),
            ]
            self.all = remote(landed, landed, at + 2, x_dev(1))

        def start(self, *which):
            for k in which:
                self.copies[k].start()

        def forward(self):
            for k in range(2):
                self.copies[k].wait_recv()
                self.total[k] = (self.hold(k) + self.relay[k].astype(F32)).astype(self.total.dtype)
                self.copies[4 + k].start()

        def finish(self, own):
            self.all.wait_recv()
            got = [self.landed[k].astype(F32) for k in range(4)]
            own[:2] = own[:2] + got[2] + got[1]
            own[2:] = own[2:] + got[0] + got[3]

        def wait_sends(self):
            for copy in self.copies:
                copy.wait_send()

    class Ring:
        def __init__(self, block, me, dev):
            self.block, self.me, self.dev = block, me, dev
            self.at = sems.take(6)

        def copy(self, k, owner):
            block = self.block((0, 1, 1, 0, 0, 1)[k], owner % 4)
            return remote(block, block, self.at + k, self.dev((1, 1, 3, 3, 1, 3)[k]))

        def start(self):
            for k in (0, 2, 1, 3):
                self.copy(k, self.me).start()

        def forward(self):
            self.copy(0, self.me + 3).wait_recv()
            self.copy(4, self.me + 3).start()
            self.copy(2, self.me + 1).wait_recv()
            self.copy(5, self.me + 1).start()

        def finish(self):
            self.copy(1, self.me + 3).wait_recv()
            self.copy(3, self.me + 1).wait_recv()
            self.copy(4, self.me + 2).wait_recv()
            self.copy(5, self.me + 2).wait_recv()

        def wait_sends(self):
            for k in range(4):
                self.copy(k, self.me).wait_send()
            self.copy(4, self.me + 3).wait_send()
            self.copy(5, self.me + 1).wait_send()

    def prod_quarter(d, out):
        corr_loads[d].wait()
        hi, lo = split2(corr_v[quarter(x + d), :])
        value = jnp.dot(hi, rates_t[...], preferred_element_type=F32) + jnp.dot(
            lo, rates_t[...], preferred_element_type=F32
        )
        for g, part in enumerate(groups(value)):
            out[g] = fold(part)

    def drive_quarter(d):
        rec_loads[d].wait()
        value = jnp.dot(rec_v[quarter(x + d), :], rates_t[...], preferred_element_type=F32)
        return [fold(part) for part in groups(value)]

    g_ring = RingSum(g_part, lambda k: g_part[1, :2] if k == 0 else g_part[2, 2:], g_relay, g_sum, g_x)
    prod_quarter(2, g_part.at[0])
    pl.semaphore_wait(barrier, jnp.where(i == j, jnp.where(zl == c, 22, 23), 24))
    g_ring.start(0, 1)
    prod_quarter(1, g_part.at[1])
    g_ring.start(2)
    prod_quarter(3, g_part.at[2])
    g_ring.start(3)

    r_t = sems.take(1)
    r_src = rates.at[:, quarter(y)]

    @pl.when(i != j)
    def _():
        remote(r_src, rx, r_t, {"row": j, "col": i}).start()

    @pl.when(i == j)
    def _():
        pltpu.make_async_copy(r_src, rx, recv_sem.at[r_t]).start()

    prod_quarter(0, g_mid)

    e_ring = RingSum(e_part, lambda k: e_hold[k], e_relay, e_sum, e_x)
    for g, part in enumerate(drive_quarter(2)):
        e_part[0, g] = part.astype(BF)
    g_ring.forward()
    e_ring.start(0, 1)
    for g, part in enumerate(drive_quarter(1)):
        if g < 2:
            e_hold[0, g] = part
        else:
            e_part[1, g] = part.astype(BF)
    e_ring.start(2)
    for g, part in enumerate(drive_quarter(3)):
        if g < 2:
            e_part[2, g] = part.astype(BF)
        else:
            e_hold[1, g - 2] = part
    e_ring.start(3)

    readout_load.wait()
    guess = sum(
        jnp.dot(term, rates_t[...], preferred_element_type=F32) for term in split2(readout[...] * (1.0 / 16.0))
    )
    kpart[3 * BLOCK : 3 * BLOCK + OUTS, :] = guess[:, :LANES]
    kpart[3 * BLOCK + OUTS :, :] = jnp.concatenate([guess[:, LANES:], guess[:, LANES:]], axis=1)

    g_ring.finish(g_mid)
    g_at = sems.take(3)

    def g_z_copy(d):
        return remote(g_mid.at[(zh + d) % 4], g_z.at[d - 1], g_at + d - 1, z_dev(d), g_at)

    for d in range(1, 4):
        g_z_copy(d).start()

    @pl.when(i != j)
    def _():
        remote(r_src, rx, r_t, {"row": j, "col": i}).wait_recv()

    @pl.when(i == j)
    def _():
        pltpu.make_async_copy(r_src, rx, recv_sem.at[r_t]).wait()

    whole = sum(
        jnp.dot(rx[...], term, preferred_element_type=F32)
        for term in split2(jnp.concatenate([unfold(g_mid[g]) for g in range(4)], axis=0))
    )
    kb = [[whole[r * BLOCK : (r + 1) * BLOCK, s * BLOCK : (s + 1) * BLOCK] for s in range(3)] for r in range(3)]
    kpart[:BLOCK, :] = jnp.concatenate([kb[0][0], kb[1][1]], axis=1)
    kpart[BLOCK : 2 * BLOCK, :] = jnp.concatenate([kb[2][2], kb[1][0]], axis=1)
    kpart[2 * BLOCK : 3 * BLOCK, :] = jnp.concatenate([kb[2][0], kb[2][1]], axis=1)

    k_r = sems.take(1)

    for d in range(1, 16):
        owner = (i + d) % 16

        @pl.when(owner < OWNERS)
        def _():
            remote(kpart.at[aligned(owner * PIECE, PIECE)], krow.at[d - 1], k_r, {"row": owner}).start()

    e_ring.forward()
    for g, part in enumerate(drive_quarter(0)):
        e_mid[g] = part

    remote(g_z, g_z, g_at, z_dev(1)).wait_recv()
    piece = g_mid[zh] + g_z[0] + g_z[1] + g_z[2]
    g_piece[...] = piece
    own = aligned(x * QUARTER + zh * GROUP, GROUP)
    left[own, STEPS:] = unfold(piece).astype(BF)
    s_t = sems.take(2)

    def swap_each(act_remote, act_local):
        for e in range(2):
            dst = g_all.at[x, zh]
            row = x * 4 + e * 2 + zh // 2

            @pl.when((i != j) | (row != i))
            def _():
                act_remote(remote(g_piece, dst, s_t + e, {"row": row, "col": i}, s_t + zh % 2))

            if act_local is not None:

                @pl.when((i == j) & (row == i))
                def _():
                    act_local(pltpu.make_async_copy(g_piece, dst, recv_sem.at[s_t + zh % 2]))

    swap_each(lambda copy: copy.start(), lambda copy: copy.start())

    k_z = sems.take(3)
    k_x = sems.take(3)

    @pl.when(i < OWNERS)
    def _():
        remote(krow, krow, k_r, {"row": (i + 1) % 16}).wait_recv()
        acc = kpart[aligned(i * PIECE, PIECE), :]
        for d in range(15):
            acc = acc + krow[d]
        ksum[...] = acc
        for d in range(1, 4):
            remote(ksum, kz.at[d - 1], k_z + d - 1, z_dev(d), k_z).start()

    e_ring.finish(e_mid)
    e_low[...] = e_mid[...].astype(BF)
    e_at = sems.take(3)

    def e_z_copy(d):
        return remote(e_low.at[(zh + d) % 4], e_z.at[d - 1], e_at + d - 1, z_dev(d), e_at)

    for d in range(1, 4):
        e_z_copy(d).start()

    @pl.when(i < OWNERS)
    def _():
        remote(kz, kz, k_z, z_dev(1)).wait_recv()
        kmid[...] = ksum[...] + kz[0] + kz[1] + kz[2]
        for d in range(1, 4):
            remote(kmid, kx.at[d - 1], k_x + d - 1, x_dev(d), k_x).start()

    targets_load.wait()
    aims = targets[:, quarter(x)].T
    e_hold[0] = jnp.stack([fold(part) for part in groups(aims[:LANES].astype(F32))])
    e_hold[1] = jnp.stack([fold(part) for part in groups(aims[LANES:].astype(F32))])

    for z in range(2):
        source = y * 4 + 2 * c + z
        dst = g_all.at[y, 2 * c + z]

        @pl.when((i != j) | (source != j))
        def _():
            remote(g_piece, dst, s_t, {"row": j, "col": source}, s_t + z).wait_recv()

        @pl.when((i == j) & (source == j))
        def _():
            pltpu.make_async_copy(g_piece, dst, recv_sem.at[s_t + z]).wait()

    y_ring = Ring(lambda half, owner: g_all.at[owner, 2 * c + half], y, y_dev)
    y_ring.start()

    remote(e_z, e_z, e_at, z_dev(1)).wait_recv()
    total = e_mid[zh] - e_hold[zh // 2, zh % 2]
    for d in range(3):
        total = total + e_z[d].astype(F32)
    left[own, :STEPS] = unfold(total).astype(BF)
    l_z = sems.take(3)

    def l_z_copy(d, z):
        rows = left.at[aligned(x * QUARTER + (z % 4) * GROUP, GROUP)]
        return remote(rows, rows, l_z + d - 1, z_dev(d))

    for d in range(1, 4):
        l_z_copy(d, zh).start()

    k_g = sems.take(1)
    own_rows = aligned(i * PIECE, PIECE)

    @pl.when(i < OWNERS)
    def _():
        remote(kx, kx, k_x, x_dev(1)).wait_recv()
        cap[own_rows, :] = kmid[...] + kx[0] + kx[1] + kx[2]
        for d in range(1, 16):
            remote(cap.at[own_rows], cap.at[own_rows], k_g, {"row": (i + d) % 16}).start()

    y_ring.forward()

    for d in range(1, 4):
        l_z_copy(d, zh + 4 - d).wait_recv()
    l_ring = Ring(lambda half, owner: left.at[aligned(owner * QUARTER + half * LANES, LANES)], x, x_dev)
    l_ring.start()

    others = cap.at[pl.ds(0, PACKED - PIECE)]

    @pl.when(i < OWNERS)
    def _():
        remote(others, others, k_g, {"row": (i + 1) % 16}).wait_recv()

    @pl.when(i >= OWNERS)
    def _():
        remote(cap, cap, k_g, {"row": (i + 1) % 16}).wait_recv()

    def rest():
        pass

    a_c = sems.take(1)
    sibling = {"row": i + 1 - 2 * c}
    mine = g_all.at[:, pl.ds(2 * c, 2)]
    theirs = g_all.at[:, pl.ds(2 - 2 * c, 2)]

    def serve_y():
        y_ring.finish()
        remote(mine, mine, a_c, sibling).start()

    def serve_core():
        remote(theirs, theirs, a_c, sibling).wait_recv()

        @pl.loop(0, 4)
        def _(q):
            for g in range(4):
                hi, lo = split2(unfold(g_all[q, g]))
                rows = aligned(q * QUARTER + g * GROUP, GROUP)
                g_hi[rows, :] = hi
                g_lo[rows, :] = lo

    invert(cap, minv, iter((rest, rest, l_ring.forward, rest, rest, serve_y, rest, rest, serve_core)))

    m_hi, m_lo = split2(minv[...])
    value = sum(
        lax.dot_general(m, g, NT, preferred_element_type=F32)
        for m, g in ((m_hi, g_lo[...]), (m_lo, g_hi[...]), (m_hi, g_hi[...]))
    )
    scaled[...] = value.astype(BF)
    goal_load.wait()
    guess = jnp.concatenate([cap[3 * BLOCK : 3 * BLOCK + OUTS, :], cap[3 * BLOCK + OUTS :, : STEPS - LANES]], axis=1)
    readout_new[...] = readout[...] - dot32(guess - goal[...], value)
    l_ring.finish()

    @pl.when(i != j)
    def _():
        remote(r_src, rx, r_t, {"row": j, "col": i}).wait_send()

    swap_each(lambda copy: copy.wait_send(), None)
    for d in range(1, 4):
        g_z_copy(d).wait_send()
        e_z_copy(d).wait_send()
        l_z_copy(d, zh).wait_send()
    for ring in (g_ring, e_ring, y_ring, l_ring):
        ring.wait_sends()

    some = kpart.at[pl.ds(0, PACKED - PIECE)]

    @pl.when(i < OWNERS)
    def _():
        remote(some, some, k_r, {"row": (i + 1) % 16}).wait_send()
        for d in range(1, 4):
            remote(ksum, kz.at[d - 1], k_z + d - 1, z_dev(d)).wait_send()
            remote(kmid, kx.at[d - 1], k_x + d - 1, x_dev(d)).wait_send()
        remote(krow, krow, k_g, {"row": (i + 1) % 16}).wait_send()

    @pl.when(i >= OWNERS)
    def _():
        remote(kpart, kpart, k_r, {"row": (i + 1) % 16}).wait_send()

    remote(mine, mine, a_c, sibling).wait_send()


N_SEMS = 96


def gather_all(rates, targets, goal, readout, corr, rec):
    hbm = pl.BlockSpec(memory_space=pl.ANY)

    def folded(dtype, *lead):
        return pltpu.VMEM((*lead, FOLDED, LANES), dtype)

    return pl.pallas_call(
        comm_kernel,
        out_shape=[
            jax.ShapeDtypeStruct((STEPS, LOCAL), BF),
            jax.ShapeDtypeStruct((OUTS, LOCAL), F32),
            jax.ShapeDtypeStruct((LOCAL, 2 * STEPS), BF),
            jax.ShapeDtypeStruct((LOCAL, LOCAL), F32),
            jax.ShapeDtypeStruct((LOCAL, LOCAL), BF),
        ],
        in_specs=[hbm] * 6,
        out_specs=[pl.BlockSpec(memory_space=pltpu.VMEM)] * 5,
        scratch_shapes=[
            pltpu.VMEM((STEPS, LOCAL), BF),
            pltpu.VMEM((LOCAL, STEPS), BF),
            pltpu.VMEM((STEPS, LOCAL), BF),
            pltpu.VMEM((OUTS, STEPS), F32),
            pltpu.VMEM((OUTS, LOCAL), F32),
            pltpu.VMEM((STEPS, QUARTER), BF),
            folded(F32, 3, 4),
            folded(F32, 4),
            folded(F32, 2, 2),
            folded(F32, 2, 2),
            folded(F32, 4, 2),
            folded(F32, 3),
            folded(F32),
            folded(F32, 4, 4),
            pltpu.VMEM((LOCAL, STEPS), BF),
            pltpu.VMEM((LOCAL, STEPS), BF),
            folded(BF, 3, 4),
            folded(F32, 2, 2),
            folded(F32, 4),
            folded(BF, 2, 2),
            folded(BF, 2, 2),
            folded(BF, 4, 2),
            folded(BF, 4),
            folded(BF, 3),
            pltpu.VMEM((PACKED, LANES), F32),
            pltpu.VMEM((15, PIECE, LANES), F32),
            pltpu.VMEM((PIECE, LANES), F32),
            pltpu.VMEM((3, PIECE, LANES), F32),
            pltpu.VMEM((PIECE, LANES), F32),
            pltpu.VMEM((3, PIECE, LANES), F32),
            pltpu.VMEM((PACKED, LANES), F32),
            pltpu.VMEM((STEPS, STEPS), F32),
            pltpu.SemaphoreType.DMA((12,)),
            pltpu.SemaphoreType.DMA((N_SEMS,)),
            pltpu.SemaphoreType.DMA((N_SEMS,)),
        ],
        compiler_params=pltpu.CompilerParams(
            collective_id=0, has_side_effects=True, vmem_limit_bytes=VMEM_LIMIT
        ),
        name="exchange",
    )(rates, targets, goal, readout, corr, rec)


TILE = 256


def update_kernel(scaled, readout_new, left, corr, rec, corr_out, rec_out, readout_out):
    rows = aligned(pl.program_id(0) * TILE, TILE)
    drop = jnp.dot(left[rows, STEPS:], scaled[...], preferred_element_type=F32)
    corr_out[...] = corr[rows, :] - drop
    drop = jnp.dot(left[rows, :STEPS], scaled[...], preferred_element_type=F32)
    rec_out[...] = (rec[rows, :].astype(F32) - drop).astype(BF)
    readout_out[...] = readout_new[...]


def update(scaled, readout_new, left, corr, rec):
    rows = pl.BlockSpec((TILE, LOCAL), lambda g: (g, 0))
    return pl.pallas_call(
        update_kernel,
        grid=(LOCAL // TILE,),
        out_shape=[
            jax.ShapeDtypeStruct((LOCAL, LOCAL), F32),
            jax.ShapeDtypeStruct((LOCAL, LOCAL), BF),
            jax.ShapeDtypeStruct((OUTS, LOCAL), F32),
        ],
        in_specs=[pl.BlockSpec(memory_space=pltpu.VMEM)] * 5,
        out_specs=[rows, rows, pl.BlockSpec((OUTS, LOCAL), lambda g: (0, 0))],
        compiler_params=pltpu.CompilerParams(vmem_limit_bytes=VMEM_LIMIT),
        name="update",
    )(scaled, readout_new, left, corr, rec)


def on_device(*args):
    rates, targets, goal, corr, rec, readout = (pltpu.with_memory_space_constraint(v, pltpu.HBM) for v in args)
    return tuple(update(*gather_all(rates, targets, goal, readout, corr, rec)))


def solution(mesh):
    placed = (P(None, "col"), P(None, "row"), P(), P("row", "col"), P("row", "col"), P(None, "col"))
    return jax.shard_map(
        on_device,
        mesh=mesh,
        in_specs=placed,
        out_specs=(P("row", "col"), P("row", "col"), P(None, "col")),
        check_vma=False,
    )
```

```python
import functools

import jax
import jax.numpy as jnp
from jax import lax
from jax.experimental import pallas as pl
from jax.experimental.pallas import tpu as pltpu
from jax.sharding import PartitionSpec as P

MESH = pl.DeviceIdType.MESH
BF, F32 = jnp.bfloat16, jnp.float32
HIGH = lax.Precision.HIGHEST

STEPS = 192
LOCAL = 1024
OUTS = 16
QUARTER = 256
GROUP = 64
PIECE = 16
BLOCK = 64
PACKED = 3 * BLOCK + 2 * OUTS
OWNERS = PACKED // PIECE
LANES = 128
FOLDED = GROUP * STEPS // LANES
NT = (((1,), (1,)), ((), ()))
VMEM_LIMIT = 32 * 1024 * 1024


def split2(x):
    hi = x.astype(BF)
    return hi, (x - hi.astype(F32)).astype(BF)


def aligned(start, size):
    return pl.ds(pl.multiple_of(start, size), size)


def fold(v):
    low = jnp.concatenate([v[: GROUP // 2, LANES:], v[GROUP // 2 :, LANES:]], axis=1)
    return jnp.concatenate([v[:, :LANES], low], axis=0)


def unfold(v):
    rest = STEPS - LANES
    high = jnp.concatenate([v[GROUP:, :rest], v[GROUP:, rest:]], axis=0)
    return jnp.concatenate([v[:GROUP], high], axis=1)


def groups(v):
    return [v[g * GROUP : (g + 1) * GROUP] for g in range(v.shape[0] // GROUP)]


class Sems:
    def __init__(self):
        self.at = 0

    def take(self, count):
        first = self.at
        self.at += count
        return first


SUBS = 8
WIDE = 4


def reciprocal(v):
    return pl.reciprocal(v, approx=True)


def factor_two(a, b, d):
    ra = reciprocal(a)
    return b * ra, ra, a * reciprocal(a * d - b * b)


def factor_four(s):
    l = [[None] * WIDE for _ in range(WIDE)]
    l[1][0], rd0, rd1 = factor_two(s[0][0], s[1][0], s[1][1])
    c = {}
    for r in (2, 3):
        l[r][0] = s[r][0] * rd0
        c[r] = s[r][1] - l[1][0] * s[r][0]
        l[r][1] = c[r] * rd1

    def left(r, t):
        return s[r][t] - (l[r][0] * s[t][0] + l[r][1] * c[t])

    l[3][2], rd2, rd3 = factor_two(left(2, 2), left(3, 2), left(3, 3))
    return l, (rd0, rd1, rd2, rd3)


def eliminate(l, v):
    v1 = v[1] - l[1][0] * v[0]
    v2 = v[2] - l[2][0] * v[0] - l[2][1] * v1
    v3 = v[3] - l[3][0] * v[0] - l[3][1] * v1 - l[3][2] * v2
    return v[0], v1, v2, v3


def inverse_block(a, services):
    rows = [a[u * SUBS : (u + 1) * SUBS] for u in range(BLOCK // SUBS)]
    shape = (SUBS, BLOCK)
    lane = lax.broadcasted_iota(jnp.int32, shape, 1)
    sub = lax.broadcasted_iota(jnp.int32, shape, 0)
    span = range(WIDE)

    def column(row, k):
        return jnp.broadcast_to(row[:, k : k + 1], shape)

    def entry(col, r):
        return jnp.broadcast_to(col[r % SUBS : r % SUBS + 1], shape)

    s = None
    for k in range(0, BLOCK, WIDE):
        v, first = k // SUBS, k % SUBS
        col = [[column(row, k + b) for row in rows] for b in span]
        if s is None:
            s = [[entry(col[b][v], k + a) for b in range(a + 1)] for a in span]
        after = k + WIDE
        if after < BLOCK:
            row = rows[after // SUBS]
            ahead = [column(row, after + b) for b in span]
            ahead = [[entry(ahead[b], after + a) for b in range(a + 1)] for a in span]
            links = [[entry(col[b][after // SUBS], after + a) for b in span] for a in span]
        inside = (lane >= k) & (lane < k + WIDE)
        top = [
            jnp.where(inside, jnp.where(lane == k + b, 1.0, 0.0), entry(rows[v], first + b))
            for b in span
        ]
        l, rd = factor_four(s)
        if after < BLOCK:
            links = [eliminate(l, link) for link in links]
            scaled = [[link[b] * rd[b] for b in span] for link in links]
            s = [
                [
                    ahead[a][b]
                    - (
                        (scaled[a][0] * links[b][0] + scaled[a][1] * links[b][1])
                        + (scaled[a][2] * links[b][2] + scaled[a][3] * links[b][3])
                    )
                    for b in range(a + 1)
                ]
                for a in span
            ]
        top = eliminate(l, top)
        new = [None] * WIDE
        for a in reversed(span):
            new[a] = rd[a] * top[a]
            for b in range(a + 1, WIDE):
                new[a] = new[a] - l[b][a] * new[b]
        for u in range(len(rows)):
            m = eliminate(l, [col[b][u] for b in span])
            drop = ((m[0] * rd[0]) * top[0] + (m[1] * rd[1]) * top[1]) + ((m[2] * rd[2]) * top[2] + (m[3] * rd[3]) * top[3])
            rows[u] = jnp.where(inside, 0.0, rows[u]) - drop
        for a in span:
            rows[v] = jnp.where(sub == first + a, new[a], rows[v])
        if k % (4 * WIDE) == 3 * WIDE:
            for serve in services:
                serve()
                break
    return jnp.concatenate(rows, axis=0)


def dot32(a, b):
    return jnp.dot(a, b, precision=HIGH, preferred_element_type=F32)


def invert(cap, minv, services):
    blocks = range(STEPS // BLOCK)
    shape = (BLOCK, BLOCK)
    eye = jnp.where(lax.broadcasted_iota(jnp.int32, shape, 0) == lax.broadcasted_iota(jnp.int32, shape, 1), 1.0, 0.0)
    (k00, k11), (k22, k10), (k20, k21) = [
        [cap[r * BLOCK : (r + 1) * BLOCK, :BLOCK], cap[r * BLOCK : (r + 1) * BLOCK, BLOCK:]] for r in blocks
    ]
    a = [[k00 + eye, k10.T, k20.T], [k10, k11 + eye, k21.T], [k20, k21, k22 + eye]]
    for k in blocks:
        inv = inverse_block(a[k][k], services)
        new = [[None] * len(blocks) for _ in blocks]
        new[k][k] = inv
        for s in blocks:
            if s != k:
                new[k][s] = dot32(inv, a[k][s])
        for r in blocks:
            if r != k:
                new[r][k] = -dot32(a[r][k], inv)
                for s in blocks:
                    if s != k:
                        new[r][s] = a[r][s] - dot32(a[r][k], new[k][s])
        a = new
    for r in blocks:
        for s in blocks:
            minv[r * BLOCK : (r + 1) * BLOCK, s * BLOCK : (s + 1) * BLOCK] = a[r][s]


def comm_kernel(
    rates_hbm, targets_hbm, goal_hbm, readout_hbm, corr_hbm, rec_hbm,
    scaled, readout_new, left, corr_v, rec_v,
    rates, rates_t, targets, goal, readout, rx,
    g_part, g_mid, g_relay, g_sum, g_x, g_zrelay, g_zsum, g_z, g_piece, g_all, g_hi, g_lo,
    e_part, e_hold, e_mid, e_relay, e_sum, e_x, e_low, e_z,
    kpart, krow, ksum, kz, kmid, kx, cap, minv,
    load_sem, send_sem, recv_sem,
):
    i = lax.axis_index("row")
    j = lax.axis_index("col")
    y, zl, c = i // 4, (i // 2) % 2, i % 2
    x, zh = j // 4, j % 4
    sems = Sems()

    def quarter(q):
        return aligned((q % 4) * QUARTER, QUARTER)

    def remote(src, dst, at, dev, land=None):
        return pltpu.make_async_remote_copy(
            src_ref=src, dst_ref=dst, send_sem=send_sem.at[at], recv_sem=recv_sem.at[at if land is None else land],
            device_id=dev, device_id_type=MESH,
        )

    def load(src, dst, at):
        copy = pltpu.make_async_copy(src, dst, load_sem.at[at])
        copy.start()
        return copy

    rates_load = load(rates_hbm, rates, 8)
    rec_loads, corr_loads = {}, {}

    def load_quarter(d, loads, src, dst, at):
        part = quarter(x + d)
        loads[d] = load(src.at[part], dst.at[part], at + d)

    load_quarter(2, corr_loads, corr_hbm, corr_v, 4)

    barrier = pltpu.get_barrier_semaphore()

    def greet(dev):
        pl.semaphore_signal(barrier, inc=1, device_id=dev, device_id_type=MESH)

    for d in range(1, 16):
        greet({"row": (i + d) % 16})

    for d in range(1, 4):
        greet({"col": x * 4 + (zh + d) % 4})
        greet({"col": ((x + d) % 4) * 4 + zh})

    @pl.when(i != j)
    def _():
        greet({"row": j, "col": i})

    for z in range(2):
        source = y * 4 + 2 * c + z

        @pl.when((i != j) | (source != j))
        def _():
            greet({"row": j, "col": source})

    for d in (1, 3, 0):
        load_quarter(d, corr_loads, corr_hbm, corr_v, 4)
    for d in (2, 1, 3, 0):
        load_quarter(d, rec_loads, rec_hbm, rec_v, 0)
    readout_load = load(readout_hbm, readout, 9)
    targets_load = load(targets_hbm, targets, 10)
    goal_load = load(goal_hbm, goal, 11)

    rates_load.wait()
    rates_t[...] = rates[...].T

    def z_dev(d):
        return {"col": x * 4 + (zh + d) % 4}

    def x_dev(d):
        return {"col": ((x + d) % 4) * 4 + zh}

    def y_dev(d):
        return {"row": ((y + d) % 4) * 4 + zl * 2 + c}

    class RingSum:
        def __init__(self, part, hold, relay, total, landed, dev):
            self.hold, self.relay, self.total, self.landed = hold, relay, total, landed
            at = sems.take(6)
            self.copies = [
                remote(part(0, 0), relay.at[0], at, dev(1)),
                remote(part(0, 1), relay.at[1], at + 1, dev(3)),
                remote(part(1, 1), landed.at[0], at + 2, dev(1), at + 2),
                remote(part(2, 0), landed.at[1], at + 3, dev(3), at + 2),
                remote(total.at[0], landed.at[2], at + 4, dev(1), at + 2),
                remote(total.at[1], landed.at[3], at + 5, dev(3), at + 2),
            ]
            self.all = remote(landed, landed, at + 2, dev(1))

        def start(self, *which):
            for k in which:
                self.copies[k].start()

        def forward(self):
            for k in range(2):
                self.copies[k].wait_recv()
                self.total[k] = (self.hold(k) + self.relay[k].astype(F32)).astype(self.total.dtype)
                self.copies[4 + k].start()

        def finish(self):
            self.all.wait_recv()
            got = [self.landed[k].astype(F32) for k in range(4)]
            return got[2] + got[1], got[0] + got[3]

        def wait_sends(self):
            for copy in self.copies:
                copy.wait_send()

    class Ring:
        def __init__(self, block, me, dev):
            self.block, self.me, self.dev = block, me, dev
            self.at = sems.take(6)

        def copy(self, k, owner):
            block = self.block((0, 1, 1, 0, 0, 1)[k], owner % 4)
            return remote(block, block, self.at + k, self.dev((1, 1, 3, 3, 1, 3)[k]))

        def start(self):
            for k in (0, 2, 1, 3):
                self.copy(k, self.me).start()

        def forward(self):
            self.copy(0, self.me + 3).wait_recv()
            self.copy(4, self.me + 3).start()
            self.copy(2, self.me + 1).wait_recv()
            self.copy(5, self.me + 1).start()

        def finish(self):
            self.copy(1, self.me + 3).wait_recv()
            self.copy(3, self.me + 1).wait_recv()
            self.copy(4, self.me + 2).wait_recv()
            self.copy(5, self.me + 2).wait_recv()

        def wait_sends(self):
            for k in range(4):
                self.copy(k, self.me).wait_send()
            self.copy(4, self.me + 3).wait_send()
            self.copy(5, self.me + 1).wait_send()

    def prod_quarter(d, out):
        corr_loads[d].wait()
        hi, lo = split2(corr_v[quarter(x + d), :])
        value = jnp.dot(hi, rates_t[...], preferred_element_type=F32) + jnp.dot(
            lo, rates_t[...], preferred_element_type=F32
        )
        for g, part in enumerate(groups(value)):
            out[g] = fold(part)

    def drive_quarter(d):
        rec_loads[d].wait()
        value = jnp.dot(rec_v[quarter(x + d), :], rates_t[...], preferred_element_type=F32)
        return [fold(part) for part in groups(value)]

    pl.semaphore_wait(barrier, jnp.where(i == j, jnp.where(zl == c, 22, 23), 24))
    r_t = sems.take(1)
    r_src = rates.at[:, quarter(y)]

    @pl.when(i != j)
    def _():
        remote(r_src, rx, r_t, {"row": j, "col": i}).start()

    @pl.when(i == j)
    def _():
        pltpu.make_async_copy(r_src, rx, recv_sem.at[r_t]).start()

    def pairs(part):
        return lambda which, half: part.at[which, pl.ds(2 * half, 2)]

    g_ring = RingSum(
        pairs(g_part), lambda k: g_part[1, :2] if k == 0 else g_part[2, 2:], g_relay, g_sum, g_x, x_dev
    )
    prod_quarter(2, g_part.at[0])
    g_ring.start(0, 1)
    prod_quarter(1, g_part.at[1])
    g_ring.start(2)
    prod_quarter(3, g_part.at[2])
    g_ring.start(3)
    prod_quarter(0, g_mid)

    e_ring = RingSum(pairs(e_part), lambda k: e_hold[k], e_relay, e_sum, e_x, x_dev)
    for g, part in enumerate(drive_quarter(2)):
        e_part[0, g] = part.astype(BF)
    g_ring.forward()
    e_ring.start(0, 1)
    for g, part in enumerate(drive_quarter(1)):
        if g < 2:
            e_hold[0, g] = part
        else:
            e_part[1, g] = part.astype(BF)
    e_ring.start(2)
    for g, part in enumerate(drive_quarter(3)):
        if g < 2:
            e_part[2, g] = part.astype(BF)
        else:
            e_hold[1, g - 2] = part
    e_ring.start(3)

    readout_load.wait()
    guess = sum(
        jnp.dot(term, rates_t[...], preferred_element_type=F32) for term in split2(readout[...] * (1.0 / 16.0))
    )
    kpart[3 * BLOCK : 3 * BLOCK + OUTS, :] = guess[:, :LANES]
    kpart[3 * BLOCK + OUTS :, :] = jnp.concatenate([guess[:, LANES:], guess[:, LANES:]], axis=1)

    @pl.when(i != j)
    def _():
        remote(r_src, rx, r_t, {"row": j, "col": i}).wait_recv()

    @pl.when(i == j)
    def _():
        pltpu.make_async_copy(r_src, rx, recv_sem.at[r_t]).wait()

    got = g_ring.finish()
    for k in range(2):
        g_mid[2 * k : 2 * k + 2] = g_mid[2 * k : 2 * k + 2] + got[k]
    whole = sum(
        jnp.dot(rx[...], term, preferred_element_type=F32)
        for term in split2(jnp.concatenate([unfold(g_mid[g]) for g in range(4)], axis=0))
    )
    kb = [[whole[r * BLOCK : (r + 1) * BLOCK, s * BLOCK : (s + 1) * BLOCK] for s in range(3)] for r in range(3)]
    kpart[:BLOCK, :] = jnp.concatenate([kb[0][0], kb[1][1]], axis=1)
    kpart[BLOCK : 2 * BLOCK, :] = jnp.concatenate([kb[2][2], kb[1][0]], axis=1)
    kpart[2 * BLOCK : 3 * BLOCK, :] = jnp.concatenate([kb[2][0], kb[2][1]], axis=1)

    k_r = sems.take(1)

    for d in range(1, 16):
        owner = (i + d) % 16

        @pl.when(owner < OWNERS)
        def _():
            remote(kpart.at[aligned(owner * PIECE, PIECE)], krow.at[d - 1], k_r, {"row": owner}).start()

    def g_slice(which, half):
        return g_mid.at[(zh + (2, 1, 3)[which]) % 4, pl.ds(half * (FOLDED // 2), FOLDED // 2)]

    z_ring = RingSum(g_slice, lambda k: g_slice(k + 1, k)[...], g_zrelay, g_zsum, g_z, z_dev)
    z_ring.start(0, 1, 2, 3)

    e_ring.forward()
    for g, part in enumerate(drive_quarter(0)):
        e_mid[g] = part

    k_x = sems.take(3)
    k_z = sems.take(3)

    @pl.when(i < OWNERS)
    def _():
        remote(krow, krow, k_r, {"row": (i + 1) % 16}).wait_recv()
        acc = kpart[aligned(i * PIECE, PIECE), :]
        for d in range(15):
            acc = acc + krow[d]
        ksum[...] = acc
        for d in range(1, 4):
            remote(ksum, kx.at[d - 1], k_x + d - 1, x_dev(d), k_x).start()

    z_ring.forward()

    got = e_ring.finish()
    for k in range(2):
        total = e_mid[2 * k : 2 * k + 2] + got[k]
        e_mid[2 * k : 2 * k + 2] = total
        e_low[2 * k : 2 * k + 2] = total.astype(BF)
    e_at = sems.take(3)

    def e_z_copy(d):
        return remote(e_low.at[(zh + d) % 4], e_z.at[d - 1], e_at + d - 1, z_dev(d), e_at)

    for d in range(1, 4):
        e_z_copy(d).start()

    @pl.when(i < OWNERS)
    def _():
        remote(kx, kx, k_x, x_dev(1)).wait_recv()
        kmid[...] = ksum[...] + kx[0] + kx[1] + kx[2]
        for d in range(1, 4):
            remote(kmid, kz.at[d - 1], k_z + d - 1, z_dev(d), k_z).start()

    targets_load.wait()
    aims = targets[:, quarter(x)].T
    e_hold[0] = jnp.stack([fold(part) for part in groups(aims[:LANES].astype(F32))])
    e_hold[1] = jnp.stack([fold(part) for part in groups(aims[LANES:].astype(F32))])

    got = z_ring.finish()
    for k in range(2):
        part = pl.ds(k * (FOLDED // 2), FOLDED // 2)
        g_piece[part, :] = g_mid[zh, part, :] + got[k]
    own = aligned(x * QUARTER + zh * GROUP, GROUP)
    s_t = sems.take(2)

    def swap_each(act_remote, act_local):
        for e in range(2):
            dst = g_all.at[x, zh]
            row = x * 4 + e * 2 + zh // 2

            @pl.when((i != j) | (row != i))
            def _():
                act_remote(remote(g_piece, dst, s_t + e, {"row": row, "col": i}, s_t + zh % 2))

            if act_local is not None:

                @pl.when((i == j) & (row == i))
                def _():
                    act_local(pltpu.make_async_copy(g_piece, dst, recv_sem.at[s_t + zh % 2]))

    swap_each(lambda copy: copy.start(), lambda copy: copy.start())
    left[own, STEPS:] = unfold(g_piece[...]).astype(BF)

    remote(e_z, e_z, e_at, z_dev(1)).wait_recv()
    total = e_mid[zh] - e_hold[zh // 2, zh % 2]
    for d in range(3):
        total = total + e_z[d].astype(F32)
    left[own, :STEPS] = unfold(total).astype(BF)
    lz_ring = Ring(
        lambda half, owner: left.at[aligned(x * QUARTER + owner * GROUP + half * (GROUP // 2), GROUP // 2)], zh, z_dev
    )
    lz_ring.start()

    k_g = sems.take(1)
    own_rows = aligned(i * PIECE, PIECE)

    @pl.when(i < OWNERS)
    def _():
        remote(kz, kz, k_z, z_dev(1)).wait_recv()
        cap[own_rows, :] = kmid[...] + kz[0] + kz[1] + kz[2]
        for d in range(1, 16):
            remote(cap.at[own_rows], cap.at[own_rows], k_g, {"row": (i + d) % 16}).start()

    for z in range(2):
        source = y * 4 + 2 * c + z
        dst = g_all.at[y, 2 * c + z]

        @pl.when((i != j) | (source != j))
        def _():
            remote(g_piece, dst, s_t, {"row": j, "col": source}, s_t + z).wait_recv()

        @pl.when((i == j) & (source == j))
        def _():
            pltpu.make_async_copy(g_piece, dst, recv_sem.at[s_t + z]).wait()

    y_ring = Ring(lambda half, owner: g_all.at[owner, 2 * c + half], y, y_dev)
    y_ring.start()
    lz_ring.forward()
    l_ring = Ring(lambda half, owner: left.at[aligned(owner * QUARTER + half * LANES, LANES)], x, x_dev)

    others = cap.at[pl.ds(0, PACKED - PIECE)]

    @pl.when(i < OWNERS)
    def _():
        remote(others, others, k_g, {"row": (i + 1) % 16}).wait_recv()

    @pl.when(i >= OWNERS)
    def _():
        remote(cap, cap, k_g, {"row": (i + 1) % 16}).wait_recv()

    def rest():
        pass

    a_c = sems.take(1)
    sibling = {"row": i + 1 - 2 * c}
    mine = g_all.at[:, pl.ds(2 * c, 2)]
    theirs = g_all.at[:, pl.ds(2 - 2 * c, 2)]

    def serve_left():
        lz_ring.finish()
        l_ring.start()

    def serve_y():
        y_ring.finish()
        remote(mine, mine, a_c, sibling).start()

    def serve_core():
        remote(theirs, theirs, a_c, sibling).wait_recv()

        @pl.loop(0, 4)
        def _(q):
            for g in range(4):
                hi, lo = split2(unfold(g_all[q, g]))
                rows = aligned(q * QUARTER + g * GROUP, GROUP)
                g_hi[rows, :] = hi
                g_lo[rows, :] = lo

    invert(cap, minv, iter((serve_left, y_ring.forward, rest, rest, l_ring.forward, rest, serve_y, rest, rest, serve_core)))

    m_hi, m_lo = split2(minv[...])
    value = sum(
        lax.dot_general(m, g, NT, preferred_element_type=F32)
        for m, g in ((m_hi, g_lo[...]), (m_lo, g_hi[...]), (m_hi, g_hi[...]))
    )
    scaled[...] = value.astype(BF)
    goal_load.wait()
    guess = jnp.concatenate([cap[3 * BLOCK : 3 * BLOCK + OUTS, :], cap[3 * BLOCK + OUTS :, : STEPS - LANES]], axis=1)
    readout_new[...] = readout[...] - dot32(guess - goal[...], value)
    l_ring.finish()

    @pl.when(i != j)
    def _():
        remote(r_src, rx, r_t, {"row": j, "col": i}).wait_send()

    swap_each(lambda copy: copy.wait_send(), None)
    for d in range(1, 4):
        e_z_copy(d).wait_send()
    for ring in (g_ring, e_ring, z_ring, lz_ring, y_ring, l_ring):
        ring.wait_sends()

    some = kpart.at[pl.ds(0, PACKED - PIECE)]

    @pl.when(i < OWNERS)
    def _():
        remote(some, some, k_r, {"row": (i + 1) % 16}).wait_send()
        for d in range(1, 4):
            remote(ksum, kz.at[d - 1], k_z + d - 1, z_dev(d)).wait_send()
            remote(kmid, kx.at[d - 1], k_x + d - 1, x_dev(d)).wait_send()
        remote(krow, krow, k_g, {"row": (i + 1) % 16}).wait_send()

    @pl.when(i >= OWNERS)
    def _():
        remote(kpart, kpart, k_r, {"row": (i + 1) % 16}).wait_send()

    remote(mine, mine, a_c, sibling).wait_send()


N_SEMS = 96


def gather_all(rates, targets, goal, readout, corr, rec):
    hbm = pl.BlockSpec(memory_space=pl.ANY)

    def folded(dtype, *lead):
        return pltpu.VMEM((*lead, FOLDED, LANES), dtype)

    return pl.pallas_call(
        comm_kernel,
        out_shape=[
            jax.ShapeDtypeStruct((STEPS, LOCAL), BF),
            jax.ShapeDtypeStruct((OUTS, LOCAL), F32),
            jax.ShapeDtypeStruct((LOCAL, 2 * STEPS), BF),
            jax.ShapeDtypeStruct((LOCAL, LOCAL), F32),
            jax.ShapeDtypeStruct((LOCAL, LOCAL), BF),
        ],
        in_specs=[hbm] * 6,
        out_specs=[pl.BlockSpec(memory_space=pltpu.VMEM)] * 5,
        scratch_shapes=[
            pltpu.VMEM((STEPS, LOCAL), BF),
            pltpu.VMEM((LOCAL, STEPS), BF),
            pltpu.VMEM((STEPS, LOCAL), BF),
            pltpu.VMEM((OUTS, STEPS), F32),
            pltpu.VMEM((OUTS, LOCAL), F32),
            pltpu.VMEM((STEPS, QUARTER), BF),
            folded(F32, 3, 4),
            folded(F32, 4),
            folded(F32, 2, 2),
            folded(F32, 2, 2),
            folded(F32, 4, 2),
            pltpu.VMEM((2, FOLDED // 2, LANES), F32),
            pltpu.VMEM((2, FOLDED // 2, LANES), F32),
            pltpu.VMEM((4, FOLDED // 2, LANES), F32),
            folded(F32),
            folded(F32, 4, 4),
            pltpu.VMEM((LOCAL, STEPS), BF),
            pltpu.VMEM((LOCAL, STEPS), BF),
            folded(BF, 3, 4),
            folded(F32, 2, 2),
            folded(F32, 4),
            folded(BF, 2, 2),
            folded(BF, 2, 2),
            folded(BF, 4, 2),
            folded(BF, 4),
            folded(BF, 3),
            pltpu.VMEM((PACKED, LANES), F32),
            pltpu.VMEM((15, PIECE, LANES), F32),
            pltpu.VMEM((PIECE, LANES), F32),
            pltpu.VMEM((3, PIECE, LANES), F32),
            pltpu.VMEM((PIECE, LANES), F32),
            pltpu.VMEM((3, PIECE, LANES), F32),
            pltpu.VMEM((PACKED, LANES), F32),
            pltpu.VMEM((STEPS, STEPS), F32),
            pltpu.SemaphoreType.DMA((12,)),
            pltpu.SemaphoreType.DMA((N_SEMS,)),
            pltpu.SemaphoreType.DMA((N_SEMS,)),
        ],
        compiler_params=pltpu.CompilerParams(
            collective_id=0, has_side_effects=True, vmem_limit_bytes=VMEM_LIMIT
        ),
        name="exchange",
    )(rates, targets, goal, readout, corr, rec)


TILE = 256


def update_kernel(scaled, readout_new, left, corr, rec, corr_out, rec_out, readout_out):
    rows = aligned(pl.program_id(0) * TILE, TILE)
    drop = jnp.dot(left[rows, STEPS:], scaled[...], preferred_element_type=F32)
    corr_out[...] = corr[rows, :] - drop
    drop = jnp.dot(left[rows, :STEPS], scaled[...], preferred_element_type=F32)
    rec_out[...] = (rec[rows, :].astype(F32) - drop).astype(BF)
    readout_out[...] = readout_new[...]


def update(scaled, readout_new, left, corr, rec):
    rows = pl.BlockSpec((TILE, LOCAL), lambda g: (g, 0))
    return pl.pallas_call(
        update_kernel,
        grid=(LOCAL // TILE,),
        out_shape=[
            jax.ShapeDtypeStruct((LOCAL, LOCAL), F32),
            jax.ShapeDtypeStruct((LOCAL, LOCAL), BF),
            jax.ShapeDtypeStruct((OUTS, LOCAL), F32),
        ],
        in_specs=[pl.BlockSpec(memory_space=pltpu.VMEM)] * 5,
        out_specs=[rows, rows, pl.BlockSpec((OUTS, LOCAL), lambda g: (0, 0))],
        compiler_params=pltpu.CompilerParams(vmem_limit_bytes=VMEM_LIMIT),
        name="update",
    )(scaled, readout_new, left, corr, rec)


def on_device(*args):
    rates, targets, goal, corr, rec, readout = (pltpu.with_memory_space_constraint(v, pltpu.HBM) for v in args)
    return tuple(update(*gather_all(rates, targets, goal, readout, corr, rec)))


def solution(mesh):
    placed = (P(None, "col"), P(None, "row"), P(), P("row", "col"), P("row", "col"), P(None, "col"))
    return jax.shard_map(
        on_device,
        mesh=mesh,
        in_specs=placed,
        out_specs=(P("row", "col"), P("row", "col"), P(None, "col")),
        check_vma=False,
    )
```

```python
import functools

import jax
import jax.numpy as jnp
from jax import lax
from jax.experimental import pallas as pl
from jax.experimental.pallas import tpu as pltpu
from jax.sharding import PartitionSpec as P

MESH = pl.DeviceIdType.MESH
BF, F32 = jnp.bfloat16, jnp.float32
HIGH = lax.Precision.HIGHEST

STEPS = 192
LOCAL = 1024
OUTS = 16
QUARTER = 256
GROUP = 64
PIECE = 16
BLOCK = 64
PACKED = 3 * BLOCK + 2 * OUTS
OWNERS = PACKED // PIECE
LANES = 128
FOLDED = GROUP * STEPS // LANES
NT = (((1,), (1,)), ((), ()))
VMEM_LIMIT = 32 * 1024 * 1024


def split2(x):
    hi = x.astype(BF)
    return hi, (x - hi.astype(F32)).astype(BF)


def aligned(start, size):
    return pl.ds(pl.multiple_of(start, size), size)


def fold(v):
    low = jnp.concatenate([v[: GROUP // 2, LANES:], v[GROUP // 2 :, LANES:]], axis=1)
    return jnp.concatenate([v[:, :LANES], low], axis=0)


def unfold(v):
    rest = STEPS - LANES
    high = jnp.concatenate([v[GROUP:, :rest], v[GROUP:, rest:]], axis=0)
    return jnp.concatenate([v[:GROUP], high], axis=1)


def groups(v):
    return [v[g * GROUP : (g + 1) * GROUP] for g in range(v.shape[0] // GROUP)]


class Sems:
    def __init__(self):
        self.at = 0

    def take(self, count):
        first = self.at
        self.at += count
        return first


SUBS = 8
WIDE = 4


def reciprocal(v):
    return pl.reciprocal(v, approx=True)


def factor_two(a, b, d):
    ra = reciprocal(a)
    return b * ra, ra, a * reciprocal(a * d - b * b)


def factor_four(s):
    l = [[None] * WIDE for _ in range(WIDE)]
    l[1][0], rd0, rd1 = factor_two(s[0][0], s[1][0], s[1][1])
    c = {}
    for r in (2, 3):
        l[r][0] = s[r][0] * rd0
        c[r] = s[r][1] - l[1][0] * s[r][0]
        l[r][1] = c[r] * rd1

    def left(r, t):
        return s[r][t] - (l[r][0] * s[t][0] + l[r][1] * c[t])

    l[3][2], rd2, rd3 = factor_two(left(2, 2), left(3, 2), left(3, 3))
    return l, (rd0, rd1, rd2, rd3)


def eliminate(l, v):
    v1 = v[1] - l[1][0] * v[0]
    v2 = v[2] - l[2][0] * v[0] - l[2][1] * v1
    v3 = v[3] - l[3][0] * v[0] - l[3][1] * v1 - l[3][2] * v2
    return v[0], v1, v2, v3


def inverse_block(a, services):
    rows = [a[u * SUBS : (u + 1) * SUBS] for u in range(BLOCK // SUBS)]
    shape = (SUBS, BLOCK)
    lane = lax.broadcasted_iota(jnp.int32, shape, 1)
    sub = lax.broadcasted_iota(jnp.int32, shape, 0)
    span = range(WIDE)

    def column(row, k):
        return jnp.broadcast_to(row[:, k : k + 1], shape)

    def entry(col, r):
        return jnp.broadcast_to(col[r % SUBS : r % SUBS + 1], shape)

    s = None
    for k in range(0, BLOCK, WIDE):
        v, first = k // SUBS, k % SUBS
        col = [[column(row, k + b) for row in rows] for b in span]
        if s is None:
            s = [[entry(col[b][v], k + a) for b in range(a + 1)] for a in span]
        after = k + WIDE
        if after < BLOCK:
            row = rows[after // SUBS]
            ahead = [column(row, after + b) for b in span]
            ahead = [[entry(ahead[b], after + a) for b in range(a + 1)] for a in span]
            links = [[entry(col[b][after // SUBS], after + a) for b in span] for a in span]
        inside = (lane >= k) & (lane < k + WIDE)
        top = [
            jnp.where(inside, jnp.where(lane == k + b, 1.0, 0.0), entry(rows[v], first + b))
            for b in span
        ]
        l, rd = factor_four(s)
        if after < BLOCK:
            links = [eliminate(l, link) for link in links]
            scaled = [[link[b] * rd[b] for b in span] for link in links]
            s = [
                [
                    ahead[a][b]
                    - (
                        (scaled[a][0] * links[b][0] + scaled[a][1] * links[b][1])
                        + (scaled[a][2] * links[b][2] + scaled[a][3] * links[b][3])
                    )
                    for b in range(a + 1)
                ]
                for a in span
            ]
        top = eliminate(l, top)
        new = [None] * WIDE
        for a in reversed(span):
            new[a] = rd[a] * top[a]
            for b in range(a + 1, WIDE):
                new[a] = new[a] - l[b][a] * new[b]
        for u in range(len(rows)):
            m = eliminate(l, [col[b][u] for b in span])
            drop = ((m[0] * rd[0]) * top[0] + (m[1] * rd[1]) * top[1]) + ((m[2] * rd[2]) * top[2] + (m[3] * rd[3]) * top[3])
            rows[u] = jnp.where(inside, 0.0, rows[u]) - drop
        for a in span:
            rows[v] = jnp.where(sub == first + a, new[a], rows[v])
        if k % (4 * WIDE) == 3 * WIDE:
            for serve in services:
                serve()
                break
    return jnp.concatenate(rows, axis=0)


def dot32(a, b):
    return jnp.dot(a, b, precision=HIGH, preferred_element_type=F32)


def invert(cap, minv, services):
    blocks = range(STEPS // BLOCK)
    shape = (BLOCK, BLOCK)
    eye = jnp.where(lax.broadcasted_iota(jnp.int32, shape, 0) == lax.broadcasted_iota(jnp.int32, shape, 1), 1.0, 0.0)
    (k00, k11), (k22, k10), (k20, k21) = [
        [cap[r * BLOCK : (r + 1) * BLOCK, :BLOCK], cap[r * BLOCK : (r + 1) * BLOCK, BLOCK:]] for r in blocks
    ]
    a = [[k00 + eye, k10.T, k20.T], [k10, k11 + eye, k21.T], [k20, k21, k22 + eye]]
    for k in blocks:
        inv = inverse_block(a[k][k], services)
        new = [[None] * len(blocks) for _ in blocks]
        new[k][k] = inv
        for s in blocks:
            if s != k:
                new[k][s] = dot32(inv, a[k][s])
        for r in blocks:
            if r != k:
                new[r][k] = -dot32(a[r][k], inv)
                for s in blocks:
                    if s != k:
                        new[r][s] = a[r][s] - dot32(a[r][k], new[k][s])
        a = new
    for r in blocks:
        for s in blocks:
            minv[r * BLOCK : (r + 1) * BLOCK, s * BLOCK : (s + 1) * BLOCK] = a[r][s]


def comm_kernel(
    rates_hbm, targets_hbm, goal_hbm, readout_hbm, corr_hbm, rec_hbm,
    scaled, readout_new, e_all, corr_v, rec_v,
    rates, rates_t, targets, goal, readout, rx,
    g_part, g_mid, g_relay, g_sum, g_x, g_zrelay, g_zsum, g_z, g_piece, g_all, g_hi, g_lo,
    g_left,
    e_part, e_hold, e_aim, e_mid, e_relay, e_sum, e_x, e_low, e_zrelay, e_zsum, e_z,
    kpart, krow, ksum, kz, kmid, kx, cap, minv,
    load_sem, send_sem, recv_sem,
):
    i = lax.axis_index("row")
    j = lax.axis_index("col")
    y, zl, c = i // 4, (i // 2) % 2, i % 2
    x, zh = j // 4, j % 4
    sems = Sems()

    def quarter(q):
        return aligned((q % 4) * QUARTER, QUARTER)

    def remote(src, dst, at, dev, land=None):
        return pltpu.make_async_remote_copy(
            src_ref=src, dst_ref=dst, send_sem=send_sem.at[at], recv_sem=recv_sem.at[at if land is None else land],
            device_id=dev, device_id_type=MESH,
        )

    def load(src, dst, at):
        copy = pltpu.make_async_copy(src, dst, load_sem.at[at])
        copy.start()
        return copy

    rates_load = load(rates_hbm, rates, 8)
    rec_loads, corr_loads = {}, {}

    def load_quarter(d, loads, src, dst, at):
        part = quarter(x + d)
        loads[d] = load(src.at[part], dst.at[part], at + d)

    load_quarter(2, corr_loads, corr_hbm, corr_v, 4)

    barrier = pltpu.get_barrier_semaphore()

    def greet(dev):
        pl.semaphore_signal(barrier, inc=1, device_id=dev, device_id_type=MESH)

    for d in range(1, 16):
        greet({"row": (i + d) % 16})

    for d in range(1, 4):
        greet({"col": x * 4 + (zh + d) % 4})
        greet({"col": ((x + d) % 4) * 4 + zh})

    @pl.when(i != j)
    def _():
        greet({"row": j, "col": i})

    for z in range(2):
        source = y * 4 + 2 * c + z

        @pl.when((i != j) | (source != j))
        def _():
            greet({"row": j, "col": source})

    for d in (1, 3, 0):
        load_quarter(d, corr_loads, corr_hbm, corr_v, 4)
    for d in (2, 1, 3, 0):
        load_quarter(d, rec_loads, rec_hbm, rec_v, 0)
    readout_load = load(readout_hbm, readout, 9)
    targets_load = load(targets_hbm, targets, 10)
    goal_load = load(goal_hbm, goal, 11)

    rates_load.wait()
    rates_t[...] = rates[...].T

    def z_dev(d):
        return {"col": x * 4 + (zh + d) % 4}

    def x_dev(d):
        return {"col": ((x + d) % 4) * 4 + zh}

    def y_dev(d):
        return {"row": ((y + d) % 4) * 4 + zl * 2 + c}

    class RingSum:
        def __init__(self, part, hold, relay, total, landed, dev):
            self.hold, self.relay, self.total, self.landed = hold, relay, total, landed
            at = sems.take(6)
            self.copies = [
                remote(part(0, 0), relay.at[0], at, dev(1)),
                remote(part(0, 1), relay.at[1], at + 1, dev(3)),
                remote(part(1, 1), landed.at[0], at + 2, dev(1), at + 2),
                remote(part(2, 0), landed.at[1], at + 3, dev(3), at + 2),
                remote(total.at[0], landed.at[2], at + 4, dev(1), at + 2),
                remote(total.at[1], landed.at[3], at + 5, dev(3), at + 2),
            ]
            self.all = remote(landed, landed, at + 2, dev(1))

        def start(self, *which):
            for k in which:
                self.copies[k].start()

        def forward(self):
            for k in range(2):
                self.copies[k].wait_recv()
                self.total[k] = (self.hold(k) + self.relay[k].astype(F32)).astype(self.total.dtype)
                self.copies[4 + k].start()

        def finish(self):
            self.all.wait_recv()
            got = [self.landed[k].astype(F32) for k in range(4)]
            return got[2] + got[1], got[0] + got[3]

        def wait_sends(self):
            for copy in self.copies:
                copy.wait_send()

    class Ring:
        def __init__(self, block, me, dev):
            self.block, self.me, self.dev = block, me, dev
            self.at = sems.take(6)

        def copy(self, k, owner):
            block = self.block((0, 1, 1, 0, 0, 1)[k], owner % 4)
            return remote(block, block, self.at + k, self.dev((1, 1, 3, 3, 1, 3)[k]))

        def start(self):
            for k in (0, 2, 1, 3):
                self.copy(k, self.me).start()

        def forward(self):
            self.copy(0, self.me + 3).wait_recv()
            self.copy(4, self.me + 3).start()
            self.copy(2, self.me + 1).wait_recv()
            self.copy(5, self.me + 1).start()

        def finish(self):
            self.copy(1, self.me + 3).wait_recv()
            self.copy(3, self.me + 1).wait_recv()
            self.copy(4, self.me + 2).wait_recv()
            self.copy(5, self.me + 2).wait_recv()

        def wait_sends(self):
            for k in range(4):
                self.copy(k, self.me).wait_send()
            self.copy(4, self.me + 3).wait_send()
            self.copy(5, self.me + 1).wait_send()

    def prod_quarter(d, out):
        corr_loads[d].wait()
        hi, lo = split2(corr_v[quarter(x + d), :])
        value = jnp.dot(hi, rates_t[...], preferred_element_type=F32) + jnp.dot(
            lo, rates_t[...], preferred_element_type=F32
        )
        for g, part in enumerate(groups(value)):
            out[g] = fold(part)

    def drive_quarter(d):
        rec_loads[d].wait()
        value = jnp.dot(rec_v[quarter(x + d), :], rates_t[...], preferred_element_type=F32)
        return [fold(part) for part in groups(value)]

    pl.semaphore_wait(barrier, jnp.where(i == j, jnp.where(zl == c, 22, 23), 24))
    r_t = sems.take(1)
    r_src = rates.at[:, quarter(y)]

    @pl.when(i != j)
    def _():
        remote(r_src, rx, r_t, {"row": j, "col": i}).start()

    @pl.when(i == j)
    def _():
        pltpu.make_async_copy(r_src, rx, recv_sem.at[r_t]).start()

    def pairs(part):
        return lambda which, half: part.at[which, pl.ds(2 * half, 2)]

    g_ring = RingSum(
        pairs(g_part), lambda k: g_part[1, :2] if k == 0 else g_part[2, 2:], g_relay, g_sum, g_x, x_dev
    )
    prod_quarter(2, g_part.at[0])
    g_ring.start(0, 1)
    prod_quarter(1, g_part.at[1])
    g_ring.start(2)
    prod_quarter(3, g_part.at[2])
    g_ring.start(3)
    prod_quarter(0, g_mid)

    e_ring = RingSum(pairs(e_part), lambda k: e_hold[k], e_relay, e_sum, e_x, x_dev)
    for g, part in enumerate(drive_quarter(2)):
        e_part[0, g] = part.astype(BF)
    g_ring.forward()
    e_ring.start(0, 1)
    for g, part in enumerate(drive_quarter(1)):
        if g < 2:
            e_hold[0, g] = part
        else:
            e_part[1, g] = part.astype(BF)
    e_ring.start(2)
    for g, part in enumerate(drive_quarter(3)):
        if g < 2:
            e_part[2, g] = part.astype(BF)
        else:
            e_hold[1, g - 2] = part
    e_ring.start(3)

    readout_load.wait()
    guess = sum(
        jnp.dot(term, rates_t[...], preferred_element_type=F32) for term in split2(readout[...] * (1.0 / 16.0))
    )
    kpart[3 * BLOCK : 3 * BLOCK + OUTS, :] = guess[:, :LANES]
    kpart[3 * BLOCK + OUTS :, :] = jnp.concatenate([guess[:, LANES:], guess[:, LANES:]], axis=1)

    for g, part in enumerate(drive_quarter(0)):
        e_mid[g] = part
    targets_load.wait()
    aims = targets[:, quarter(x)].T.astype(F32)
    for g, part in enumerate(groups(aims)):
        e_aim[g] = fold(part)

    @pl.when(i != j)
    def _():
        remote(r_src, rx, r_t, {"row": j, "col": i}).wait_recv()

    @pl.when(i == j)
    def _():
        pltpu.make_async_copy(r_src, rx, recv_sem.at[r_t]).wait()

    got = g_ring.finish()
    for k in range(2):
        g_mid[2 * k : 2 * k + 2] = g_mid[2 * k : 2 * k + 2] + got[k]

    def g_slice(which, half):
        return g_mid.at[(zh + (2, 1, 3)[which]) % 4, pl.ds(half * (FOLDED // 2), FOLDED // 2)]

    z_ring = RingSum(g_slice, lambda k: g_slice(k + 1, k)[...], g_zrelay, g_zsum, g_z, z_dev)
    z_ring.start(0, 1, 2, 3)

    whole = sum(
        jnp.dot(rx[...], term, preferred_element_type=F32)
        for term in split2(jnp.concatenate([unfold(g_mid[g]) for g in range(4)], axis=0))
    )
    kb = [[whole[r * BLOCK : (r + 1) * BLOCK, s * BLOCK : (s + 1) * BLOCK] for s in range(3)] for r in range(3)]
    kpart[:BLOCK, :] = jnp.concatenate([kb[0][0], kb[1][1]], axis=1)
    kpart[BLOCK : 2 * BLOCK, :] = jnp.concatenate([kb[2][2], kb[1][0]], axis=1)
    kpart[2 * BLOCK : 3 * BLOCK, :] = jnp.concatenate([kb[2][0], kb[2][1]], axis=1)

    e_ring.forward()

    k_r = sems.take(1)

    for d in range(1, 16):
        owner = (i + d) % 16

        @pl.when(owner < OWNERS)
        def _():
            remote(kpart.at[aligned(owner * PIECE, PIECE)], krow.at[d - 1], k_r, {"row": owner}).start()

    z_ring.forward()
    k_x = sems.take(3)
    k_z = sems.take(3)

    @pl.when(i < OWNERS)
    def _():
        remote(krow, krow, k_r, {"row": (i + 1) % 16}).wait_recv()
        acc = kpart[aligned(i * PIECE, PIECE), :]
        for d in range(15):
            acc = acc + krow[d]
        ksum[...] = acc
        for d in range(1, 4):
            remote(ksum, kx.at[d - 1], k_x + d - 1, x_dev(d), k_x).start()

    got = e_ring.finish()
    for k in range(2):
        total = e_mid[2 * k : 2 * k + 2] + got[k]
        e_mid[2 * k : 2 * k + 2] = total
        e_low[2 * k : 2 * k + 2] = total.astype(BF)

    def e_slice(buf, which, half):
        return buf.at[(zh + (2, 1, 3)[which]) % 4, pl.ds(half * (FOLDED // 2), FOLDED // 2)]

    ez_ring = RingSum(
        functools.partial(e_slice, e_low), lambda k: e_slice(e_mid, k + 1, k)[...], e_zrelay, e_zsum, e_z, z_dev
    )
    ez_ring.start(0, 1, 2, 3)

    got = z_ring.finish()
    for k in range(2):
        part = pl.ds(k * (FOLDED // 2), FOLDED // 2)
        g_piece[part, :] = g_mid[zh, part, :] + got[k]
    s_t = sems.take(2)

    def swap_each(act_remote, act_local):
        for e in range(2):
            dst = g_all.at[x, zh]
            row = x * 4 + e * 2 + zh // 2

            @pl.when((i != j) | (row != i))
            def _():
                act_remote(remote(g_piece, dst, s_t + e, {"row": row, "col": i}, s_t + zh % 2))

            if act_local is not None:

                @pl.when((i == j) & (row == i))
                def _():
                    act_local(pltpu.make_async_copy(g_piece, dst, recv_sem.at[s_t + zh % 2]))

    swap_each(lambda copy: copy.start(), lambda copy: copy.start())

    def z_gather(buf):
        return Ring(
            lambda half, owner: buf.at[x, owner, pl.ds(half * (FOLDED // 2), FOLDED // 2)], zh, z_dev
        )

    def x_gather(buf):
        return Ring(lambda half, owner: buf.at[owner, pl.ds(2 * half, 2)], x, x_dev)

    g_left[x, zh] = g_piece[...].astype(BF)
    gz_gather = z_gather(g_left)
    gz_gather.start()

    @pl.when(i < OWNERS)
    def _():
        remote(kx, kx, k_x, x_dev(1)).wait_recv()
        kmid[...] = ksum[...] + kx[0] + kx[1] + kx[2]
        for d in range(1, 4):
            remote(kmid, kz.at[d - 1], k_z + d - 1, z_dev(d), k_z).start()

    ez_ring.forward()
    gz_gather.forward()

    k_g = sems.take(1)
    own_rows = aligned(i * PIECE, PIECE)

    @pl.when(i < OWNERS)
    def _():
        remote(kz, kz, k_z, z_dev(1)).wait_recv()
        cap[own_rows, :] = kmid[...] + kz[0] + kz[1] + kz[2]
        for d in range(1, 16):
            remote(cap.at[own_rows], cap.at[own_rows], k_g, {"row": (i + d) % 16}).start()

    got = ez_ring.finish()
    for k in range(2):
        part = pl.ds(k * (FOLDED // 2), FOLDED // 2)
        e_all[x, zh, part, :] = (e_mid[zh, part, :] + got[k] - e_aim[zh, part, :]).astype(BF)
    ez_gather = z_gather(e_all)
    ez_gather.start()

    for z in range(2):
        source = y * 4 + 2 * c + z
        dst = g_all.at[y, 2 * c + z]

        @pl.when((i != j) | (source != j))
        def _():
            remote(g_piece, dst, s_t, {"row": j, "col": source}, s_t + z).wait_recv()

        @pl.when((i == j) & (source == j))
        def _():
            pltpu.make_async_copy(g_piece, dst, recv_sem.at[s_t + z]).wait()

    y_ring = Ring(lambda half, owner: g_all.at[owner, 2 * c + half], y, y_dev)
    y_ring.start()
    gz_gather.finish()
    gx_gather = x_gather(g_left)
    gx_gather.start()
    ex_gather = x_gather(e_all)
    ez_gather.forward()

    others = cap.at[pl.ds(0, PACKED - PIECE)]

    @pl.when(i < OWNERS)
    def _():
        remote(others, others, k_g, {"row": (i + 1) % 16}).wait_recv()

    @pl.when(i >= OWNERS)
    def _():
        remote(cap, cap, k_g, {"row": (i + 1) % 16}).wait_recv()

    def rest():
        pass

    a_c = sems.take(1)
    sibling = {"row": i + 1 - 2 * c}
    mine = g_all.at[:, pl.ds(2 * c, 2)]
    theirs = g_all.at[:, pl.ds(2 - 2 * c, 2)]

    def serve_error():
        ez_gather.finish()
        ex_gather.start()

    def serve_y():
        y_ring.finish()
        remote(mine, mine, a_c, sibling).start()

    def serve_core():
        remote(theirs, theirs, a_c, sibling).wait_recv()

        @pl.loop(0, 4)
        def _(q):
            for g in range(4):
                hi, lo = split2(unfold(g_all[q, g]))
                rows = aligned(q * QUARTER + g * GROUP, GROUP)
                g_hi[rows, :] = hi
                g_lo[rows, :] = lo

    invert(
        cap, minv,
        iter((serve_error, y_ring.forward, gx_gather.forward, rest, ex_gather.forward, serve_y, rest, rest, serve_core)),
    )

    m_hi, m_lo = split2(minv[...])
    value = sum(
        lax.dot_general(m, g, NT, preferred_element_type=F32)
        for m, g in ((m_hi, g_lo[...]), (m_lo, g_hi[...]), (m_hi, g_hi[...]))
    )
    scaled[...] = value.astype(BF)
    goal_load.wait()
    guess = jnp.concatenate([cap[3 * BLOCK : 3 * BLOCK + OUTS, :], cap[3 * BLOCK + OUTS :, : STEPS - LANES]], axis=1)
    readout_new[...] = readout[...] - dot32(guess - goal[...], value)
    gx_gather.finish()

    @pl.loop(0, 4)
    def _(q):
        factor = jnp.concatenate([unfold(g_left[q, g]) for g in range(4)], axis=0)
        rows = quarter(q)
        corr_v[rows, :] = corr_v[rows, :] - jnp.dot(factor, scaled[...], preferred_element_type=F32)

    ex_gather.finish()

    @pl.when(i != j)
    def _():
        remote(r_src, rx, r_t, {"row": j, "col": i}).wait_send()

    swap_each(lambda copy: copy.wait_send(), None)
    for ring in (g_ring, e_ring, z_ring, ez_ring, gz_gather, gx_gather, ez_gather, ex_gather, y_ring):
        ring.wait_sends()

    some = kpart.at[pl.ds(0, PACKED - PIECE)]

    @pl.when(i < OWNERS)
    def _():
        remote(some, some, k_r, {"row": (i + 1) % 16}).wait_send()
        for d in range(1, 4):
            remote(ksum, kz.at[d - 1], k_z + d - 1, z_dev(d)).wait_send()
            remote(kmid, kx.at[d - 1], k_x + d - 1, x_dev(d)).wait_send()
        remote(krow, krow, k_g, {"row": (i + 1) % 16}).wait_send()

    @pl.when(i >= OWNERS)
    def _():
        remote(kpart, kpart, k_r, {"row": (i + 1) % 16}).wait_send()

    remote(mine, mine, a_c, sibling).wait_send()


N_SEMS = 96


def gather_all(rates, targets, goal, readout, corr, rec):
    hbm = pl.BlockSpec(memory_space=pl.ANY)

    def folded(dtype, *lead):
        return pltpu.VMEM((*lead, FOLDED, LANES), dtype)

    return pl.pallas_call(
        comm_kernel,
        out_shape=[
            jax.ShapeDtypeStruct((STEPS, LOCAL), BF),
            jax.ShapeDtypeStruct((OUTS, LOCAL), F32),
            jax.ShapeDtypeStruct((4, 4, FOLDED, LANES), BF),
            jax.ShapeDtypeStruct((LOCAL, LOCAL), F32),
            jax.ShapeDtypeStruct((LOCAL, LOCAL), BF),
        ],
        in_specs=[hbm] * 6,
        out_specs=[pl.BlockSpec(memory_space=pltpu.VMEM)] * 5,
        scratch_shapes=[
            pltpu.VMEM((STEPS, LOCAL), BF),
            pltpu.VMEM((LOCAL, STEPS), BF),
            pltpu.VMEM((STEPS, LOCAL), BF),
            pltpu.VMEM((OUTS, STEPS), F32),
            pltpu.VMEM((OUTS, LOCAL), F32),
            pltpu.VMEM((STEPS, QUARTER), BF),
            folded(F32, 3, 4),
            folded(F32, 4),
            folded(F32, 2, 2),
            folded(F32, 2, 2),
            folded(F32, 4, 2),
            pltpu.VMEM((2, FOLDED // 2, LANES), F32),
            pltpu.VMEM((2, FOLDED // 2, LANES), F32),
            pltpu.VMEM((4, FOLDED // 2, LANES), F32),
            folded(F32),
            folded(F32, 4, 4),
            pltpu.VMEM((LOCAL, STEPS), BF),
            pltpu.VMEM((LOCAL, STEPS), BF),
            folded(BF, 4, 4),
            folded(BF, 3, 4),
            folded(F32, 2, 2),
            folded(F32, 4),
            folded(F32, 4),
            folded(BF, 2, 2),
            folded(BF, 2, 2),
            folded(BF, 4, 2),
            folded(BF, 4),
            pltpu.VMEM((2, FOLDED // 2, LANES), BF),
            pltpu.VMEM((2, FOLDED // 2, LANES), BF),
            pltpu.VMEM((4, FOLDED // 2, LANES), BF),
            pltpu.VMEM((PACKED, LANES), F32),
            pltpu.VMEM((15, PIECE, LANES), F32),
            pltpu.VMEM((PIECE, LANES), F32),
            pltpu.VMEM((3, PIECE, LANES), F32),
            pltpu.VMEM((PIECE, LANES), F32),
            pltpu.VMEM((3, PIECE, LANES), F32),
            pltpu.VMEM((PACKED, LANES), F32),
            pltpu.VMEM((STEPS, STEPS), F32),
            pltpu.SemaphoreType.DMA((12,)),
            pltpu.SemaphoreType.DMA((N_SEMS,)),
            pltpu.SemaphoreType.DMA((N_SEMS,)),
        ],
        compiler_params=pltpu.CompilerParams(
            collective_id=0, has_side_effects=True, vmem_limit_bytes=VMEM_LIMIT
        ),
        name="exchange",
    )(rates, targets, goal, readout, corr, rec)


def update_kernel(scaled, readout_new, e_all, corr, rec, corr_out, rec_out, readout_out, fresh, sems):
    copies = [
        pltpu.make_async_copy(corr, corr_out, sems.at[0]),
        pltpu.make_async_copy(readout_new, readout_out, sems.at[1]),
    ]
    for copy in copies:
        copy.start()
    for q in range(4):
        rows = pl.ds(q * QUARTER, QUARTER)
        factor = jnp.concatenate([unfold(e_all[q, g]) for g in range(4)], axis=0)
        drop = jnp.dot(factor, scaled[...], preferred_element_type=F32)
        fresh[rows, :] = (rec[rows, :].astype(F32) - drop).astype(BF)
        copies.append(pltpu.make_async_copy(fresh.at[rows], rec_out.at[rows], sems.at[2 + q]))
        copies[-1].start()
    for copy in copies:
        copy.wait()


def update(scaled, readout_new, e_all, corr, rec):
    return pl.pallas_call(
        update_kernel,
        out_shape=[
            jax.ShapeDtypeStruct((LOCAL, LOCAL), F32),
            jax.ShapeDtypeStruct((LOCAL, LOCAL), BF),
            jax.ShapeDtypeStruct((OUTS, LOCAL), F32),
        ],
        in_specs=[pl.BlockSpec(memory_space=pltpu.VMEM)] * 5,
        out_specs=[pl.BlockSpec(memory_space=pl.ANY)] * 3,
        scratch_shapes=[pltpu.VMEM((LOCAL, LOCAL), BF), pltpu.SemaphoreType.DMA((6,))],
        compiler_params=pltpu.CompilerParams(vmem_limit_bytes=VMEM_LIMIT),
        name="update",
    )(scaled, readout_new, e_all, corr, rec)


def on_device(*args):
    rates, targets, goal, corr, rec, readout = (pltpu.with_memory_space_constraint(v, pltpu.HBM) for v in args)
    return tuple(update(*gather_all(rates, targets, goal, readout, corr, rec)))


def solution(mesh):
    placed = (P(None, "col"), P(None, "row"), P(), P("row", "col"), P("row", "col"), P(None, "col"))
    return jax.shard_map(
        on_device,
        mesh=mesh,
        in_specs=placed,
        out_specs=(P("row", "col"), P("row", "col"), P(None, "col")),
        check_vma=False,
    )
```

```python
import functools

import jax
import jax.numpy as jnp
from jax import lax
from jax.experimental import pallas as pl
from jax.experimental.pallas import tpu as pltpu
from jax.sharding import PartitionSpec as P

MESH = pl.DeviceIdType.MESH
BF, F32 = jnp.bfloat16, jnp.float32
HIGH = lax.Precision.HIGHEST

STEPS = 192
LOCAL = 1024
OUTS = 16
QUARTER = 256
GROUP = 64
PIECE = 16
BLOCK = 64
PACKED = 3 * BLOCK + 2 * OUTS
OWNERS = PACKED // PIECE
LANES = 128
FOLDED = GROUP * STEPS // LANES
NT = (((1,), (1,)), ((), ()))
VMEM_LIMIT = 32 * 1024 * 1024


def split2(x):
    hi = x.astype(BF)
    return hi, (x - hi.astype(F32)).astype(BF)


def aligned(start, size):
    return pl.ds(pl.multiple_of(start, size), size)


def fold(v):
    low = jnp.concatenate([v[: GROUP // 2, LANES:], v[GROUP // 2 :, LANES:]], axis=1)
    return jnp.concatenate([v[:, :LANES], low], axis=0)


def unfold(v):
    rest = STEPS - LANES
    high = jnp.concatenate([v[GROUP:, :rest], v[GROUP:, rest:]], axis=0)
    return jnp.concatenate([v[:GROUP], high], axis=1)


def groups(v):
    return [v[g * GROUP : (g + 1) * GROUP] for g in range(v.shape[0] // GROUP)]


class Sems:
    def __init__(self):
        self.at = 0

    def take(self, count):
        first = self.at
        self.at += count
        return first


SUBS = 8
WIDE = 4


def reciprocal(v):
    return pl.reciprocal(v, approx=True)


def factor_two(a, b, d):
    ra = reciprocal(a)
    return b * ra, ra, a * reciprocal(a * d - b * b)


def factor_four(s):
    l = [[None] * WIDE for _ in range(WIDE)]
    l[1][0], rd0, rd1 = factor_two(s[0][0], s[1][0], s[1][1])
    c = {}
    for r in (2, 3):
        l[r][0] = s[r][0] * rd0
        c[r] = s[r][1] - l[1][0] * s[r][0]
        l[r][1] = c[r] * rd1

    def left(r, t):
        return s[r][t] - (l[r][0] * s[t][0] + l[r][1] * c[t])

    l[3][2], rd2, rd3 = factor_two(left(2, 2), left(3, 2), left(3, 3))
    return l, (rd0, rd1, rd2, rd3)


def eliminate(l, v):
    v1 = v[1] - l[1][0] * v[0]
    v2 = v[2] - l[2][0] * v[0] - l[2][1] * v1
    v3 = v[3] - l[3][0] * v[0] - l[3][1] * v1 - l[3][2] * v2
    return v[0], v1, v2, v3


def inverse_block(a, services):
    rows = [a[u * SUBS : (u + 1) * SUBS] for u in range(BLOCK // SUBS)]
    shape = (SUBS, BLOCK)
    lane = lax.broadcasted_iota(jnp.int32, shape, 1)
    sub = lax.broadcasted_iota(jnp.int32, shape, 0)
    span = range(WIDE)

    def column(row, k):
        return jnp.broadcast_to(row[:, k : k + 1], shape)

    def entry(col, r):
        return jnp.broadcast_to(col[r % SUBS : r % SUBS + 1], shape)

    s = None
    for k in range(0, BLOCK, WIDE):
        v, first = k // SUBS, k % SUBS
        col = [[column(row, k + b) for row in rows] for b in span]
        if s is None:
            s = [[entry(col[b][v], k + a) for b in range(a + 1)] for a in span]
        after = k + WIDE
        if after < BLOCK:
            row = rows[after // SUBS]
            ahead = [column(row, after + b) for b in span]
            ahead = [[entry(ahead[b], after + a) for b in range(a + 1)] for a in span]
            links = [[entry(col[b][after // SUBS], after + a) for b in span] for a in span]
        inside = (lane >= k) & (lane < k + WIDE)
        top = [
            jnp.where(inside, jnp.where(lane == k + b, 1.0, 0.0), entry(rows[v], first + b))
            for b in span
        ]
        l, rd = factor_four(s)
        if after < BLOCK:
            links = [eliminate(l, link) for link in links]
            scaled = [[link[b] * rd[b] for b in span] for link in links]
            s = [
                [
                    ahead[a][b]
                    - (
                        (scaled[a][0] * links[b][0] + scaled[a][1] * links[b][1])
                        + (scaled[a][2] * links[b][2] + scaled[a][3] * links[b][3])
                    )
                    for b in range(a + 1)
                ]
                for a in span
            ]
        top = eliminate(l, top)
        new = [None] * WIDE
        for a in reversed(span):
            new[a] = rd[a] * top[a]
            for b in range(a + 1, WIDE):
                new[a] = new[a] - l[b][a] * new[b]
        for u in range(len(rows)):
            m = eliminate(l, [col[b][u] for b in span])
            drop = ((m[0] * rd[0]) * top[0] + (m[1] * rd[1]) * top[1]) + ((m[2] * rd[2]) * top[2] + (m[3] * rd[3]) * top[3])
            rows[u] = jnp.where(inside, 0.0, rows[u]) - drop
        for a in span:
            rows[v] = jnp.where(sub == first + a, new[a], rows[v])
        if k % (4 * WIDE) == 3 * WIDE:
            for serve in services:
                serve()
                break
    return jnp.concatenate(rows, axis=0)


def dot32(a, b):
    return jnp.dot(a, b, precision=HIGH, preferred_element_type=F32)


def invert(cap, minv, services):
    blocks = range(STEPS // BLOCK)
    shape = (BLOCK, BLOCK)
    eye = jnp.where(lax.broadcasted_iota(jnp.int32, shape, 0) == lax.broadcasted_iota(jnp.int32, shape, 1), 1.0, 0.0)
    (k00, k11), (k22, k10), (k20, k21) = [
        [cap[r * BLOCK : (r + 1) * BLOCK, :BLOCK], cap[r * BLOCK : (r + 1) * BLOCK, BLOCK:]] for r in blocks
    ]
    a = [[k00 + eye, k10.T, k20.T], [k10, k11 + eye, k21.T], [k20, k21, k22 + eye]]
    for k in blocks:
        inv = inverse_block(a[k][k], services)
        new = [[None] * len(blocks) for _ in blocks]
        new[k][k] = inv
        for s in blocks:
            if s != k:
                new[k][s] = dot32(inv, a[k][s])
        for r in blocks:
            if r != k:
                new[r][k] = -dot32(a[r][k], inv)
                for s in blocks:
                    if s != k:
                        new[r][s] = a[r][s] - dot32(a[r][k], new[k][s])
        a = new
    for r in blocks:
        for s in blocks:
            minv[r * BLOCK : (r + 1) * BLOCK, s * BLOCK : (s + 1) * BLOCK] = a[r][s]


def comm_kernel(
    rates_hbm, targets_hbm, goal_hbm, readout_hbm, corr_hbm, rec_hbm,
    scaled, readout_new, left, corr_v, rec_v,
    rates, rates_t, targets, goal, readout, rx,
    g_part, g_mid, g_relay, g_sum, g_x, g_zrelay, g_zsum, g_z, g_piece, g_all, g_hi, g_lo,
    e_part, e_hold, e_aim, e_mid, e_relay, e_sum, e_x, e_low, e_z,
    kpart, krow, ksum, kz, kmid, kx, cap, minv,
    load_sem, send_sem, recv_sem,
):
    i = lax.axis_index("row")
    j = lax.axis_index("col")
    y, zl, c = i // 4, (i // 2) % 2, i % 2
    x, zh = j // 4, j % 4
    sems = Sems()

    def quarter(q):
        return aligned((q % 4) * QUARTER, QUARTER)

    def remote(src, dst, at, dev, land=None):
        return pltpu.make_async_remote_copy(
            src_ref=src, dst_ref=dst, send_sem=send_sem.at[at], recv_sem=recv_sem.at[at if land is None else land],
            device_id=dev, device_id_type=MESH,
        )

    def load(src, dst, at):
        copy = pltpu.make_async_copy(src, dst, load_sem.at[at])
        copy.start()
        return copy

    rates_load = load(rates_hbm, rates, 8)
    rec_loads, corr_loads = {}, {}

    def load_quarter(d, loads, src, dst, at):
        part = quarter(x + d)
        loads[d] = load(src.at[part], dst.at[part], at + d)

    load_quarter(2, corr_loads, corr_hbm, corr_v, 4)

    barrier = pltpu.get_barrier_semaphore()

    def greet(dev):
        pl.semaphore_signal(barrier, inc=1, device_id=dev, device_id_type=MESH)

    for d in range(1, 16):
        greet({"row": (i + d) % 16})

    for d in range(1, 4):
        greet({"col": x * 4 + (zh + d) % 4})
        greet({"col": ((x + d) % 4) * 4 + zh})

    @pl.when(i != j)
    def _():
        greet({"row": j, "col": i})

    for z in range(2):
        source = y * 4 + 2 * c + z

        @pl.when((i != j) | (source != j))
        def _():
            greet({"row": j, "col": source})

    for d in (1, 3, 0):
        load_quarter(d, corr_loads, corr_hbm, corr_v, 4)
    for d in (2, 1, 3, 0):
        load_quarter(d, rec_loads, rec_hbm, rec_v, 0)
    readout_load = load(readout_hbm, readout, 9)
    targets_load = load(targets_hbm, targets, 10)
    goal_load = load(goal_hbm, goal, 11)

    rates_load.wait()
    rates_t[...] = rates[...].T

    def z_dev(d):
        return {"col": x * 4 + (zh + d) % 4}

    def x_dev(d):
        return {"col": ((x + d) % 4) * 4 + zh}

    def y_dev(d):
        return {"row": ((y + d) % 4) * 4 + zl * 2 + c}

    class RingSum:
        def __init__(self, part, hold, relay, total, landed, sent, dev):
            self.hold, self.relay, self.total, self.landed = hold, relay, total, landed
            at = sems.take(3)
            self.copies = [
                remote(part(0, 0), relay.at[0], at, dev(1), at),
                remote(part(0, 1), relay.at[1], at, dev(3), at + 1),
                remote(part(1, 1), landed.at[0], at, dev(1), at + 2),
                remote(part(2, 0), landed.at[1], at, dev(3), at + 2),
                remote(total.at[0], landed.at[2], at, dev(1), at + 2),
                remote(total.at[1], landed.at[3], at, dev(3), at + 2),
            ]
            self.arrived = remote(landed, landed, at, dev(1), at + 2)
            self.sent = remote(sent, sent, at, dev(1))

        def start(self, *which):
            for k in which:
                self.copies[k].start()

        def forward(self):
            for k in range(2):
                self.copies[k].wait_recv()
                self.total[k] = (self.hold(k) + self.relay[k].astype(F32)).astype(self.total.dtype)
                self.copies[4 + k].start()

        def finish(self):
            self.arrived.wait_recv()
            got = [self.landed[k].astype(F32) for k in range(4)]
            return got[2] + got[1], got[0] + got[3]

        def wait_sends(self):
            self.sent.wait_send()

    class Ring:
        def __init__(self, block, me, dev, four, six):
            self.block, self.me, self.dev = block, me, dev
            self.at = sems.take(3)
            self.arrived = remote(four, four, self.at, dev(1), self.at + 2)
            self.sent = remote(six, six, self.at, dev(1))

        def copy(self, k, owner):
            block = self.block((0, 1, 1, 0, 0, 1)[k], owner % 4)
            land = self.at + (0, 2, 1, 2, 2, 2)[k]
            return remote(block, block, self.at, self.dev((1, 1, 3, 3, 1, 3)[k]), land)

        def start(self):
            for k in (0, 2, 1, 3):
                self.copy(k, self.me).start()

        def forward(self):
            self.copy(0, self.me + 3).wait_recv()
            self.copy(4, self.me + 3).start()
            self.copy(2, self.me + 1).wait_recv()
            self.copy(5, self.me + 1).start()

        def finish(self):
            self.arrived.wait_recv()

        def wait_sends(self):
            self.sent.wait_send()

    def prod_quarter(d, out):
        corr_loads[d].wait()
        hi, lo = split2(corr_v[quarter(x + d), :])
        value = jnp.dot(hi, rates_t[...], preferred_element_type=F32) + jnp.dot(
            lo, rates_t[...], preferred_element_type=F32
        )
        for g, part in enumerate(groups(value)):
            out[g] = fold(part)

    def drive_quarter(d):
        rec_loads[d].wait()
        value = jnp.dot(rec_v[quarter(x + d), :], rates_t[...], preferred_element_type=F32)
        return [fold(part) for part in groups(value)]

    pl.semaphore_wait(barrier, jnp.where(i == j, jnp.where(zl == c, 22, 23), 24))
    r_t = sems.take(1)
    r_src = rates.at[:, quarter(y)]

    @pl.when(i != j)
    def _():
        remote(r_src, rx, r_t, {"row": j, "col": i}).start()

    @pl.when(i == j)
    def _():
        pltpu.make_async_copy(r_src, rx, recv_sem.at[r_t]).start()

    def pairs(part):
        return lambda which, half: part.at[which, pl.ds(2 * half, 2)]

    g_ring = RingSum(
        pairs(g_part), lambda k: g_part[1, :2] if k == 0 else g_part[2, 2:], g_relay, g_sum, g_x, g_part, x_dev
    )
    prod_quarter(2, g_part.at[0])
    g_ring.start(0, 1)
    prod_quarter(1, g_part.at[1])
    g_ring.start(2)
    prod_quarter(3, g_part.at[2])
    g_ring.start(3)
    prod_quarter(0, g_mid)

    e_ring = RingSum(pairs(e_part), lambda k: e_hold[k], e_relay, e_sum, e_x, e_part, x_dev)
    for g, part in enumerate(drive_quarter(2)):
        e_part[0, g] = part.astype(BF)
    g_ring.forward()
    e_ring.start(0, 1)
    for g, part in enumerate(drive_quarter(1)):
        if g < 2:
            e_hold[0, g] = part
        else:
            e_part[1, g] = part.astype(BF)
    e_ring.start(2)
    for g, part in enumerate(drive_quarter(3)):
        if g < 2:
            e_part[2, g] = part.astype(BF)
        else:
            e_hold[1, g - 2] = part
    e_ring.start(3)

    readout_load.wait()
    guess = sum(
        jnp.dot(term, rates_t[...], preferred_element_type=F32) for term in split2(readout[...] * (1.0 / 16.0))
    )
    kpart[3 * BLOCK : 3 * BLOCK + OUTS, :] = guess[:, :LANES]
    kpart[3 * BLOCK + OUTS :, :] = jnp.concatenate([guess[:, LANES:], guess[:, LANES:]], axis=1)

    for g, part in enumerate(drive_quarter(0)):
        e_mid[g] = part
    targets_load.wait()
    aims = targets[:, quarter(x)].T.astype(F32)
    for g, part in enumerate(groups(aims)):
        e_aim[g] = fold(part)

    @pl.when(i != j)
    def _():
        remote(r_src, rx, r_t, {"row": j, "col": i}).wait_recv()

    @pl.when(i == j)
    def _():
        pltpu.make_async_copy(r_src, rx, recv_sem.at[r_t]).wait()

    got = g_ring.finish()
    for k in range(2):
        g_mid[2 * k : 2 * k + 2] = g_mid[2 * k : 2 * k + 2] + got[k]

    def g_slice(which, half):
        return g_mid.at[(zh + (2, 1, 3)[which]) % 4, pl.ds(half * (FOLDED // 2), FOLDED // 2)]

    z_ring = RingSum(g_slice, lambda k: g_slice(k + 1, k)[...], g_zrelay, g_zsum, g_z, g_part.at[0, pl.ds(0, 3)], z_dev)
    z_ring.start(0, 1, 2, 3)

    whole = sum(
        jnp.dot(rx[...], term, preferred_element_type=F32)
        for term in split2(jnp.concatenate([unfold(g_mid[g]) for g in range(4)], axis=0))
    )
    kb = [[whole[r * BLOCK : (r + 1) * BLOCK, s * BLOCK : (s + 1) * BLOCK] for s in range(3)] for r in range(3)]
    kpart[:BLOCK, :] = jnp.concatenate([kb[0][0], kb[1][1]], axis=1)
    kpart[BLOCK : 2 * BLOCK, :] = jnp.concatenate([kb[2][2], kb[1][0]], axis=1)
    kpart[2 * BLOCK : 3 * BLOCK, :] = jnp.concatenate([kb[2][0], kb[2][1]], axis=1)

    e_ring.forward()

    k_r = sems.take(1)

    for d in range(1, 16):
        owner = (i + d) % 16

        @pl.when(owner < OWNERS)
        def _():
            remote(kpart.at[aligned(owner * PIECE, PIECE)], krow.at[d - 1], k_r, {"row": owner}).start()

    z_ring.forward()
    k_x = sems.take(1)
    k_z = sems.take(1)

    @pl.when(i < OWNERS)
    def _():
        remote(krow, krow, k_r, {"row": (i + 1) % 16}).wait_recv()
        acc = kpart[aligned(i * PIECE, PIECE), :]
        for d in range(15):
            acc = acc + krow[d]
        ksum[...] = acc
        for d in range(1, 4):
            remote(ksum, kx.at[d - 1], k_x, x_dev(d)).start()

    got = e_ring.finish()
    for k in range(2):
        total = e_mid[2 * k : 2 * k + 2] + got[k]
        e_mid[2 * k : 2 * k + 2] = total
        e_low[2 * k : 2 * k + 2] = total.astype(BF)
    e_at = sems.take(1)

    def e_z_copy(d):
        return remote(e_low.at[(zh + d) % 4], e_z.at[d - 1], e_at, z_dev(d))

    for d in range(1, 4):
        e_z_copy(d).start()

    @pl.when(i < OWNERS)
    def _():
        remote(kx, kx, k_x, x_dev(1)).wait_recv()
        kmid[...] = ksum[...] + kx[0] + kx[1] + kx[2]
        for d in range(1, 4):
            remote(kmid, kz.at[d - 1], k_z, z_dev(d)).start()

    got = z_ring.finish()
    for k in range(2):
        part = pl.ds(k * (FOLDED // 2), FOLDED // 2)
        g_piece[part, :] = g_mid[zh, part, :] + got[k]
    own = aligned(x * QUARTER + zh * GROUP, GROUP)
    s_t = sems.take(2)

    def swap_each(act_remote, act_local):
        for e in range(2):
            dst = g_all.at[x, zh]
            row = x * 4 + e * 2 + zh // 2

            @pl.when((i != j) | (row != i))
            def _():
                act_remote(remote(g_piece, dst, s_t + e, {"row": row, "col": i}, s_t + zh % 2))

            if act_local is not None:

                @pl.when((i == j) & (row == i))
                def _():
                    act_local(pltpu.make_async_copy(g_piece, dst, recv_sem.at[s_t + zh % 2]))

    swap_each(lambda copy: copy.start(), lambda copy: copy.start())
    left[own, STEPS:] = unfold(g_piece[...]).astype(BF)

    remote(e_z, e_z, e_at, z_dev(1)).wait_recv()
    total = e_mid[zh] - e_aim[zh]
    for d in range(3):
        total = total + e_z[d].astype(F32)
    left[own, :STEPS] = unfold(total).astype(BF)
    lz_ring = Ring(
        lambda half, owner: left.at[aligned(x * QUARTER + owner * GROUP + half * (GROUP // 2), GROUP // 2)], zh, z_dev,
        left.at[pl.ds(0, 2 * GROUP)], left.at[pl.ds(0, 3 * GROUP)],
    )
    lz_ring.start()

    k_g = sems.take(1)
    own_rows = aligned(i * PIECE, PIECE)

    @pl.when(i < OWNERS)
    def _():
        remote(kz, kz, k_z, z_dev(1)).wait_recv()
        cap[own_rows, :] = kmid[...] + kz[0] + kz[1] + kz[2]
        for d in range(1, 16):
            remote(cap.at[own_rows], cap.at[own_rows], k_g, {"row": (i + d) % 16}).start()

    for z in range(2):
        source = y * 4 + 2 * c + z
        dst = g_all.at[y, 2 * c + z]

        @pl.when((i != j) | (source != j))
        def _():
            remote(g_piece, dst, s_t, {"row": j, "col": source}, s_t + z).wait_recv()

        @pl.when((i == j) & (source == j))
        def _():
            pltpu.make_async_copy(g_piece, dst, recv_sem.at[s_t + z]).wait()

    y_ring = Ring(lambda half, owner: g_all.at[owner, 2 * c + half], y, y_dev, g_all.at[0], g_all.at[pl.ds(0, 3), pl.ds(0, 2)])
    y_ring.start()
    lz_ring.forward()
    l_ring = Ring(
        lambda half, owner: left.at[aligned(owner * QUARTER + half * LANES, LANES)], x, x_dev,
        left.at[pl.ds(0, 2 * QUARTER)], left.at[pl.ds(0, 3 * QUARTER)],
    )

    others = cap.at[pl.ds(0, PACKED - PIECE)]

    @pl.when(i < OWNERS)
    def _():
        remote(others, others, k_g, {"row": (i + 1) % 16}).wait_recv()

    @pl.when(i >= OWNERS)
    def _():
        remote(cap, cap, k_g, {"row": (i + 1) % 16}).wait_recv()

    def rest():
        pass

    a_c = sems.take(1)
    sibling = {"row": i + 1 - 2 * c}
    mine = g_all.at[:, pl.ds(2 * c, 2)]
    theirs = g_all.at[:, pl.ds(2 - 2 * c, 2)]

    def serve_left():
        lz_ring.finish()
        l_ring.start()

    def serve_y():
        y_ring.finish()
        remote(mine, mine, a_c, sibling).start()

    def serve_core():
        remote(theirs, theirs, a_c, sibling).wait_recv()

        @pl.loop(0, 4)
        def _(q):
            for g in range(4):
                hi, lo = split2(unfold(g_all[q, g]))
                rows = aligned(q * QUARTER + g * GROUP, GROUP)
                g_hi[rows, :] = hi
                g_lo[rows, :] = lo

    invert(cap, minv, iter((serve_left, y_ring.forward, rest, rest, l_ring.forward, rest, serve_y, rest, rest, serve_core)))

    m_hi, m_lo = split2(minv[...])
    value = sum(
        lax.dot_general(m, g, NT, preferred_element_type=F32)
        for m, g in ((m_hi, g_lo[...]), (m_lo, g_hi[...]), (m_hi, g_hi[...]))
    )
    scaled[...] = value.astype(BF)
    goal_load.wait()
    guess = jnp.concatenate([cap[3 * BLOCK : 3 * BLOCK + OUTS, :], cap[3 * BLOCK + OUTS :, : STEPS - LANES]], axis=1)
    readout_new[...] = readout[...] - dot32(guess - goal[...], value)
    l_ring.finish()

    @pl.when(i != j)
    def _():
        remote(r_src, rx, r_t, {"row": j, "col": i}).wait_send()

    swap_each(lambda copy: copy.wait_send(), None)
    remote(e_z, e_z, e_at, z_dev(1)).wait_send()
    for ring in (g_ring, e_ring, z_ring, lz_ring, y_ring, l_ring):
        ring.wait_sends()

    some = kpart.at[pl.ds(0, PACKED - PIECE)]

    @pl.when(i < OWNERS)
    def _():
        remote(some, some, k_r, {"row": (i + 1) % 16}).wait_send()
        remote(kx, kx, k_x, x_dev(1)).wait_send()
        remote(kz, kz, k_z, z_dev(1)).wait_send()
        remote(krow, krow, k_g, {"row": (i + 1) % 16}).wait_send()

    @pl.when(i >= OWNERS)
    def _():
        remote(kpart, kpart, k_r, {"row": (i + 1) % 16}).wait_send()

    remote(mine, mine, a_c, sibling).wait_send()


N_SEMS = 96


def gather_all(rates, targets, goal, readout, corr, rec):
    hbm = pl.BlockSpec(memory_space=pl.ANY)

    def folded(dtype, *lead):
        return pltpu.VMEM((*lead, FOLDED, LANES), dtype)

    return pl.pallas_call(
        comm_kernel,
        out_shape=[
            jax.ShapeDtypeStruct((STEPS, LOCAL), BF),
            jax.ShapeDtypeStruct((OUTS, LOCAL), F32),
            jax.ShapeDtypeStruct((LOCAL, 2 * STEPS), BF),
            jax.ShapeDtypeStruct((LOCAL, LOCAL), F32),
            jax.ShapeDtypeStruct((LOCAL, LOCAL), BF),
        ],
        in_specs=[hbm] * 6,
        out_specs=[pl.BlockSpec(memory_space=pltpu.VMEM)] * 5,
        scratch_shapes=[
            pltpu.VMEM((STEPS, LOCAL), BF),
            pltpu.VMEM((LOCAL, STEPS), BF),
            pltpu.VMEM((STEPS, LOCAL), BF),
            pltpu.VMEM((OUTS, STEPS), F32),
            pltpu.VMEM((OUTS, LOCAL), F32),
            pltpu.VMEM((STEPS, QUARTER), BF),
            folded(F32, 3, 4),
            folded(F32, 4),
            folded(F32, 2, 2),
            folded(F32, 2, 2),
            folded(F32, 4, 2),
            pltpu.VMEM((2, FOLDED // 2, LANES), F32),
            pltpu.VMEM((2, FOLDED // 2, LANES), F32),
            pltpu.VMEM((4, FOLDED // 2, LANES), F32),
            folded(F32),
            folded(F32, 4, 4),
            pltpu.VMEM((LOCAL, STEPS), BF),
            pltpu.VMEM((LOCAL, STEPS), BF),
            folded(BF, 3, 4),
            folded(F32, 2, 2),
            folded(F32, 4),
            folded(F32, 4),
            folded(BF, 2, 2),
            folded(BF, 2, 2),
            folded(BF, 4, 2),
            folded(BF, 4),
            folded(BF, 3),
            pltpu.VMEM((PACKED, LANES), F32),
            pltpu.VMEM((15, PIECE, LANES), F32),
            pltpu.VMEM((PIECE, LANES), F32),
            pltpu.VMEM((3, PIECE, LANES), F32),
            pltpu.VMEM((PIECE, LANES), F32),
            pltpu.VMEM((3, PIECE, LANES), F32),
            pltpu.VMEM((PACKED, LANES), F32),
            pltpu.VMEM((STEPS, STEPS), F32),
            pltpu.SemaphoreType.DMA((12,)),
            pltpu.SemaphoreType.DMA((N_SEMS,)),
            pltpu.SemaphoreType.DMA((N_SEMS,)),
        ],
        compiler_params=pltpu.CompilerParams(
            collective_id=0, has_side_effects=True, vmem_limit_bytes=VMEM_LIMIT
        ),
        name="exchange",
    )(rates, targets, goal, readout, corr, rec)


TILE = 256


def update_kernel(scaled, readout_new, left, corr, rec, corr_out, rec_out, readout_out):
    rows = aligned(pl.program_id(0) * TILE, TILE)
    drop = jnp.dot(left[rows, STEPS:], scaled[...], preferred_element_type=F32)
    corr_out[...] = corr[rows, :] - drop
    drop = jnp.dot(left[rows, :STEPS], scaled[...], preferred_element_type=F32)
    rec_out[...] = (rec[rows, :].astype(F32) - drop).astype(BF)
    readout_out[...] = readout_new[...]


def update(scaled, readout_new, left, corr, rec):
    rows = pl.BlockSpec((TILE, LOCAL), lambda g: (g, 0))
    return pl.pallas_call(
        update_kernel,
        grid=(LOCAL // TILE,),
        out_shape=[
            jax.ShapeDtypeStruct((LOCAL, LOCAL), F32),
            jax.ShapeDtypeStruct((LOCAL, LOCAL), BF),
            jax.ShapeDtypeStruct((OUTS, LOCAL), F32),
        ],
        in_specs=[pl.BlockSpec(memory_space=pltpu.VMEM)] * 5,
        out_specs=[rows, rows, pl.BlockSpec((OUTS, LOCAL), lambda g: (0, 0))],
        compiler_params=pltpu.CompilerParams(vmem_limit_bytes=VMEM_LIMIT),
        name="update",
    )(scaled, readout_new, left, corr, rec)


def on_device(*args):
    rates, targets, goal, corr, rec, readout = (pltpu.with_memory_space_constraint(v, pltpu.HBM) for v in args)
    return tuple(update(*gather_all(rates, targets, goal, readout, corr, rec)))


def solution(mesh):
    placed = (P(None, "col"), P(None, "row"), P(), P("row", "col"), P("row", "col"), P(None, "col"))
    return jax.shard_map(
        on_device,
        mesh=mesh,
        in_specs=placed,
        out_specs=(P("row", "col"), P("row", "col"), P(None, "col")),
        check_vma=False,
    )
```

```python
import functools

import jax
import jax.numpy as jnp
from jax import lax
from jax.experimental import pallas as pl
from jax.experimental.pallas import tpu as pltpu
from jax.sharding import PartitionSpec as P

MESH = pl.DeviceIdType.MESH
BF, F32 = jnp.bfloat16, jnp.float32
HIGH = lax.Precision.HIGHEST

STEPS = 192
LOCAL = 1024
OUTS = 16
QUARTER = 256
GROUP = 64
PIECE = 16
BLOCK = 64
PACKED = 3 * BLOCK + 2 * OUTS
OWNERS = PACKED // PIECE
LANES = 128
FOLDED = GROUP * STEPS // LANES
NT = (((1,), (1,)), ((), ()))
VMEM_LIMIT = 32 * 1024 * 1024


def split2(x):
    hi = x.astype(BF)
    return hi, (x - hi.astype(F32)).astype(BF)


def aligned(start, size):
    return pl.ds(pl.multiple_of(start, size), size)


def fold(v):
    low = jnp.concatenate([v[: GROUP // 2, LANES:], v[GROUP // 2 :, LANES:]], axis=1)
    return jnp.concatenate([v[:, :LANES], low], axis=0)


def unfold(v):
    rest = STEPS - LANES
    high = jnp.concatenate([v[GROUP:, :rest], v[GROUP:, rest:]], axis=0)
    return jnp.concatenate([v[:GROUP], high], axis=1)


def groups(v):
    return [v[g * GROUP : (g + 1) * GROUP] for g in range(v.shape[0] // GROUP)]


class Sems:
    def __init__(self):
        self.at = 0

    def take(self, count):
        first = self.at
        self.at += count
        return first


SUBS = 8
WIDE = 4


def reciprocal(v):
    return pl.reciprocal(v, approx=True)


def factor_two(a, b, d):
    ra = reciprocal(a)
    return b * ra, ra, a * reciprocal(a * d - b * b)


def factor_four(s):
    l = [[None] * WIDE for _ in range(WIDE)]
    l[1][0], rd0, rd1 = factor_two(s[0][0], s[1][0], s[1][1])
    c = {}
    for r in (2, 3):
        l[r][0] = s[r][0] * rd0
        c[r] = s[r][1] - l[1][0] * s[r][0]
        l[r][1] = c[r] * rd1

    def left(r, t):
        return s[r][t] - (l[r][0] * s[t][0] + l[r][1] * c[t])

    l[3][2], rd2, rd3 = factor_two(left(2, 2), left(3, 2), left(3, 3))
    return l, (rd0, rd1, rd2, rd3)


def eliminate(l, v):
    v1 = v[1] - l[1][0] * v[0]
    v2 = v[2] - l[2][0] * v[0] - l[2][1] * v1
    v3 = v[3] - l[3][0] * v[0] - l[3][1] * v1 - l[3][2] * v2
    return v[0], v1, v2, v3


def inverse_block(a, services):
    rows = [a[u * SUBS : (u + 1) * SUBS] for u in range(BLOCK // SUBS)]
    shape = (SUBS, BLOCK)
    lane = lax.broadcasted_iota(jnp.int32, shape, 1)
    sub = lax.broadcasted_iota(jnp.int32, shape, 0)
    span = range(WIDE)

    def column(row, k):
        return jnp.broadcast_to(row[:, k : k + 1], shape)

    def entry(col, r):
        return jnp.broadcast_to(col[r % SUBS : r % SUBS + 1], shape)

    s = None
    for k in range(0, BLOCK, WIDE):
        v, first = k // SUBS, k % SUBS
        col = [[column(row, k + b) for row in rows] for b in span]
        if s is None:
            s = [[entry(col[b][v], k + a) for b in range(a + 1)] for a in span]
        after = k + WIDE
        if after < BLOCK:
            row = rows[after // SUBS]
            ahead = [column(row, after + b) for b in span]
            ahead = [[entry(ahead[b], after + a) for b in range(a + 1)] for a in span]
            links = [[entry(col[b][after // SUBS], after + a) for b in span] for a in span]
        inside = (lane >= k) & (lane < k + WIDE)
        top = [
            jnp.where(inside, jnp.where(lane == k + b, 1.0, 0.0), entry(rows[v], first + b))
            for b in span
        ]
        l, rd = factor_four(s)
        if after < BLOCK:
            links = [eliminate(l, link) for link in links]
            scaled = [[link[b] * rd[b] for b in span] for link in links]
            s = [
                [
                    ahead[a][b]
                    - (
                        (scaled[a][0] * links[b][0] + scaled[a][1] * links[b][1])
                        + (scaled[a][2] * links[b][2] + scaled[a][3] * links[b][3])
                    )
                    for b in range(a + 1)
                ]
                for a in span
            ]
        top = eliminate(l, top)
        new = [None] * WIDE
        for a in reversed(span):
            new[a] = rd[a] * top[a]
            for b in range(a + 1, WIDE):
                new[a] = new[a] - l[b][a] * new[b]
        for u in range(len(rows)):
            m = eliminate(l, [col[b][u] for b in span])
            drop = ((m[0] * rd[0]) * top[0] + (m[1] * rd[1]) * top[1]) + ((m[2] * rd[2]) * top[2] + (m[3] * rd[3]) * top[3])
            rows[u] = jnp.where(inside, 0.0, rows[u]) - drop
        for a in span:
            rows[v] = jnp.where(sub == first + a, new[a], rows[v])
        if k % (4 * WIDE) == 3 * WIDE:
            for serve in services:
                serve()
                break
    return jnp.concatenate(rows, axis=0)


def dot32(a, b):
    return jnp.dot(a, b, precision=HIGH, preferred_element_type=F32)


def invert(cap, minv, services):
    blocks = range(STEPS // BLOCK)
    shape = (BLOCK, BLOCK)
    eye = jnp.where(lax.broadcasted_iota(jnp.int32, shape, 0) == lax.broadcasted_iota(jnp.int32, shape, 1), 1.0, 0.0)
    (k00, k11), (k22, k10), (k20, k21) = [
        [cap[r * BLOCK : (r + 1) * BLOCK, :BLOCK], cap[r * BLOCK : (r + 1) * BLOCK, BLOCK:]] for r in blocks
    ]
    a = [[k00 + eye, k10.T, k20.T], [k10, k11 + eye, k21.T], [k20, k21, k22 + eye]]
    for k in blocks:
        inv = inverse_block(a[k][k], services)
        new = [[None] * len(blocks) for _ in blocks]
        new[k][k] = inv
        for s in blocks:
            if s != k:
                new[k][s] = dot32(inv, a[k][s])
        for r in blocks:
            if r != k:
                new[r][k] = -dot32(a[r][k], inv)
                for s in blocks:
                    if s != k:
                        new[r][s] = a[r][s] - dot32(a[r][k], new[k][s])
        a = new
    for r in blocks:
        for s in blocks:
            minv[r * BLOCK : (r + 1) * BLOCK, s * BLOCK : (s + 1) * BLOCK] = a[r][s]


def comm_kernel(
    rates_hbm, targets_hbm, goal_hbm, readout_hbm, corr_hbm, rec_hbm,
    scaled, readout_new, left, corr_v, rec_v,
    rates, rates_t, targets, goal, readout, rx,
    g_part, g_mid, g_relay, g_sum, g_x, g_zrelay, g_zsum, g_z, g_piece, g_all, g_hi, g_lo,
    e_part, e_hold, e_aim, e_mid, e_relay, e_sum, e_x, e_low, e_z,
    kpart, krow, ksum, kz, kmid, kx, cap, minv,
    load_sem, send_sem, recv_sem,
):
    i = lax.axis_index("row")
    j = lax.axis_index("col")
    y, zl, c = i // 4, (i // 2) % 2, i % 2
    x, zh = j // 4, j % 4
    sems = Sems()

    def quarter(q):
        return aligned((q % 4) * QUARTER, QUARTER)

    def remote(src, dst, at, dev, land=None):
        return pltpu.make_async_remote_copy(
            src_ref=src, dst_ref=dst, send_sem=send_sem.at[at], recv_sem=recv_sem.at[at if land is None else land],
            device_id=dev, device_id_type=MESH,
        )

    def load(src, dst, at):
        copy = pltpu.make_async_copy(src, dst, load_sem.at[at])
        copy.start()
        return copy

    rates_load = load(rates_hbm, rates, 8)
    rec_loads, corr_loads = {}, {}

    def load_quarter(d, loads, src, dst, at):
        part = quarter(x + d)
        loads[d] = load(src.at[part], dst.at[part], at + d)

    load_quarter(2, corr_loads, corr_hbm, corr_v, 4)

    barrier = pltpu.get_barrier_semaphore()

    def greet(dev):
        pl.semaphore_signal(barrier, inc=1, device_id=dev, device_id_type=MESH)

    for d in range(1, 16):
        greet({"row": (i + d) % 16})

    for d in range(1, 4):
        greet({"col": x * 4 + (zh + d) % 4})
        greet({"col": ((x + d) % 4) * 4 + zh})

    @pl.when(i != j)
    def _():
        greet({"row": j, "col": i})

    for z in range(2):
        source = y * 4 + 2 * c + z

        @pl.when((i != j) | (source != j))
        def _():
            greet({"row": j, "col": source})

    for d in (1, 3, 0):
        load_quarter(d, corr_loads, corr_hbm, corr_v, 4)
    for d in (2, 1, 3, 0):
        load_quarter(d, rec_loads, rec_hbm, rec_v, 0)
    readout_load = load(readout_hbm, readout, 9)
    targets_load = load(targets_hbm, targets, 10)
    goal_load = load(goal_hbm, goal, 11)

    rates_load.wait()
    rates_t[...] = rates[...].T

    def z_dev(d):
        return {"col": x * 4 + (zh + d) % 4}

    def x_dev(d):
        return {"col": ((x + d) % 4) * 4 + zh}

    def y_dev(d):
        return {"row": ((y + d) % 4) * 4 + zl * 2 + c}

    class RingSum:
        def __init__(self, part, hold, relay, total, landed, sent, dev):
            self.hold, self.relay, self.total, self.landed = hold, relay, total, landed
            at = sems.take(3)
            self.copies = [
                remote(part(0, 0), relay.at[0], at, dev(1), at),
                remote(part(0, 1), relay.at[1], at, dev(3), at + 1),
                remote(part(1, 1), landed.at[0], at, dev(1), at + 2),
                remote(part(2, 0), landed.at[1], at, dev(3), at + 2),
                remote(total.at[0], landed.at[2], at, dev(1), at + 2),
                remote(total.at[1], landed.at[3], at, dev(3), at + 2),
            ]
            self.arrived = remote(landed, landed, at, dev(1), at + 2)
            self.sent = remote(sent, sent, at, dev(1))

        def start(self, *which):
            for k in which:
                self.copies[k].start()

        def forward(self):
            for k in range(2):
                self.copies[k].wait_recv()
                self.total[k] = (self.hold(k) + self.relay[k].astype(F32)).astype(self.total.dtype)
                self.copies[4 + k].start()

        def finish(self):
            self.arrived.wait_recv()
            got = [self.landed[k].astype(F32) for k in range(4)]
            return got[2] + got[1], got[0] + got[3]

        def wait_sends(self):
            self.sent.wait_send()

    class Ring:
        def __init__(self, block, me, dev, four, six):
            self.block, self.me, self.dev = block, me, dev
            self.at = sems.take(3)
            self.arrived = remote(four, four, self.at, dev(1), self.at + 2)
            self.sent = remote(six, six, self.at, dev(1))

        def copy(self, k, owner):
            block = self.block((0, 1, 1, 0, 0, 1)[k], owner % 4)
            land = self.at + (0, 2, 1, 2, 2, 2)[k]
            return remote(block, block, self.at, self.dev((1, 1, 3, 3, 1, 3)[k]), land)

        def start(self):
            for k in (0, 2, 1, 3):
                self.copy(k, self.me).start()

        def forward(self):
            self.copy(0, self.me + 3).wait_recv()
            self.copy(4, self.me + 3).start()
            self.copy(2, self.me + 1).wait_recv()
            self.copy(5, self.me + 1).start()

        def finish(self):
            self.arrived.wait_recv()

        def wait_sends(self):
            self.sent.wait_send()

    def prod_quarter(d, out):
        corr_loads[d].wait()
        hi, lo = split2(corr_v[quarter(x + d), :])
        value = jnp.dot(hi, rates_t[...], preferred_element_type=F32) + jnp.dot(
            lo, rates_t[...], preferred_element_type=F32
        )
        for g, part in enumerate(groups(value)):
            out[g] = fold(part)

    def drive_quarter(d):
        rec_loads[d].wait()
        value = jnp.dot(rec_v[quarter(x + d), :], rates_t[...], preferred_element_type=F32)
        return [fold(part) for part in groups(value)]

    pl.semaphore_wait(barrier, jnp.where(i == j, jnp.where(zl == c, 22, 23), 24))
    r_t = sems.take(1)
    r_src = rates.at[:, quarter(y)]

    @pl.when(i != j)
    def _():
        remote(r_src, rx, r_t, {"row": j, "col": i}).start()

    @pl.when(i == j)
    def _():
        pltpu.make_async_copy(r_src, rx, recv_sem.at[r_t]).start()

    def pairs(part):
        return lambda which, half: part.at[which, pl.ds(2 * half, 2)]

    g_ring = RingSum(
        pairs(g_part), lambda k: g_part[1, :2] if k == 0 else g_part[2, 2:], g_relay, g_sum, g_x, g_part, x_dev
    )
    prod_quarter(2, g_part.at[0])
    g_ring.start(0, 1)
    prod_quarter(1, g_part.at[1])
    g_ring.start(2)
    prod_quarter(3, g_part.at[2])
    g_ring.start(3)
    prod_quarter(0, g_mid)

    e_ring = RingSum(pairs(e_part), lambda k: e_hold[k], e_relay, e_sum, e_x, e_part, x_dev)
    for g, part in enumerate(drive_quarter(2)):
        e_part[0, g] = part.astype(BF)
    g_ring.forward()
    e_ring.start(0, 1)
    for g, part in enumerate(drive_quarter(1)):
        if g < 2:
            e_hold[0, g] = part
        else:
            e_part[1, g] = part.astype(BF)
    e_ring.start(2)
    for g, part in enumerate(drive_quarter(3)):
        if g < 2:
            e_part[2, g] = part.astype(BF)
        else:
            e_hold[1, g - 2] = part
    e_ring.start(3)

    readout_load.wait()
    guess = sum(
        jnp.dot(term, rates_t[...], preferred_element_type=F32) for term in split2(readout[...] * (1.0 / 16.0))
    )
    kpart[3 * BLOCK : 3 * BLOCK + OUTS, :] = guess[:, :LANES]
    kpart[3 * BLOCK + OUTS :, :] = jnp.concatenate([guess[:, LANES:], guess[:, LANES:]], axis=1)

    for g, part in enumerate(drive_quarter(0)):
        e_mid[g] = part
    targets_load.wait()
    aims = targets[:, quarter(x)].T.astype(F32)
    for g, part in enumerate(groups(aims)):
        e_aim[g] = fold(part)

    @pl.when(i != j)
    def _():
        remote(r_src, rx, r_t, {"row": j, "col": i}).wait_recv()

    @pl.when(i == j)
    def _():
        pltpu.make_async_copy(r_src, rx, recv_sem.at[r_t]).wait()

    got = g_ring.finish()
    for k in range(2):
        g_mid[2 * k : 2 * k + 2] = g_mid[2 * k : 2 * k + 2] + got[k]

    def g_slice(which, half):
        return g_mid.at[(zh + (2, 1, 3)[which]) % 4, pl.ds(half * (FOLDED // 2), FOLDED // 2)]

    z_ring = RingSum(g_slice, lambda k: g_slice(k + 1, k)[...], g_zrelay, g_zsum, g_z, g_part.at[0, pl.ds(0, 3)], z_dev)
    z_ring.start(0, 1, 2, 3)

    whole = sum(
        jnp.dot(rx[...], term, preferred_element_type=F32)
        for term in split2(jnp.concatenate([unfold(g_mid[g]) for g in range(4)], axis=0))
    )
    kb = [[whole[r * BLOCK : (r + 1) * BLOCK, s * BLOCK : (s + 1) * BLOCK] for s in range(3)] for r in range(3)]
    kpart[:BLOCK, :] = jnp.concatenate([kb[0][0], kb[1][1]], axis=1)
    kpart[BLOCK : 2 * BLOCK, :] = jnp.concatenate([kb[2][2], kb[1][0]], axis=1)
    kpart[2 * BLOCK : 3 * BLOCK, :] = jnp.concatenate([kb[2][0], kb[2][1]], axis=1)

    e_ring.forward()

    k_r = sems.take(1)

    for d in range(1, 16):
        owner = (i + d) % 16

        @pl.when(owner < OWNERS)
        def _():
            remote(kpart.at[aligned(owner * PIECE, PIECE)], krow.at[d - 1], k_r, {"row": owner}).start()

    z_ring.forward()
    got = e_ring.finish()
    for k in range(2):
        total = e_mid[2 * k : 2 * k + 2] + got[k]
        e_mid[2 * k : 2 * k + 2] = total
        e_low[2 * k : 2 * k + 2] = total.astype(BF)
    e_at = sems.take(1)

    def e_z_copy(d):
        return remote(e_low.at[(zh + d) % 4], e_z.at[d - 1], e_at, z_dev(d))

    for d in range(1, 4):
        e_z_copy(d).start()

    k_x = sems.take(1)
    k_z = sems.take(1)

    @pl.when(i < OWNERS)
    def _():
        remote(krow, krow, k_r, {"row": (i + 1) % 16}).wait_recv()
        acc = kpart[aligned(i * PIECE, PIECE), :]
        for d in range(15):
            acc = acc + krow[d]
        ksum[...] = acc
        for d in range(1, 4):
            remote(ksum, kx.at[d - 1], k_x, x_dev(d)).start()

    got = z_ring.finish()
    for k in range(2):
        part = pl.ds(k * (FOLDED // 2), FOLDED // 2)
        g_piece[part, :] = g_mid[zh, part, :] + got[k]

    @pl.when(i < OWNERS)
    def _():
        remote(kx, kx, k_x, x_dev(1)).wait_recv()
        kmid[...] = ksum[...] + kx[0] + kx[1] + kx[2]
        for d in range(1, 4):
            remote(kmid, kz.at[d - 1], k_z, z_dev(d)).start()

    own = aligned(x * QUARTER + zh * GROUP, GROUP)
    s_t = sems.take(2)

    def swap_each(act_remote, act_local):
        for e in range(2):
            dst = g_all.at[x, zh]
            row = x * 4 + e * 2 + zh // 2

            @pl.when((i != j) | (row != i))
            def _():
                act_remote(remote(g_piece, dst, s_t + e, {"row": row, "col": i}, s_t + zh % 2))

            if act_local is not None:

                @pl.when((i == j) & (row == i))
                def _():
                    act_local(pltpu.make_async_copy(g_piece, dst, recv_sem.at[s_t + zh % 2]))

    swap_each(lambda copy: copy.start(), lambda copy: copy.start())
    left[own, STEPS:] = unfold(g_piece[...]).astype(BF)

    remote(e_z, e_z, e_at, z_dev(1)).wait_recv()
    total = e_mid[zh] - e_aim[zh]
    for d in range(3):
        total = total + e_z[d].astype(F32)
    left[own, :STEPS] = unfold(total).astype(BF)
    lz_ring = Ring(
        lambda half, owner: left.at[aligned(x * QUARTER + owner * GROUP + half * (GROUP // 2), GROUP // 2)], zh, z_dev,
        left.at[pl.ds(0, 2 * GROUP)], left.at[pl.ds(0, 3 * GROUP)],
    )
    lz_ring.start()

    k_g = sems.take(1)
    own_rows = aligned(i * PIECE, PIECE)

    @pl.when(i < OWNERS)
    def _():
        remote(kz, kz, k_z, z_dev(1)).wait_recv()
        cap[own_rows, :] = kmid[...] + kz[0] + kz[1] + kz[2]
        for d in range(1, 16):
            remote(cap.at[own_rows], cap.at[own_rows], k_g, {"row": (i + d) % 16}).start()

    for z in range(2):
        source = y * 4 + 2 * c + z
        dst = g_all.at[y, 2 * c + z]

        @pl.when((i != j) | (source != j))
        def _():
            remote(g_piece, dst, s_t, {"row": j, "col": source}, s_t + z).wait_recv()

        @pl.when((i == j) & (source == j))
        def _():
            pltpu.make_async_copy(g_piece, dst, recv_sem.at[s_t + z]).wait()

    y_ring = Ring(lambda half, owner: g_all.at[owner, 2 * c + half], y, y_dev, g_all.at[0], g_all.at[pl.ds(0, 3), pl.ds(0, 2)])
    y_ring.start()
    lz_ring.forward()
    l_ring = Ring(
        lambda half, owner: left.at[aligned(owner * QUARTER + half * LANES, LANES)], x, x_dev,
        left.at[pl.ds(0, 2 * QUARTER)], left.at[pl.ds(0, 3 * QUARTER)],
    )

    others = cap.at[pl.ds(0, PACKED - PIECE)]

    @pl.when(i < OWNERS)
    def _():
        remote(others, others, k_g, {"row": (i + 1) % 16}).wait_recv()

    @pl.when(i >= OWNERS)
    def _():
        remote(cap, cap, k_g, {"row": (i + 1) % 16}).wait_recv()

    def rest():
        pass

    a_c = sems.take(1)
    sibling = {"row": i + 1 - 2 * c}
    mine = g_all.at[:, pl.ds(2 * c, 2)]
    theirs = g_all.at[:, pl.ds(2 - 2 * c, 2)]

    def serve_left():
        y_ring.forward()
        lz_ring.finish()
        l_ring.start()

    def serve_y():
        y_ring.finish()
        remote(mine, mine, a_c, sibling).start()

    def serve_core():
        remote(theirs, theirs, a_c, sibling).wait_recv()

        @pl.loop(0, 4)
        def _(q):
            for g in range(4):
                hi, lo = split2(unfold(g_all[q, g]))
                rows = aligned(q * QUARTER + g * GROUP, GROUP)
                g_hi[rows, :] = hi
                g_lo[rows, :] = lo

    invert(cap, minv, iter((serve_left, rest, rest, rest, rest, rest, serve_y, l_ring.forward)))
    serve_core()

    m_hi, m_lo = split2(minv[...])
    value = sum(
        lax.dot_general(m, g, NT, preferred_element_type=F32)
        for m, g in ((m_hi, g_lo[...]), (m_lo, g_hi[...]), (m_hi, g_hi[...]))
    )
    scaled[...] = value.astype(BF)
    goal_load.wait()
    guess = jnp.concatenate([cap[3 * BLOCK : 3 * BLOCK + OUTS, :], cap[3 * BLOCK + OUTS :, : STEPS - LANES]], axis=1)
    readout_new[...] = readout[...] - dot32(guess - goal[...], value)
    l_ring.finish()

    @pl.when(i != j)
    def _():
        remote(r_src, rx, r_t, {"row": j, "col": i}).wait_send()

    swap_each(lambda copy: copy.wait_send(), None)
    remote(e_z, e_z, e_at, z_dev(1)).wait_send()
    for ring in (g_ring, e_ring, z_ring, lz_ring, y_ring, l_ring):
        ring.wait_sends()

    some = kpart.at[pl.ds(0, PACKED - PIECE)]

    @pl.when(i < OWNERS)
    def _():
        remote(some, some, k_r, {"row": (i + 1) % 16}).wait_send()
        remote(kx, kx, k_x, x_dev(1)).wait_send()
        remote(kz, kz, k_z, z_dev(1)).wait_send()
        remote(krow, krow, k_g, {"row": (i + 1) % 16}).wait_send()

    @pl.when(i >= OWNERS)
    def _():
        remote(kpart, kpart, k_r, {"row": (i + 1) % 16}).wait_send()

    remote(mine, mine, a_c, sibling).wait_send()


N_SEMS = 96


def gather_all(rates, targets, goal, readout, corr, rec):
    hbm = pl.BlockSpec(memory_space=pl.ANY)

    def folded(dtype, *lead):
        return pltpu.VMEM((*lead, FOLDED, LANES), dtype)

    return pl.pallas_call(
        comm_kernel,
        out_shape=[
            jax.ShapeDtypeStruct((STEPS, LOCAL), BF),
            jax.ShapeDtypeStruct((OUTS, LOCAL), F32),
            jax.ShapeDtypeStruct((LOCAL, 2 * STEPS), BF),
            jax.ShapeDtypeStruct((LOCAL, LOCAL), F32),
            jax.ShapeDtypeStruct((LOCAL, LOCAL), BF),
        ],
        in_specs=[hbm] * 6,
        out_specs=[pl.BlockSpec(memory_space=pltpu.VMEM)] * 5,
        scratch_shapes=[
            pltpu.VMEM((STEPS, LOCAL), BF),
            pltpu.VMEM((LOCAL, STEPS), BF),
            pltpu.VMEM((STEPS, LOCAL), BF),
            pltpu.VMEM((OUTS, STEPS), F32),
            pltpu.VMEM((OUTS, LOCAL), F32),
            pltpu.VMEM((STEPS, QUARTER), BF),
            folded(F32, 3, 4),
            folded(F32, 4),
            folded(F32, 2, 2),
            folded(F32, 2, 2),
            folded(F32, 4, 2),
            pltpu.VMEM((2, FOLDED // 2, LANES), F32),
            pltpu.VMEM((2, FOLDED // 2, LANES), F32),
            pltpu.VMEM((4, FOLDED // 2, LANES), F32),
            folded(F32),
            folded(F32, 4, 4),
            pltpu.VMEM((LOCAL, STEPS), BF),
            pltpu.VMEM((LOCAL, STEPS), BF),
            folded(BF, 3, 4),
            folded(F32, 2, 2),
            folded(F32, 4),
            folded(F32, 4),
            folded(BF, 2, 2),
            folded(BF, 2, 2),
            folded(BF, 4, 2),
            folded(BF, 4),
            folded(BF, 3),
            pltpu.VMEM((PACKED, LANES), F32),
            pltpu.VMEM((15, PIECE, LANES), F32),
            pltpu.VMEM((PIECE, LANES), F32),
            pltpu.VMEM((3, PIECE, LANES), F32),
            pltpu.VMEM((PIECE, LANES), F32),
            pltpu.VMEM((3, PIECE, LANES), F32),
            pltpu.VMEM((PACKED, LANES), F32),
            pltpu.VMEM((STEPS, STEPS), F32),
            pltpu.SemaphoreType.DMA((12,)),
            pltpu.SemaphoreType.DMA((N_SEMS,)),
            pltpu.SemaphoreType.DMA((N_SEMS,)),
        ],
        compiler_params=pltpu.CompilerParams(
            collective_id=0, has_side_effects=True, vmem_limit_bytes=VMEM_LIMIT
        ),
        name="exchange",
    )(rates, targets, goal, readout, corr, rec)


TILE = 256


def update_kernel(scaled, readout_new, left, corr, rec, corr_out, rec_out, readout_out):
    rows = aligned(pl.program_id(0) * TILE, TILE)
    drop = jnp.dot(left[rows, STEPS:], scaled[...], preferred_element_type=F32)
    corr_out[...] = corr[rows, :] - drop
    drop = jnp.dot(left[rows, :STEPS], scaled[...], preferred_element_type=F32)
    rec_out[...] = (rec[rows, :].astype(F32) - drop).astype(BF)
    readout_out[...] = readout_new[...]


def update(scaled, readout_new, left, corr, rec):
    rows = pl.BlockSpec((TILE, LOCAL), lambda g: (g, 0))
    return pl.pallas_call(
        update_kernel,
        grid=(LOCAL // TILE,),
        out_shape=[
            jax.ShapeDtypeStruct((LOCAL, LOCAL), F32),
            jax.ShapeDtypeStruct((LOCAL, LOCAL), BF),
            jax.ShapeDtypeStruct((OUTS, LOCAL), F32),
        ],
        in_specs=[pl.BlockSpec(memory_space=pltpu.VMEM)] * 5,
        out_specs=[rows, rows, pl.BlockSpec((OUTS, LOCAL), lambda g: (0, 0))],
        compiler_params=pltpu.CompilerParams(vmem_limit_bytes=VMEM_LIMIT),
        name="update",
    )(scaled, readout_new, left, corr, rec)


def on_device(*args):
    rates, targets, goal, corr, rec, readout = (pltpu.with_memory_space_constraint(v, pltpu.HBM) for v in args)
    return tuple(update(*gather_all(rates, targets, goal, readout, corr, rec)))


def solution(mesh):
    placed = (P(None, "col"), P(None, "row"), P(), P("row", "col"), P("row", "col"), P(None, "col"))
    return jax.shard_map(
        on_device,
        mesh=mesh,
        in_specs=placed,
        out_specs=(P("row", "col"), P("row", "col"), P(None, "col")),
        check_vma=False,
    )
```

```python
import functools

import jax
import jax.numpy as jnp
from jax import lax
from jax.experimental import pallas as pl
from jax.experimental.pallas import tpu as pltpu
from jax.sharding import PartitionSpec as P

MESH = pl.DeviceIdType.MESH
BF, F32 = jnp.bfloat16, jnp.float32
HIGH = lax.Precision.HIGHEST

STEPS = 192
LOCAL = 1024
OUTS = 16
QUARTER = 256
GROUP = 64
PIECE = 16
BLOCK = 64
PACKED = 3 * BLOCK + 2 * OUTS
OWNERS = PACKED // PIECE
LANES = 128
FOLDED = GROUP * STEPS // LANES
NT = (((1,), (1,)), ((), ()))
VMEM_LIMIT = 32 * 1024 * 1024


def split2(x):
    hi = x.astype(BF)
    return hi, (x - hi.astype(F32)).astype(BF)


def aligned(start, size):
    return pl.ds(pl.multiple_of(start, size), size)


def fold(v):
    low = jnp.concatenate([v[: GROUP // 2, LANES:], v[GROUP // 2 :, LANES:]], axis=1)
    return jnp.concatenate([v[:, :LANES], low], axis=0)


def unfold(v):
    rest = STEPS - LANES
    high = jnp.concatenate([v[GROUP:, :rest], v[GROUP:, rest:]], axis=0)
    return jnp.concatenate([v[:GROUP], high], axis=1)


def groups(v):
    return [v[g * GROUP : (g + 1) * GROUP] for g in range(v.shape[0] // GROUP)]


class Sems:
    def __init__(self):
        self.at = 0

    def take(self, count):
        first = self.at
        self.at += count
        return first


SUBS = 8
WIDE = 4


def reciprocal(v):
    return pl.reciprocal(v, approx=True)


def factor_two(a, b, d):
    ra = reciprocal(a)
    return b * ra, ra, a * reciprocal(a * d - b * b)


def factor_four(s):
    l = [[None] * WIDE for _ in range(WIDE)]
    l[1][0], rd0, rd1 = factor_two(s[0][0], s[1][0], s[1][1])
    c = {}
    for r in (2, 3):
        l[r][0] = s[r][0] * rd0
        c[r] = s[r][1] - l[1][0] * s[r][0]
        l[r][1] = c[r] * rd1

    def left(r, t):
        return s[r][t] - (l[r][0] * s[t][0] + l[r][1] * c[t])

    l[3][2], rd2, rd3 = factor_two(left(2, 2), left(3, 2), left(3, 3))
    return l, (rd0, rd1, rd2, rd3)


def eliminate(l, v):
    v1 = v[1] - l[1][0] * v[0]
    v2 = v[2] - l[2][0] * v[0] - l[2][1] * v1
    v3 = v[3] - l[3][0] * v[0] - l[3][1] * v1 - l[3][2] * v2
    return v[0], v1, v2, v3


def inverse_block(a, services):
    rows = [a[u * SUBS : (u + 1) * SUBS] for u in range(BLOCK // SUBS)]
    shape = (SUBS, BLOCK)
    lane = lax.broadcasted_iota(jnp.int32, shape, 1)
    sub = lax.broadcasted_iota(jnp.int32, shape, 0)
    span = range(WIDE)

    def column(row, k):
        return jnp.broadcast_to(row[:, k : k + 1], shape)

    def entry(col, r):
        return jnp.broadcast_to(col[r % SUBS : r % SUBS + 1], shape)

    s = None
    for k in range(0, BLOCK, WIDE):
        v, first = k // SUBS, k % SUBS
        col = [[column(row, k + b) for row in rows] for b in span]
        if s is None:
            s = [[entry(col[b][v], k + a) for b in range(a + 1)] for a in span]
        after = k + WIDE
        if after < BLOCK:
            row = rows[after // SUBS]
            ahead = [column(row, after + b) for b in span]
            ahead = [[entry(ahead[b], after + a) for b in range(a + 1)] for a in span]
            links = [[entry(col[b][after // SUBS], after + a) for b in span] for a in span]
        inside = (lane >= k) & (lane < k + WIDE)
        top = [
            jnp.where(inside, jnp.where(lane == k + b, 1.0, 0.0), entry(rows[v], first + b))
            for b in span
        ]
        l, rd = factor_four(s)
        if after < BLOCK:
            links = [eliminate(l, link) for link in links]
            scaled = [[link[b] * rd[b] for b in span] for link in links]
            s = [
                [
                    ahead[a][b]
                    - (
                        (scaled[a][0] * links[b][0] + scaled[a][1] * links[b][1])
                        + (scaled[a][2] * links[b][2] + scaled[a][3] * links[b][3])
                    )
                    for b in range(a + 1)
                ]
                for a in span
            ]
        top = eliminate(l, top)
        new = [None] * WIDE
        for a in reversed(span):
            new[a] = rd[a] * top[a]
            for b in range(a + 1, WIDE):
                new[a] = new[a] - l[b][a] * new[b]
        for u in range(len(rows)):
            m = eliminate(l, [col[b][u] for b in span])
            drop = ((m[0] * rd[0]) * top[0] + (m[1] * rd[1]) * top[1]) + ((m[2] * rd[2]) * top[2] + (m[3] * rd[3]) * top[3])
            rows[u] = jnp.where(inside, 0.0, rows[u]) - drop
        for a in span:
            rows[v] = jnp.where(sub == first + a, new[a], rows[v])
        if k % (4 * WIDE) == 3 * WIDE:
            for serve in services:
                serve()
                break
    return jnp.concatenate(rows, axis=0)


def dot32(a, b):
    return jnp.dot(a, b, precision=HIGH, preferred_element_type=F32)


def invert(cap, minv, services):
    count = STEPS // BLOCK

    def at(r):
        return pl.ds(r * BLOCK, BLOCK)

    (k00, k11), (k22, k10), (k20, k21) = [
        [cap[at(r), :BLOCK], cap[at(r), BLOCK:]] for r in range(count)
    ]
    minv[at(0), :] = jnp.concatenate([k00, k10.T, k20.T], axis=1)
    minv[at(1), :] = jnp.concatenate([k10, k11, k21.T], axis=1)
    minv[at(2), :] = jnp.concatenate([k20, k21, k22], axis=1)
    shape = (STEPS, STEPS)
    lane = lax.broadcasted_iota(jnp.int32, shape, 1)
    minv[...] += jnp.where(lax.broadcasted_iota(jnp.int32, shape, 0) == lane, 1.0, 0.0)
    lane1 = lax.broadcasted_iota(jnp.int32, (BLOCK, STEPS), 1)
    sub1 = lax.broadcasted_iota(jnp.int32, (BLOCK, STEPS), 0)
    for k in range(count):
        first, last = k * BLOCK, (k + 1) * BLOCK
        inv = inverse_block(minv[at(k), first:last], services)
        inside = (lane1 >= first) & (lane1 < last)
        row = jnp.where(inside, jnp.where(lane1 - first == sub1, 1.0, 0.0), minv[at(k), :])
        new = dot32(inv, row)
        drop = dot32(minv[:, first:last], new)
        minv[...] = jnp.where((lane >= first) & (lane < last), 0.0, minv[...]) - drop
        minv[at(k), :] = new


def comm_kernel(
    rates_hbm, targets_hbm, goal_hbm, readout_hbm, corr_hbm, rec_hbm,
    scaled, readout_new, left, corr_v, rec_v,
    rates, rates_t, targets, goal, readout, rx,
    g_part, g_mid, g_relay, g_sum, g_x, g_zrelay, g_zsum, g_z, g_piece, g_all, g_hi, g_lo,
    e_part, e_hold, e_aim, e_mid, e_relay, e_sum, e_x, e_low, e_z,
    kpart, krow, ksum, kz, kmid, kx, cap, minv,
    load_sem, send_sem, recv_sem,
):
    i = lax.axis_index("row")
    j = lax.axis_index("col")
    y, zl, c = i // 4, (i // 2) % 2, i % 2
    x, zh = j // 4, j % 4
    sems = Sems()

    def quarter(q):
        return aligned((q % 4) * QUARTER, QUARTER)

    def remote(src, dst, at, dev, land=None):
        return pltpu.make_async_remote_copy(
            src_ref=src, dst_ref=dst, send_sem=send_sem.at[at], recv_sem=recv_sem.at[at if land is None else land],
            device_id=dev, device_id_type=MESH,
        )

    def load(src, dst, at):
        copy = pltpu.make_async_copy(src, dst, load_sem.at[at])
        copy.start()
        return copy

    rates_load = load(rates_hbm, rates, 8)
    rec_loads, corr_loads = {}, {}

    def load_quarter(d, loads, src, dst, at):
        part = quarter(x + d)
        loads[d] = load(src.at[part], dst.at[part], at + d)

    load_quarter(2, corr_loads, corr_hbm, corr_v, 4)

    barrier = pltpu.get_barrier_semaphore()

    def greet(dev):
        pl.semaphore_signal(barrier, inc=1, device_id=dev, device_id_type=MESH)

    for d in range(1, 16):
        greet({"row": (i + d) % 16})

    for d in range(1, 4):
        greet({"col": x * 4 + (zh + d) % 4})
        greet({"col": ((x + d) % 4) * 4 + zh})

    @pl.when(i != j)
    def _():
        greet({"row": j, "col": i})

    for z in range(2):
        source = y * 4 + 2 * c + z

        @pl.when((i != j) | (source != j))
        def _():
            greet({"row": j, "col": source})

    for d in (1, 3, 0):
        load_quarter(d, corr_loads, corr_hbm, corr_v, 4)
    for d in (2, 1, 3, 0):
        load_quarter(d, rec_loads, rec_hbm, rec_v, 0)
    readout_load = load(readout_hbm, readout, 9)
    targets_load = load(targets_hbm, targets, 10)
    goal_load = load(goal_hbm, goal, 11)

    rates_load.wait()
    rates_t[...] = rates[...].T

    def z_dev(d):
        return {"col": x * 4 + (zh + d) % 4}

    def x_dev(d):
        return {"col": ((x + d) % 4) * 4 + zh}

    def y_dev(d):
        return {"row": ((y + d) % 4) * 4 + zl * 2 + c}

    class RingSum:
        def __init__(self, part, hold, relay, total, landed, sent, dev):
            self.hold, self.relay, self.total, self.landed = hold, relay, total, landed
            at = sems.take(3)
            self.copies = [
                remote(part(0, 0), relay.at[0], at, dev(1), at),
                remote(part(0, 1), relay.at[1], at, dev(3), at + 1),
                remote(part(1, 1), landed.at[0], at, dev(1), at + 2),
                remote(part(2, 0), landed.at[1], at, dev(3), at + 2),
                remote(total.at[0], landed.at[2], at, dev(1), at + 2),
                remote(total.at[1], landed.at[3], at, dev(3), at + 2),
            ]
            self.arrived = remote(landed, landed, at, dev(1), at + 2)
            self.sent = remote(sent, sent, at, dev(1))

        def start(self, *which):
            for k in which:
                self.copies[k].start()

        def forward(self):
            for k in range(2):
                self.copies[k].wait_recv()
                self.total[k] = (self.hold(k) + self.relay[k].astype(F32)).astype(self.total.dtype)
                self.copies[4 + k].start()

        def finish(self):
            self.arrived.wait_recv()
            got = [self.landed[k].astype(F32) for k in range(4)]
            return got[2] + got[1], got[0] + got[3]

        def wait_sends(self):
            self.sent.wait_send()

    class Ring:
        def __init__(self, block, me, dev, four, six):
            self.block, self.me, self.dev = block, me, dev
            self.at = sems.take(3)
            self.arrived = remote(four, four, self.at, dev(1), self.at + 2)
            self.sent = remote(six, six, self.at, dev(1))

        def copy(self, k, owner):
            block = self.block((0, 1, 1, 0, 0, 1)[k], owner % 4)
            land = self.at + (0, 2, 1, 2, 2, 2)[k]
            return remote(block, block, self.at, self.dev((1, 1, 3, 3, 1, 3)[k]), land)

        def start(self):
            for k in (0, 2, 1, 3):
                self.copy(k, self.me).start()

        def forward(self):
            self.copy(0, self.me + 3).wait_recv()
            self.copy(4, self.me + 3).start()
            self.copy(2, self.me + 1).wait_recv()
            self.copy(5, self.me + 1).start()

        def finish(self):
            self.arrived.wait_recv()

        def wait_sends(self):
            self.sent.wait_send()

    def prod_quarter(d, out):
        corr_loads[d].wait()
        hi, lo = split2(corr_v[quarter(x + d), :])
        value = jnp.dot(hi, rates_t[...], preferred_element_type=F32) + jnp.dot(
            lo, rates_t[...], preferred_element_type=F32
        )
        for g, part in enumerate(groups(value)):
            out[g] = fold(part)

    def drive_quarter(d):
        rec_loads[d].wait()
        value = jnp.dot(rec_v[quarter(x + d), :], rates_t[...], preferred_element_type=F32)
        return [fold(part) for part in groups(value)]

    pl.semaphore_wait(barrier, jnp.where(i == j, jnp.where(zl == c, 22, 23), 24))
    r_t = sems.take(1)
    r_src = rates.at[:, quarter(y)]

    @pl.when(i != j)
    def _():
        remote(r_src, rx, r_t, {"row": j, "col": i}).start()

    @pl.when(i == j)
    def _():
        pltpu.make_async_copy(r_src, rx, recv_sem.at[r_t]).start()

    def pairs(part):
        return lambda which, half: part.at[which, pl.ds(2 * half, 2)]

    g_ring = RingSum(
        pairs(g_part), lambda k: g_part[1, :2] if k == 0 else g_part[2, 2:], g_relay, g_sum, g_x, g_part, x_dev
    )
    prod_quarter(2, g_part.at[0])
    g_ring.start(0, 1)
    prod_quarter(1, g_part.at[1])
    g_ring.start(2)
    prod_quarter(3, g_part.at[2])
    g_ring.start(3)
    prod_quarter(0, g_mid)

    e_ring = RingSum(pairs(e_part), lambda k: e_hold[k], e_relay, e_sum, e_x, e_part, x_dev)
    for g, part in enumerate(drive_quarter(2)):
        e_part[0, g] = part.astype(BF)
    g_ring.forward()
    e_ring.start(0, 1)
    for g, part in enumerate(drive_quarter(1)):
        if g < 2:
            e_hold[0, g] = part
        else:
            e_part[1, g] = part.astype(BF)
    e_ring.start(2)
    for g, part in enumerate(drive_quarter(3)):
        if g < 2:
            e_part[2, g] = part.astype(BF)
        else:
            e_hold[1, g - 2] = part
    e_ring.start(3)

    readout_load.wait()
    guess = sum(
        jnp.dot(term, rates_t[...], preferred_element_type=F32) for term in split2(readout[...] * (1.0 / 16.0))
    )
    kpart[3 * BLOCK : 3 * BLOCK + OUTS, :] = guess[:, :LANES]
    kpart[3 * BLOCK + OUTS :, :] = jnp.concatenate([guess[:, LANES:], guess[:, LANES:]], axis=1)

    for g, part in enumerate(drive_quarter(0)):
        e_mid[g] = part
    targets_load.wait()
    aims = targets[:, quarter(x)].T.astype(F32)
    for g, part in enumerate(groups(aims)):
        e_aim[g] = fold(part)

    @pl.when(i != j)
    def _():
        remote(r_src, rx, r_t, {"row": j, "col": i}).wait_recv()

    @pl.when(i == j)
    def _():
        pltpu.make_async_copy(r_src, rx, recv_sem.at[r_t]).wait()

    got = g_ring.finish()
    for k in range(2):
        g_mid[2 * k : 2 * k + 2] = g_mid[2 * k : 2 * k + 2] + got[k]

    def g_slice(which, half):
        return g_mid.at[(zh + (2, 1, 3)[which]) % 4, pl.ds(half * (FOLDED // 2), FOLDED // 2)]

    z_ring = RingSum(g_slice, lambda k: g_slice(k + 1, k)[...], g_zrelay, g_zsum, g_z, g_part.at[0, pl.ds(0, 3)], z_dev)
    z_ring.start(0, 1, 2, 3)

    whole = sum(
        jnp.dot(rx[...], term, preferred_element_type=F32)
        for term in split2(jnp.concatenate([unfold(g_mid[g]) for g in range(4)], axis=0))
    )
    kb = [[whole[r * BLOCK : (r + 1) * BLOCK, s * BLOCK : (s + 1) * BLOCK] for s in range(3)] for r in range(3)]
    kpart[:BLOCK, :] = jnp.concatenate([kb[0][0], kb[1][1]], axis=1)
    kpart[BLOCK : 2 * BLOCK, :] = jnp.concatenate([kb[2][2], kb[1][0]], axis=1)
    kpart[2 * BLOCK : 3 * BLOCK, :] = jnp.concatenate([kb[2][0], kb[2][1]], axis=1)

    e_ring.forward()

    k_r = sems.take(1)

    for d in range(1, 16):
        owner = (i + d) % 16

        @pl.when(owner < OWNERS)
        def _():
            remote(kpart.at[aligned(owner * PIECE, PIECE)], krow.at[d - 1], k_r, {"row": owner}).start()

    z_ring.forward()
    k_x = sems.take(1)
    k_z = sems.take(1)

    @pl.when(i < OWNERS)
    def _():
        remote(krow, krow, k_r, {"row": (i + 1) % 16}).wait_recv()
        acc = kpart[aligned(i * PIECE, PIECE), :]
        for d in range(15):
            acc = acc + krow[d]
        ksum[...] = acc
        for d in range(1, 4):
            remote(ksum, kx.at[d - 1], k_x, x_dev(d)).start()

    got = e_ring.finish()
    for k in range(2):
        total = e_mid[2 * k : 2 * k + 2] + got[k]
        e_mid[2 * k : 2 * k + 2] = total
        e_low[2 * k : 2 * k + 2] = total.astype(BF)
    e_at = sems.take(1)

    def e_z_copy(d):
        return remote(e_low.at[(zh + d) % 4], e_z.at[d - 1], e_at, z_dev(d))

    for d in range(1, 4):
        e_z_copy(d).start()

    @pl.when(i < OWNERS)
    def _():
        remote(kx, kx, k_x, x_dev(1)).wait_recv()
        kmid[...] = ksum[...] + kx[0] + kx[1] + kx[2]
        for d in range(1, 4):
            remote(kmid, kz.at[d - 1], k_z, z_dev(d)).start()

    got = z_ring.finish()
    for k in range(2):
        part = pl.ds(k * (FOLDED // 2), FOLDED // 2)
        g_piece[part, :] = g_mid[zh, part, :] + got[k]
    own = aligned(x * QUARTER + zh * GROUP, GROUP)
    s_t = sems.take(2)

    def swap_each(act_remote, act_local):
        for e in range(2):
            dst = g_all.at[x, zh]
            row = x * 4 + e * 2 + zh // 2

            @pl.when((i != j) | (row != i))
            def _():
                act_remote(remote(g_piece, dst, s_t + e, {"row": row, "col": i}, s_t + zh % 2))

            if act_local is not None:

                @pl.when((i == j) & (row == i))
                def _():
                    act_local(pltpu.make_async_copy(g_piece, dst, recv_sem.at[s_t + zh % 2]))

    swap_each(lambda copy: copy.start(), lambda copy: copy.start())
    left[own, STEPS:] = unfold(g_piece[...]).astype(BF)

    remote(e_z, e_z, e_at, z_dev(1)).wait_recv()
    total = e_mid[zh] - e_aim[zh]
    for d in range(3):
        total = total + e_z[d].astype(F32)
    left[own, :STEPS] = unfold(total).astype(BF)
    lz_ring = Ring(
        lambda half, owner: left.at[aligned(x * QUARTER + owner * GROUP + half * (GROUP // 2), GROUP // 2)], zh, z_dev,
        left.at[pl.ds(0, 2 * GROUP)], left.at[pl.ds(0, 3 * GROUP)],
    )
    lz_ring.start()

    k_g = sems.take(1)
    own_rows = aligned(i * PIECE, PIECE)

    @pl.when(i < OWNERS)
    def _():
        remote(kz, kz, k_z, z_dev(1)).wait_recv()
        cap[own_rows, :] = kmid[...] + kz[0] + kz[1] + kz[2]
        for d in range(1, 16):
            remote(cap.at[own_rows], cap.at[own_rows], k_g, {"row": (i + d) % 16}).start()

    for z in range(2):
        source = y * 4 + 2 * c + z
        dst = g_all.at[y, 2 * c + z]

        @pl.when((i != j) | (source != j))
        def _():
            remote(g_piece, dst, s_t, {"row": j, "col": source}, s_t + z).wait_recv()

        @pl.when((i == j) & (source == j))
        def _():
            pltpu.make_async_copy(g_piece, dst, recv_sem.at[s_t + z]).wait()

    y_ring = Ring(lambda half, owner: g_all.at[owner, 2 * c + half], y, y_dev, g_all.at[0], g_all.at[pl.ds(0, 3), pl.ds(0, 2)])
    y_ring.start()
    lz_ring.forward()
    l_ring = Ring(
        lambda half, owner: left.at[aligned(owner * QUARTER + half * LANES, LANES)], x, x_dev,
        left.at[pl.ds(0, 2 * QUARTER)], left.at[pl.ds(0, 3 * QUARTER)],
    )

    others = cap.at[pl.ds(0, PACKED - PIECE)]

    @pl.when(i < OWNERS)
    def _():
        remote(others, others, k_g, {"row": (i + 1) % 16}).wait_recv()

    @pl.when(i >= OWNERS)
    def _():
        remote(cap, cap, k_g, {"row": (i + 1) % 16}).wait_recv()

    def rest():
        pass

    a_c = sems.take(1)
    sibling = {"row": i + 1 - 2 * c}
    mine = g_all.at[:, pl.ds(2 * c, 2)]
    theirs = g_all.at[:, pl.ds(2 - 2 * c, 2)]

    def serve_left():
        lz_ring.finish()
        l_ring.start()

    def serve_y():
        y_ring.finish()
        remote(mine, mine, a_c, sibling).start()

    def serve_core():
        remote(theirs, theirs, a_c, sibling).wait_recv()

        @pl.loop(0, 4)
        def _(q):
            for g in range(4):
                hi, lo = split2(unfold(g_all[q, g]))
                rows = aligned(q * QUARTER + g * GROUP, GROUP)
                g_hi[rows, :] = hi
                g_lo[rows, :] = lo

    invert(cap, minv, iter((serve_left, y_ring.forward, rest, rest, rest, rest, serve_y, l_ring.forward)))
    serve_core()

    m_hi, m_lo = split2(minv[...])
    value = sum(
        lax.dot_general(m, g, NT, preferred_element_type=F32)
        for m, g in ((m_hi, g_lo[...]), (m_lo, g_hi[...]), (m_hi, g_hi[...]))
    )
    scaled[...] = value.astype(BF)
    goal_load.wait()
    guess = jnp.concatenate([cap[3 * BLOCK : 3 * BLOCK + OUTS, :], cap[3 * BLOCK + OUTS :, : STEPS - LANES]], axis=1)
    readout_new[...] = readout[...] - dot32(guess - goal[...], value)
    l_ring.finish()

    @pl.when(i != j)
    def _():
        remote(r_src, rx, r_t, {"row": j, "col": i}).wait_send()

    swap_each(lambda copy: copy.wait_send(), None)
    remote(e_z, e_z, e_at, z_dev(1)).wait_send()
    for ring in (g_ring, e_ring, z_ring, lz_ring, y_ring, l_ring):
        ring.wait_sends()

    some = kpart.at[pl.ds(0, PACKED - PIECE)]

    @pl.when(i < OWNERS)
    def _():
        remote(some, some, k_r, {"row": (i + 1) % 16}).wait_send()
        remote(kx, kx, k_x, x_dev(1)).wait_send()
        remote(kz, kz, k_z, z_dev(1)).wait_send()
        remote(krow, krow, k_g, {"row": (i + 1) % 16}).wait_send()

    @pl.when(i >= OWNERS)
    def _():
        remote(kpart, kpart, k_r, {"row": (i + 1) % 16}).wait_send()

    remote(mine, mine, a_c, sibling).wait_send()


N_SEMS = 96


def gather_all(rates, targets, goal, readout, corr, rec):
    hbm = pl.BlockSpec(memory_space=pl.ANY)

    def folded(dtype, *lead):
        return pltpu.VMEM((*lead, FOLDED, LANES), dtype)

    return pl.pallas_call(
        comm_kernel,
        out_shape=[
            jax.ShapeDtypeStruct((STEPS, LOCAL), BF),
            jax.ShapeDtypeStruct((OUTS, LOCAL), F32),
            jax.ShapeDtypeStruct((LOCAL, 2 * STEPS), BF),
            jax.ShapeDtypeStruct((LOCAL, LOCAL), F32),
            jax.ShapeDtypeStruct((LOCAL, LOCAL), BF),
        ],
        in_specs=[hbm] * 6,
        out_specs=[pl.BlockSpec(memory_space=pltpu.VMEM)] * 5,
        scratch_shapes=[
            pltpu.VMEM((STEPS, LOCAL), BF),
            pltpu.VMEM((LOCAL, STEPS), BF),
            pltpu.VMEM((STEPS, LOCAL), BF),
            pltpu.VMEM((OUTS, STEPS), F32),
            pltpu.VMEM((OUTS, LOCAL), F32),
            pltpu.VMEM((STEPS, QUARTER), BF),
            folded(F32, 3, 4),
            folded(F32, 4),
            folded(F32, 2, 2),
            folded(F32, 2, 2),
            folded(F32, 4, 2),
            pltpu.VMEM((2, FOLDED // 2, LANES), F32),
            pltpu.VMEM((2, FOLDED // 2, LANES), F32),
            pltpu.VMEM((4, FOLDED // 2, LANES), F32),
            folded(F32),
            folded(F32, 4, 4),
            pltpu.VMEM((LOCAL, STEPS), BF),
            pltpu.VMEM((LOCAL, STEPS), BF),
            folded(BF, 3, 4),
            folded(F32, 2, 2),
            folded(F32, 4),
            folded(F32, 4),
            folded(BF, 2, 2),
            folded(BF, 2, 2),
            folded(BF, 4, 2),
            folded(BF, 4),
            folded(BF, 3),
            pltpu.VMEM((PACKED, LANES), F32),
            pltpu.VMEM((15, PIECE, LANES), F32),
            pltpu.VMEM((PIECE, LANES), F32),
            pltpu.VMEM((3, PIECE, LANES), F32),
            pltpu.VMEM((PIECE, LANES), F32),
            pltpu.VMEM((3, PIECE, LANES), F32),
            pltpu.VMEM((PACKED, LANES), F32),
            pltpu.VMEM((STEPS, STEPS), F32),
            pltpu.SemaphoreType.DMA((12,)),
            pltpu.SemaphoreType.DMA((N_SEMS,)),
            pltpu.SemaphoreType.DMA((N_SEMS,)),
        ],
        compiler_params=pltpu.CompilerParams(
            collective_id=0, has_side_effects=True, vmem_limit_bytes=VMEM_LIMIT
        ),
        name="exchange",
    )(rates, targets, goal, readout, corr, rec)


def update_kernel(scaled, readout_new, left, corr, rec, corr_out, rec_out, readout_out, corr_new, rec_new, sems):
    copies = [pltpu.make_async_copy(readout_new, readout_out, sems.at[8])]
    copies[0].start()
    for q in range(4):
        rows = pl.ds(q * QUARTER, QUARTER)
        drop = jnp.dot(left[rows, STEPS:], scaled[...], preferred_element_type=F32)
        corr_new[rows, :] = corr[rows, :] - drop
        copies.append(pltpu.make_async_copy(corr_new.at[rows], corr_out.at[rows], sems.at[2 * q]))
        copies[-1].start()
        drop = jnp.dot(left[rows, :STEPS], scaled[...], preferred_element_type=F32)
        rec_new[rows, :] = (rec[rows, :].astype(F32) - drop).astype(BF)
        copies.append(pltpu.make_async_copy(rec_new.at[rows], rec_out.at[rows], sems.at[2 * q + 1]))
        copies[-1].start()
    for copy in copies:
        copy.wait()


def update(scaled, readout_new, left, corr, rec):
    return pl.pallas_call(
        update_kernel,
        out_shape=[
            jax.ShapeDtypeStruct((LOCAL, LOCAL), F32),
            jax.ShapeDtypeStruct((LOCAL, LOCAL), BF),
            jax.ShapeDtypeStruct((OUTS, LOCAL), F32),
        ],
        in_specs=[pl.BlockSpec(memory_space=pltpu.VMEM)] * 5,
        out_specs=[pl.BlockSpec(memory_space=pl.ANY)] * 3,
        scratch_shapes=[
            pltpu.VMEM((LOCAL, LOCAL), F32),
            pltpu.VMEM((LOCAL, LOCAL), BF),
            pltpu.SemaphoreType.DMA((9,)),
        ],
        compiler_params=pltpu.CompilerParams(vmem_limit_bytes=VMEM_LIMIT),
        name="update",
    )(scaled, readout_new, left, corr, rec)


def on_device(*args):
    rates, targets, goal, corr, rec, readout = (pltpu.with_memory_space_constraint(v, pltpu.HBM) for v in args)
    return tuple(update(*gather_all(rates, targets, goal, readout, corr, rec)))


def solution(mesh):
    placed = (P(None, "col"), P(None, "row"), P(), P("row", "col"), P("row", "col"), P(None, "col"))
    return jax.shard_map(
        on_device,
        mesh=mesh,
        in_specs=placed,
        out_specs=(P("row", "col"), P("row", "col"), P(None, "col")),
        check_vma=False,
    )
```

```python
import functools

import jax
import jax.numpy as jnp
from jax import lax
from jax.experimental import pallas as pl
from jax.experimental.pallas import tpu as pltpu
from jax.sharding import PartitionSpec as P

MESH = pl.DeviceIdType.MESH
BF, F32 = jnp.bfloat16, jnp.float32
HIGH = lax.Precision.HIGHEST

STEPS = 192
LOCAL = 1024
OUTS = 16
QUARTER = 256
GROUP = 64
PIECE = 16
BLOCK = 64
PACKED = 3 * BLOCK + 2 * OUTS
OWNERS = PACKED // PIECE
LANES = 128
FOLDED = GROUP * STEPS // LANES
NT = (((1,), (1,)), ((), ()))
VMEM_LIMIT = 32 * 1024 * 1024


def split2(x):
    hi = x.astype(BF)
    return hi, (x - hi.astype(F32)).astype(BF)


def aligned(start, size):
    return pl.ds(pl.multiple_of(start, size), size)


def fold(v):
    low = jnp.concatenate([v[: GROUP // 2, LANES:], v[GROUP // 2 :, LANES:]], axis=1)
    return jnp.concatenate([v[:, :LANES], low], axis=0)


def unfold(v):
    rest = STEPS - LANES
    high = jnp.concatenate([v[GROUP:, :rest], v[GROUP:, rest:]], axis=0)
    return jnp.concatenate([v[:GROUP], high], axis=1)


def groups(v):
    return [v[g * GROUP : (g + 1) * GROUP] for g in range(v.shape[0] // GROUP)]


class Sems:
    def __init__(self):
        self.at = 0

    def take(self, count):
        first = self.at
        self.at += count
        return first


SUBS = 8
WIDE = 4


def reciprocal(v):
    return pl.reciprocal(v, approx=True)


def factor_two(a, b, d):
    ra = reciprocal(a)
    return b * ra, ra, a * reciprocal(a * d - b * b)


def factor_four(s):
    l = [[None] * WIDE for _ in range(WIDE)]
    l[1][0], rd0, rd1 = factor_two(s[0][0], s[1][0], s[1][1])
    c = {}
    for r in (2, 3):
        l[r][0] = s[r][0] * rd0
        c[r] = s[r][1] - l[1][0] * s[r][0]
        l[r][1] = c[r] * rd1

    def left(r, t):
        return s[r][t] - (l[r][0] * s[t][0] + l[r][1] * c[t])

    l[3][2], rd2, rd3 = factor_two(left(2, 2), left(3, 2), left(3, 3))
    return l, (rd0, rd1, rd2, rd3)


def eliminate(l, v):
    v1 = v[1] - l[1][0] * v[0]
    v2 = v[2] - l[2][0] * v[0] - l[2][1] * v1
    v3 = v[3] - l[3][0] * v[0] - l[3][1] * v1 - l[3][2] * v2
    return v[0], v1, v2, v3


def inverse_block(a, services):
    rows = [a[u * SUBS : (u + 1) * SUBS] for u in range(BLOCK // SUBS)]
    shape = (SUBS, BLOCK)
    lane = lax.broadcasted_iota(jnp.int32, shape, 1)
    sub = lax.broadcasted_iota(jnp.int32, shape, 0)
    span = range(WIDE)

    def column(row, k):
        return jnp.broadcast_to(row[:, k : k + 1], shape)

    def entry(col, r):
        return jnp.broadcast_to(col[r % SUBS : r % SUBS + 1], shape)

    s = None
    for k in range(0, BLOCK, WIDE):
        v, first = k // SUBS, k % SUBS
        col = [[column(row, k + b) for row in rows] for b in span]
        if s is None:
            s = [[entry(col[b][v], k + a) for b in range(a + 1)] for a in span]
        after = k + WIDE
        if after < BLOCK:
            row = rows[after // SUBS]
            ahead = [column(row, after + b) for b in span]
            ahead = [[entry(ahead[b], after + a) for b in range(a + 1)] for a in span]
            links = [[entry(col[b][after // SUBS], after + a) for b in span] for a in span]
        inside = (lane >= k) & (lane < k + WIDE)
        top = [
            jnp.where(inside, jnp.where(lane == k + b, 1.0, 0.0), entry(rows[v], first + b))
            for b in span
        ]
        l, rd = factor_four(s)
        if after < BLOCK:
            links = [eliminate(l, link) for link in links]
            scaled = [[link[b] * rd[b] for b in span] for link in links]
            s = [
                [
                    ahead[a][b]
                    - (
                        (scaled[a][0] * links[b][0] + scaled[a][1] * links[b][1])
                        + (scaled[a][2] * links[b][2] + scaled[a][3] * links[b][3])
                    )
                    for b in range(a + 1)
                ]
                for a in span
            ]
        top = eliminate(l, top)
        new = [None] * WIDE
        for a in reversed(span):
            new[a] = rd[a] * top[a]
            for b in range(a + 1, WIDE):
                new[a] = new[a] - l[b][a] * new[b]
        for u in range(len(rows)):
            m = eliminate(l, [col[b][u] for b in span])
            drop = ((m[0] * rd[0]) * top[0] + (m[1] * rd[1]) * top[1]) + ((m[2] * rd[2]) * top[2] + (m[3] * rd[3]) * top[3])
            rows[u] = jnp.where(inside, 0.0, rows[u]) - drop
        for a in span:
            rows[v] = jnp.where(sub == first + a, new[a], rows[v])
        if k % (4 * WIDE) == 3 * WIDE:
            for serve in services:
                serve()
                break
    return jnp.concatenate(rows, axis=0)


def dot32(a, b):
    return jnp.dot(a, b, precision=HIGH, preferred_element_type=F32)


def invert(cap, minv, services):
    count = STEPS // BLOCK

    def at(r):
        return pl.ds(r * BLOCK, BLOCK)

    (k00, k11), (k22, k10), (k20, k21) = [
        [cap[at(r), :BLOCK], cap[at(r), BLOCK:]] for r in range(count)
    ]
    minv[at(0), :] = jnp.concatenate([k00, k10.T, k20.T], axis=1)
    minv[at(1), :] = jnp.concatenate([k10, k11, k21.T], axis=1)
    minv[at(2), :] = jnp.concatenate([k20, k21, k22], axis=1)
    shape = (STEPS, STEPS)
    lane = lax.broadcasted_iota(jnp.int32, shape, 1)
    minv[...] += jnp.where(lax.broadcasted_iota(jnp.int32, shape, 0) == lane, 1.0, 0.0)
    lane1 = lax.broadcasted_iota(jnp.int32, (BLOCK, STEPS), 1)
    sub1 = lax.broadcasted_iota(jnp.int32, (BLOCK, STEPS), 0)
    for k in range(count):
        first, last = k * BLOCK, (k + 1) * BLOCK
        inv = inverse_block(minv[at(k), first:last], services)
        inside = (lane1 >= first) & (lane1 < last)
        row = jnp.where(inside, jnp.where(lane1 - first == sub1, 1.0, 0.0), minv[at(k), :])
        new = dot32(inv, row)
        drop = dot32(minv[:, first:last], new)
        minv[...] = jnp.where((lane >= first) & (lane < last), 0.0, minv[...]) - drop
        minv[at(k), :] = new


def comm_kernel(
    rates_hbm, targets_hbm, goal_hbm, readout_hbm, corr_hbm, rec_hbm,
    scaled, readout_new, left, corr_v, rec_v,
    rates, rates_t, targets, goal, readout, rx,
    g_part, g_mid, g_relay, g_sum, g_x, g_zrelay, g_zsum, g_z, g_piece, g_all, g_hi, g_lo,
    e_part, e_hold, e_aim, e_mid, e_relay, e_sum, e_x, e_low, e_z,
    kpart, krow, ksum, kz, kmid, kx, cap, minv,
    load_sem, send_sem, recv_sem,
):
    i = lax.axis_index("row")
    j = lax.axis_index("col")
    y, zl, c = i // 4, (i // 2) % 2, i % 2
    x, zh = j // 4, j % 4
    sems = Sems()

    def quarter(q):
        return aligned((q % 4) * QUARTER, QUARTER)

    def remote(src, dst, at, dev, land=None):
        return pltpu.make_async_remote_copy(
            src_ref=src, dst_ref=dst, send_sem=send_sem.at[at], recv_sem=recv_sem.at[at if land is None else land],
            device_id=dev, device_id_type=MESH,
        )

    def load(src, dst, at):
        copy = pltpu.make_async_copy(src, dst, load_sem.at[at])
        copy.start()
        return copy

    rates_load = load(rates_hbm, rates, 8)
    rec_loads, corr_loads = {}, {}

    def load_quarter(d, loads, src, dst, at):
        part = quarter(x + d)
        loads[d] = load(src.at[part], dst.at[part], at + d)

    load_quarter(2, corr_loads, corr_hbm, corr_v, 4)

    barrier = pltpu.get_barrier_semaphore()

    def greet(dev):
        pl.semaphore_signal(barrier, inc=1, device_id=dev, device_id_type=MESH)

    for d in range(1, 16):
        greet({"row": (i + d) % 16})

    for d in range(1, 4):
        greet({"col": x * 4 + (zh + d) % 4})
        greet({"col": ((x + d) % 4) * 4 + zh})

    @pl.when(i != j)
    def _():
        greet({"row": j, "col": i})

    for z in range(2):
        source = y * 4 + 2 * c + z

        @pl.when((i != j) | (source != j))
        def _():
            greet({"row": j, "col": source})

    for d in (1, 3, 0):
        load_quarter(d, corr_loads, corr_hbm, corr_v, 4)
    for d in (2, 1, 3, 0):
        load_quarter(d, rec_loads, rec_hbm, rec_v, 0)
    readout_load = load(readout_hbm, readout, 9)
    targets_load = load(targets_hbm, targets, 10)
    goal_load = load(goal_hbm, goal, 11)

    rates_load.wait()
    rates_t[...] = rates[...].T

    def z_dev(d):
        return {"col": x * 4 + (zh + d) % 4}

    def x_dev(d):
        return {"col": ((x + d) % 4) * 4 + zh}

    def y_dev(d):
        return {"row": ((y + d) % 4) * 4 + zl * 2 + c}

    class RingSum:
        def __init__(self, part, hold, relay, total, landed, sent, dev):
            self.hold, self.relay, self.total, self.landed = hold, relay, total, landed
            at = sems.take(3)
            self.copies = [
                remote(part(0, 0), relay.at[0], at, dev(1), at),
                remote(part(0, 1), relay.at[1], at, dev(3), at + 1),
                remote(part(1, 1), landed.at[0], at, dev(1), at + 2),
                remote(part(2, 0), landed.at[1], at, dev(3), at + 2),
                remote(total.at[0], landed.at[2], at, dev(1), at + 2),
                remote(total.at[1], landed.at[3], at, dev(3), at + 2),
            ]
            self.arrived = remote(landed, landed, at, dev(1), at + 2)
            self.sent = remote(sent, sent, at, dev(1))

        def start(self, *which):
            for k in which:
                self.copies[k].start()

        def forward(self):
            for k in range(2):
                self.copies[k].wait_recv()
                self.total[k] = (self.hold(k) + self.relay[k].astype(F32)).astype(self.total.dtype)
                self.copies[4 + k].start()

        def finish(self):
            self.arrived.wait_recv()
            got = [self.landed[k].astype(F32) for k in range(4)]
            return got[2] + got[1], got[0] + got[3]

        def wait_sends(self):
            self.sent.wait_send()

    class Ring:
        def __init__(self, block, me, dev, four, six):
            self.block, self.me, self.dev = block, me, dev
            self.at = sems.take(3)
            self.arrived = remote(four, four, self.at, dev(1), self.at + 2)
            self.sent = remote(six, six, self.at, dev(1))

        def copy(self, k, owner):
            block = self.block((0, 1, 1, 0, 0, 1)[k], owner % 4)
            land = self.at + (0, 2, 1, 2, 2, 2)[k]
            return remote(block, block, self.at, self.dev((1, 1, 3, 3, 1, 3)[k]), land)

        def start(self):
            for k in (0, 2, 1, 3):
                self.copy(k, self.me).start()

        def forward(self):
            self.copy(0, self.me + 3).wait_recv()
            self.copy(4, self.me + 3).start()
            self.copy(2, self.me + 1).wait_recv()
            self.copy(5, self.me + 1).start()

        def finish(self):
            self.arrived.wait_recv()

        def wait_sends(self):
            self.sent.wait_send()

    def prod_quarter(d, out):
        corr_loads[d].wait()
        both = jnp.concatenate(split2(corr_v[quarter(x + d), :]), axis=0)
        both = jnp.dot(both, rates_t[...], preferred_element_type=F32)
        value = both[:QUARTER] + both[QUARTER:]
        for g, part in enumerate(groups(value)):
            out[g] = fold(part)

    def drive_quarter(d):
        rec_loads[d].wait()
        value = jnp.dot(rec_v[quarter(x + d), :], rates_t[...], preferred_element_type=F32)
        return [fold(part) for part in groups(value)]

    pl.semaphore_wait(barrier, jnp.where(i == j, jnp.where(zl == c, 22, 23), 24))
    r_t = sems.take(1)
    r_src = rates.at[:, quarter(y)]

    @pl.when(i != j)
    def _():
        remote(r_src, rx, r_t, {"row": j, "col": i}).start()

    @pl.when(i == j)
    def _():
        pltpu.make_async_copy(r_src, rx, recv_sem.at[r_t]).start()

    def pairs(part):
        return lambda which, half: part.at[which, pl.ds(2 * half, 2)]

    g_ring = RingSum(
        pairs(g_part), lambda k: g_part[1, :2] if k == 0 else g_part[2, 2:], g_relay, g_sum, g_x, g_part, x_dev
    )
    prod_quarter(2, g_part.at[0])
    g_ring.start(0, 1)
    prod_quarter(1, g_part.at[1])
    g_ring.start(2)
    prod_quarter(3, g_part.at[2])
    g_ring.start(3)
    prod_quarter(0, g_mid)

    e_ring = RingSum(pairs(e_part), lambda k: e_hold[k], e_relay, e_sum, e_x, e_part, x_dev)
    for g, part in enumerate(drive_quarter(2)):
        e_part[0, g] = part.astype(BF)
    g_ring.forward()
    e_ring.start(0, 1)
    for g, part in enumerate(drive_quarter(1)):
        if g < 2:
            e_hold[0, g] = part
        else:
            e_part[1, g] = part.astype(BF)
    e_ring.start(2)
    for g, part in enumerate(drive_quarter(3)):
        if g < 2:
            e_part[2, g] = part.astype(BF)
        else:
            e_hold[1, g - 2] = part
    e_ring.start(3)

    readout_load.wait()
    guess = sum(
        jnp.dot(term, rates_t[...], preferred_element_type=F32) for term in split2(readout[...] * (1.0 / 16.0))
    )
    kpart[3 * BLOCK : 3 * BLOCK + OUTS, :] = guess[:, :LANES]
    kpart[3 * BLOCK + OUTS :, :] = jnp.concatenate([guess[:, LANES:], guess[:, LANES:]], axis=1)

    for g, part in enumerate(drive_quarter(0)):
        e_mid[g] = part
    targets_load.wait()
    aims = targets[:, quarter(x)].T.astype(F32)
    for g, part in enumerate(groups(aims)):
        e_aim[g] = fold(part)

    @pl.when(i != j)
    def _():
        remote(r_src, rx, r_t, {"row": j, "col": i}).wait_recv()

    @pl.when(i == j)
    def _():
        pltpu.make_async_copy(r_src, rx, recv_sem.at[r_t]).wait()

    got = g_ring.finish()
    for k in range(2):
        g_mid[2 * k : 2 * k + 2] = g_mid[2 * k : 2 * k + 2] + got[k]

    def g_slice(which, half):
        return g_mid.at[(zh + (2, 1, 3)[which]) % 4, pl.ds(half * (FOLDED // 2), FOLDED // 2)]

    z_ring = RingSum(g_slice, lambda k: g_slice(k + 1, k)[...], g_zrelay, g_zsum, g_z, g_part.at[0, pl.ds(0, 3)], z_dev)
    z_ring.start(0, 1, 2, 3)

    whole = sum(
        jnp.dot(rx[...], term, preferred_element_type=F32)
        for term in split2(jnp.concatenate([unfold(g_mid[g]) for g in range(4)], axis=0))
    )
    kb = [[whole[r * BLOCK : (r + 1) * BLOCK, s * BLOCK : (s + 1) * BLOCK] for s in range(3)] for r in range(3)]
    kpart[:BLOCK, :] = jnp.concatenate([kb[0][0], kb[1][1]], axis=1)
    kpart[BLOCK : 2 * BLOCK, :] = jnp.concatenate([kb[2][2], kb[1][0]], axis=1)
    kpart[2 * BLOCK : 3 * BLOCK, :] = jnp.concatenate([kb[2][0], kb[2][1]], axis=1)

    e_ring.forward()

    k_r = sems.take(1)

    for d in range(1, 16):
        owner = (i + d) % 16

        @pl.when(owner < OWNERS)
        def _():
            remote(kpart.at[aligned(owner * PIECE, PIECE)], krow.at[d - 1], k_r, {"row": owner}).start()

    z_ring.forward()
    k_x = sems.take(1)
    k_z = sems.take(1)

    @pl.when(i < OWNERS)
    def _():
        remote(krow, krow, k_r, {"row": (i + 1) % 16}).wait_recv()
        acc = kpart[aligned(i * PIECE, PIECE), :]
        for d in range(15):
            acc = acc + krow[d]
        ksum[...] = acc
        for d in range(1, 4):
            remote(ksum, kx.at[d - 1], k_x, x_dev(d)).start()

    got = e_ring.finish()
    for k in range(2):
        total = e_mid[2 * k : 2 * k + 2] + got[k]
        e_mid[2 * k : 2 * k + 2] = total
        e_low[2 * k : 2 * k + 2] = total.astype(BF)
    e_at = sems.take(1)

    def e_z_copy(d):
        return remote(e_low.at[(zh + d) % 4], e_z.at[d - 1], e_at, z_dev(d))

    for d in range(1, 4):
        e_z_copy(d).start()

    @pl.when(i < OWNERS)
    def _():
        remote(kx, kx, k_x, x_dev(1)).wait_recv()
        kmid[...] = ksum[...] + kx[0] + kx[1] + kx[2]
        for d in range(1, 4):
            remote(kmid, kz.at[d - 1], k_z, z_dev(d)).start()

    got = z_ring.finish()
    for k in range(2):
        part = pl.ds(k * (FOLDED // 2), FOLDED // 2)
        g_piece[part, :] = g_mid[zh, part, :] + got[k]
    own = aligned(x * QUARTER + zh * GROUP, GROUP)
    s_t = sems.take(2)

    def swap_each(act_remote, act_local):
        for e in range(2):
            dst = g_all.at[x, zh]
            row = x * 4 + e * 2 + zh // 2

            @pl.when((i != j) | (row != i))
            def _():
                act_remote(remote(g_piece, dst, s_t + e, {"row": row, "col": i}, s_t + zh % 2))

            if act_local is not None:

                @pl.when((i == j) & (row == i))
                def _():
                    act_local(pltpu.make_async_copy(g_piece, dst, recv_sem.at[s_t + zh % 2]))

    swap_each(lambda copy: copy.start(), lambda copy: copy.start())
    left[own, STEPS:] = unfold(g_piece[...]).astype(BF)

    remote(e_z, e_z, e_at, z_dev(1)).wait_recv()
    total = e_mid[zh] - e_aim[zh]
    for d in range(3):
        total = total + e_z[d].astype(F32)
    left[own, :STEPS] = unfold(total).astype(BF)
    lz_ring = Ring(
        lambda half, owner: left.at[aligned(x * QUARTER + owner * GROUP + half * (GROUP // 2), GROUP // 2)], zh, z_dev,
        left.at[pl.ds(0, 2 * GROUP)], left.at[pl.ds(0, 3 * GROUP)],
    )
    lz_ring.start()

    k_g = sems.take(1)
    own_rows = aligned(i * PIECE, PIECE)

    @pl.when(i < OWNERS)
    def _():
        remote(kz, kz, k_z, z_dev(1)).wait_recv()
        cap[own_rows, :] = kmid[...] + kz[0] + kz[1] + kz[2]
        for d in range(1, 16):
            remote(cap.at[own_rows], cap.at[own_rows], k_g, {"row": (i + d) % 16}).start()

    for z in range(2):
        source = y * 4 + 2 * c + z
        dst = g_all.at[y, 2 * c + z]

        @pl.when((i != j) | (source != j))
        def _():
            remote(g_piece, dst, s_t, {"row": j, "col": source}, s_t + z).wait_recv()

        @pl.when((i == j) & (source == j))
        def _():
            pltpu.make_async_copy(g_piece, dst, recv_sem.at[s_t + z]).wait()

    y_ring = Ring(lambda half, owner: g_all.at[owner, 2 * c + half], y, y_dev, g_all.at[0], g_all.at[pl.ds(0, 3), pl.ds(0, 2)])
    y_ring.start()
    lz_ring.forward()
    l_ring = Ring(
        lambda half, owner: left.at[aligned(owner * QUARTER + half * LANES, LANES)], x, x_dev,
        left.at[pl.ds(0, 2 * QUARTER)], left.at[pl.ds(0, 3 * QUARTER)],
    )

    others = cap.at[pl.ds(0, PACKED - PIECE)]

    @pl.when(i < OWNERS)
    def _():
        remote(others, others, k_g, {"row": (i + 1) % 16}).wait_recv()

    @pl.when(i >= OWNERS)
    def _():
        remote(cap, cap, k_g, {"row": (i + 1) % 16}).wait_recv()

    def rest():
        pass

    a_c = sems.take(1)
    sibling = {"row": i + 1 - 2 * c}
    mine = g_all.at[:, pl.ds(2 * c, 2)]
    theirs = g_all.at[:, pl.ds(2 - 2 * c, 2)]

    def serve_left():
        lz_ring.finish()
        l_ring.start()

    def serve_y():
        y_ring.finish()
        remote(mine, mine, a_c, sibling).start()

    def serve_core():
        remote(theirs, theirs, a_c, sibling).wait_recv()

        @pl.loop(0, 4)
        def _(q):
            for g in range(4):
                hi, lo = split2(unfold(g_all[q, g]))
                rows = aligned(q * QUARTER + g * GROUP, GROUP)
                g_hi[rows, :] = hi
                g_lo[rows, :] = lo

    invert(cap, minv, iter((serve_left, y_ring.forward, rest, rest, rest, rest, serve_y, l_ring.forward)))
    serve_core()

    m_hi, m_lo = split2(minv[...])
    both = lax.dot_general(jnp.concatenate([m_hi, m_lo], axis=0), g_hi[...], NT, preferred_element_type=F32)
    value = both[:STEPS] + (both[STEPS:] + lax.dot_general(m_hi, g_lo[...], NT, preferred_element_type=F32))
    scaled[...] = value.astype(BF)
    goal_load.wait()
    guess = jnp.concatenate([cap[3 * BLOCK : 3 * BLOCK + OUTS, :], cap[3 * BLOCK + OUTS :, : STEPS - LANES]], axis=1)
    readout_new[...] = readout[...] - dot32(guess - goal[...], value)
    l_ring.finish()

    @pl.when(i != j)
    def _():
        remote(r_src, rx, r_t, {"row": j, "col": i}).wait_send()

    swap_each(lambda copy: copy.wait_send(), None)
    remote(e_z, e_z, e_at, z_dev(1)).wait_send()
    for ring in (g_ring, e_ring, z_ring, lz_ring, y_ring, l_ring):
        ring.wait_sends()

    some = kpart.at[pl.ds(0, PACKED - PIECE)]

    @pl.when(i < OWNERS)
    def _():
        remote(some, some, k_r, {"row": (i + 1) % 16}).wait_send()
        remote(kx, kx, k_x, x_dev(1)).wait_send()
        remote(kz, kz, k_z, z_dev(1)).wait_send()
        remote(krow, krow, k_g, {"row": (i + 1) % 16}).wait_send()

    @pl.when(i >= OWNERS)
    def _():
        remote(kpart, kpart, k_r, {"row": (i + 1) % 16}).wait_send()

    remote(mine, mine, a_c, sibling).wait_send()


N_SEMS = 96


def gather_all(rates, targets, goal, readout, corr, rec):
    hbm = pl.BlockSpec(memory_space=pl.ANY)

    def folded(dtype, *lead):
        return pltpu.VMEM((*lead, FOLDED, LANES), dtype)

    return pl.pallas_call(
        comm_kernel,
        out_shape=[
            jax.ShapeDtypeStruct((STEPS, LOCAL), BF),
            jax.ShapeDtypeStruct((OUTS, LOCAL), F32),
            jax.ShapeDtypeStruct((LOCAL, 2 * STEPS), BF),
            jax.ShapeDtypeStruct((LOCAL, LOCAL), F32),
            jax.ShapeDtypeStruct((LOCAL, LOCAL), BF),
        ],
        in_specs=[hbm] * 6,
        out_specs=[pl.BlockSpec(memory_space=pltpu.VMEM)] * 5,
        scratch_shapes=[
            pltpu.VMEM((STEPS, LOCAL), BF),
            pltpu.VMEM((LOCAL, STEPS), BF),
            pltpu.VMEM((STEPS, LOCAL), BF),
            pltpu.VMEM((OUTS, STEPS), F32),
            pltpu.VMEM((OUTS, LOCAL), F32),
            pltpu.VMEM((STEPS, QUARTER), BF),
            folded(F32, 3, 4),
            folded(F32, 4),
            folded(F32, 2, 2),
            folded(F32, 2, 2),
            folded(F32, 4, 2),
            pltpu.VMEM((2, FOLDED // 2, LANES), F32),
            pltpu.VMEM((2, FOLDED // 2, LANES), F32),
            pltpu.VMEM((4, FOLDED // 2, LANES), F32),
            folded(F32),
            folded(F32, 4, 4),
            pltpu.VMEM((LOCAL, STEPS), BF),
            pltpu.VMEM((LOCAL, STEPS), BF),
            folded(BF, 3, 4),
            folded(F32, 2, 2),
            folded(F32, 4),
            folded(F32, 4),
            folded(BF, 2, 2),
            folded(BF, 2, 2),
            folded(BF, 4, 2),
            folded(BF, 4),
            folded(BF, 3),
            pltpu.VMEM((PACKED, LANES), F32),
            pltpu.VMEM((15, PIECE, LANES), F32),
            pltpu.VMEM((PIECE, LANES), F32),
            pltpu.VMEM((3, PIECE, LANES), F32),
            pltpu.VMEM((PIECE, LANES), F32),
            pltpu.VMEM((3, PIECE, LANES), F32),
            pltpu.VMEM((PACKED, LANES), F32),
            pltpu.VMEM((STEPS, STEPS), F32),
            pltpu.SemaphoreType.DMA((12,)),
            pltpu.SemaphoreType.DMA((N_SEMS,)),
            pltpu.SemaphoreType.DMA((N_SEMS,)),
        ],
        compiler_params=pltpu.CompilerParams(
            collective_id=0, has_side_effects=True, vmem_limit_bytes=VMEM_LIMIT
        ),
        name="exchange",
    )(rates, targets, goal, readout, corr, rec)


def update_kernel(scaled, readout_new, left, corr, rec, corr_out, rec_out, readout_out, corr_new, rec_new, sems):
    copies = [pltpu.make_async_copy(readout_new, readout_out, sems.at[8])]
    copies[0].start()
    for q in range(4):
        rows = pl.ds(q * QUARTER, QUARTER)
        drop = jnp.dot(left[rows, STEPS:], scaled[...], preferred_element_type=F32)
        corr_new[rows, :] = corr[rows, :] - drop
        copies.append(pltpu.make_async_copy(corr_new.at[rows], corr_out.at[rows], sems.at[2 * q]))
        copies[-1].start()
        drop = jnp.dot(left[rows, :STEPS], scaled[...], preferred_element_type=F32)
        rec_new[rows, :] = (rec[rows, :].astype(F32) - drop).astype(BF)
        copies.append(pltpu.make_async_copy(rec_new.at[rows], rec_out.at[rows], sems.at[2 * q + 1]))
        copies[-1].start()
    for copy in copies:
        copy.wait()


def update(scaled, readout_new, left, corr, rec):
    return pl.pallas_call(
        update_kernel,
        out_shape=[
            jax.ShapeDtypeStruct((LOCAL, LOCAL), F32),
            jax.ShapeDtypeStruct((LOCAL, LOCAL), BF),
            jax.ShapeDtypeStruct((OUTS, LOCAL), F32),
        ],
        in_specs=[pl.BlockSpec(memory_space=pltpu.VMEM)] * 5,
        out_specs=[pl.BlockSpec(memory_space=pl.ANY)] * 3,
        scratch_shapes=[
            pltpu.VMEM((LOCAL, LOCAL), F32),
            pltpu.VMEM((LOCAL, LOCAL), BF),
            pltpu.SemaphoreType.DMA((9,)),
        ],
        compiler_params=pltpu.CompilerParams(vmem_limit_bytes=VMEM_LIMIT),
        name="update",
    )(scaled, readout_new, left, corr, rec)


def on_device(*args):
    rates, targets, goal, corr, rec, readout = (pltpu.with_memory_space_constraint(v, pltpu.HBM) for v in args)
    return tuple(update(*gather_all(rates, targets, goal, readout, corr, rec)))


def solution(mesh):
    placed = (P(None, "col"), P(None, "row"), P(), P("row", "col"), P("row", "col"), P(None, "col"))
    return jax.shard_map(
        on_device,
        mesh=mesh,
        in_specs=placed,
        out_specs=(P("row", "col"), P("row", "col"), P(None, "col")),
        check_vma=False,
    )
```
